32 devices in a mesh: dp: 8 (over z, y), mp: 4 (over x, core).
Axes of the slice: x: 2, y: 2, z: 4, core: 2. Of those that a mesh axis runs over, the one named last changes fastest.
Arguments:
- prompts: bfloat16 [2048, 4096], P('dp'), may hold values from -6 to 6
- responses: bfloat16 [2048, 4096], P('dp'), may hold values from -6 to 6
- head_projection_matrix: bfloat16 [4096, 1024], P('dp', 'mp'), may hold values from -0.09375 to 0.09375
- positive: int32 [2048], P('dp'), may hold values from 0 to 2047, as said below
Outputs:
- row_loss: float32 [2048], P('dp')
- head_grad: float32 [4096, 1024], P('dp', 'mp')
The draws below stay inside these ranges and needn't reach their ends.
Inputs may be any that keep to these rules, and one draw needn't show every extreme that they name: `positive`: positive_i lies in a block whose index is block(i) - k mod the number of blocks for some k in 0 to 7.
All inputs are finite; a program needn't handle non-finite values.
Results may differ from the reference program's by a relative error of at most 0.0039.
Values may be sent and summed in bfloat16 or wider, within the bound.
No kernel may reach another device: no remote copies, remote signals or barrier semaphores. Data moves between devices by JAX's collectives and lax.ppermute only.
A program may use at most 64 MiB of HBM per device.

```python
import math
import jax
import jax.numpy as jnp
from jax import lax

FEAT = 4096
E = 1024
ROWS = 256
STEPS = 8
PAIRS = 2048


def draw_positive(key, part):
    key = jax.random.fold_in(key, 11)
    block_total = PAIRS // ROWS
    key_lag, key_within = jax.random.split(key)
    lag_blocks = jax.random.randint(key_lag, (PAIRS,), 0, STEPS)
    within_block = jax.random.randint(key_within, (PAIRS,), 0, ROWS)
    row_index = jnp.arange(PAIRS, dtype=jnp.int32)
    owner_block = row_index // ROWS
    final_row = row_index == PAIRS - 1
    first_row = row_index == 0
    lag_blocks = jnp.where(final_row | first_row, 0, lag_blocks)
    within_block = jnp.where(final_row, ROWS - 1, jnp.where(first_row, 0, within_block))
    return ((owner_block - lag_blocks) % block_total * ROWS + within_block).astype(jnp.int32)


def with_spikes(array, own_key, source, target, shards_of, factor):
    def block_of(dim):
        return (jnp.arange(array.shape[dim]) // (array.shape[dim] // shards_of)).reshape((-1,) + (1,) * (array.ndim - 1 - dim))

    first = jax.random.permutation(own_key, shards_of)[block_of(target)]
    far = (block_of(target) + shards_of // 2) % shards_of
    return jnp.where((block_of(source) == first) | (block_of(source) == far), factor * array, array)


def shard_levels(key, extent, pieces, smallest, high):
    factor_of = 1.0
    for dim, shards_of in pieces:
        draws = jax.random.uniform(jax.random.fold_in(jax.random.fold_in(key, 6), dim), (shards_of,), jnp.float32, smallest / len(pieces), high / len(pieces))
        factor_of = factor_of * jnp.repeat(jnp.exp(draws), extent[dim] // shards_of).reshape((-1,) + (1,) * (len(extent) - 1 - dim))
    return factor_of


def gaussian(rng, extent, width, bound, cuts=(), kind=jnp.bfloat16):
    entries = jax.random.normal(rng, extent, jnp.float32) * width
    if len(cuts) > 0:
        entries = shard_levels(rng, extent, cuts, -0.22, 0.18) * entries
    return jnp.clip(entries, min=-bound, max=bound).astype(kind)


def noise_with(own_key, dims, spread, most, cuts, heavy, kind=jnp.bfloat16):
    result = spread * jax.random.normal(own_key, dims, jnp.float32)
    if cuts:
        result = result * shard_levels(own_key, dims, cuts, -0.22, 0.18)
    return jnp.clip(with_spikes(result, jax.random.fold_in(own_key, 3), *heavy), -most, most).astype(kind)


def setup_inputs(seed: int = 0) -> dict:
    streams_of = jax.random.split(jax.random.key(seed), 5)
    prompts = noise_with(streams_of[0], (PAIRS, FEAT), 1.0, 6.0, ((0, 8),), (0, 1, 8, 2.0))
    responses = noise_with(streams_of[1], (PAIRS, FEAT), 1.0, 6.0, ((0, 8),), (0, 1, 8, 2.0))
    head_projection_matrix = gaussian(streams_of[2], (FEAT, E), FEAT ** -0.5, 0.09375, ((0, 8), (1, 4)))
    positive = draw_positive(jax.random.fold_in(streams_of[4], 71), 0)
    return {"prompts": prompts, "responses": responses, "head_projection_matrix": head_projection_matrix, "positive": positive}


LOGIT_SCALE = 3.0
LOGIT_BIAS = -3.0

def reference(prompts, responses, head_projection_matrix, positive):
    block_total = PAIRS // ROWS
    factor = LOGIT_SCALE / math.sqrt(E)
    prompt_emb = jnp.dot(prompts, head_projection_matrix, preferred_element_type=jnp.float32).astype(jnp.bfloat16)
    response_emb = jnp.dot(responses, head_projection_matrix, preferred_element_type=jnp.float32).astype(jnp.bfloat16)
    prompt_block_list = prompt_emb.reshape(block_total, ROWS, E).astype(jnp.float32)
    response_blocks = response_emb.reshape(block_total, ROWS, E).astype(jnp.float32)
    local_ids = jnp.arange(ROWS, dtype=jnp.int32)
    block_ids = jnp.arange(block_total, dtype=jnp.int32)
    positive_blocks = positive.reshape(block_total, ROWS)
    prompt_gradient_total = jnp.zeros((block_total, ROWS, E), jnp.float32)
    grad_response = jnp.zeros((block_total, ROWS, E), jnp.float32)
    row_losses = jnp.zeros((block_total, ROWS), jnp.float32)
    for offset in range(STEPS):
        rotated_block = jnp.roll(response_blocks, offset, axis=0)
        pair_scores = jnp.einsum('swz,syz->swy', prompt_block_list, rotated_block, precision=lax.Precision.HIGHEST)
        pair_scores = pair_scores * factor + LOGIT_BIAS
        anchor = (block_ids - offset) % block_total
        column_ids = (anchor[:, None] * ROWS + local_ids[None, :]).astype(jnp.int32)
        labels = jnp.where(positive_blocks[:, :, None] == column_ids[:, None, :], 1.0, -1.0).astype(jnp.float32)
        margin = -labels * pair_scores
        row_losses = row_losses + lax.optimization_barrier(jnp.sum(jax.nn.softplus(margin), axis=2))
        pairwise_weight = (-labels * jax.nn.sigmoid(margin) * (factor / ROWS)).astype(jnp.bfloat16).astype(jnp.float32)
        prompt_gradient_total = prompt_gradient_total + jnp.einsum('fwt,ftv->fwv', pairwise_weight, rotated_block, precision=lax.Precision.HIGHEST)
        handed_back = jnp.einsum('fhd,fhz->fdz', pairwise_weight, prompt_block_list, precision=lax.Precision.HIGHEST)
        grad_response = grad_response + jnp.roll(handed_back, -offset, axis=0)
    grad_prompt_b = prompt_gradient_total.reshape(PAIRS, E).astype(jnp.bfloat16)
    grad_response_b = grad_response.reshape(PAIRS, E).astype(jnp.bfloat16)
    head_grad = jnp.dot(prompts.T, grad_prompt_b, preferred_element_type=jnp.float32)
    head_grad = head_grad + jnp.dot(responses.T, grad_response_b, preferred_element_type=jnp.float32)
    return ((row_losses / ROWS).reshape(PAIRS), head_grad)
```

```python
import math

import jax
import jax.numpy as jnp
from jax import lax
from jax.sharding import PartitionSpec as P

E = 1024
STEPS = 8


LOGIT_SCALE = 3.0
LOGIT_BIAS = -3.0


def passed_along(block, axis, distance):
    devices = range(lax.axis_size(axis))
    route = [((i - distance) % len(devices), i) for i in devices]
    return lax.ppermute(block, axis, route)


def cross_rows(left_side, righthand_term):
    return lax.dot_general(
        left_side, righthand_term, (((0,), (0,)), ((), ())), preferred_element_type=jnp.float32
    )


def cross_cols(left_side, righthand_term):
    return lax.dot_general(
        left_side, righthand_term, (((1,), (1,)), ((), ())), preferred_element_type=jnp.float32
    )


def matmul(left_side, righthand_term):
    return jnp.dot(left_side, righthand_term, preferred_element_type=jnp.float32)


def general(prompts, responses, head_projection_matrix, positive):
    row_count = prompts.shape[0]
    col_count = head_projection_matrix.shape[1]
    factor = LOGIT_SCALE / math.sqrt(E)
    cycle_size = lax.axis_size("dp")
    position = lax.axis_index("dp")
    segment = lax.all_gather(head_projection_matrix, "dp", axis=0, tiled=True)
    prompt_emb = matmul(prompts, segment).astype(jnp.bfloat16)
    visiting = matmul(responses, segment).astype(jnp.bfloat16)
    local_ids = lax.iota(jnp.int32, row_count)
    prompt_gradient_total = jnp.zeros((row_count, col_count), jnp.float32)
    grad_response = jnp.zeros((row_count, col_count), jnp.float32)
    row_losses = jnp.zeros((row_count,), jnp.float32)
    for offset in range(STEPS):
        partial_logits = cross_cols(prompt_emb, visiting)
        pair_scores = lax.psum(partial_logits, "mp") * factor + LOGIT_BIAS
        anchor = (position - offset) % cycle_size
        column_ids = anchor * row_count + local_ids
        labels = jnp.where(positive[:, None] == column_ids[None, :], 1.0, -1.0).astype(jnp.float32)
        margin = -labels * pair_scores
        row_losses = row_losses + jnp.sum(jax.nn.softplus(margin), axis=1)
        pairwise_weight = (-labels * jax.nn.sigmoid(margin) * (factor / row_count)).astype(
            jnp.bfloat16
        )
        prompt_gradient_total = prompt_gradient_total + matmul(pairwise_weight, visiting)
        contribution = cross_rows(pairwise_weight, prompt_emb)
        if offset == 0:
            grad_response = contribution
        else:
            grad_response = grad_response + passed_along(contribution, "dp", -offset)
        if offset < STEPS - 1:
            visiting = passed_along(visiting, "dp", 1)
    grad_prompt_b = prompt_gradient_total.astype(jnp.bfloat16)
    grad_response_b = grad_response.astype(jnp.bfloat16)
    head_grad = lax.psum_scatter(
        cross_rows(prompts, grad_prompt_b) + cross_rows(responses, grad_response_b),
        "dp",
        scatter_dimension=0,
        tiled=True,
    )
    return (row_losses / row_count, head_grad)


LINE, PAIR, SIDE, CORES = 4, 2, 2, 2


def routes(move):
    table = []
    for z in range(LINE):
        for y in range(PAIR):
            for x in range(SIDE):
                for c in range(CORES):
                    goal = move(z, y, x, c)
                    if goal is not None:
                        gz, gy, gx, gc = goal
                        source = (z * PAIR + y) * SIDE * CORES + x * CORES + c
                        target = (gz * PAIR + gy) * SIDE * CORES + gx * CORES + gc
                        table.append((source, target))
    return table


def along_line(moves):
    return routes(lambda z, y, x, c: (moves[z], y, x, c) if z in moves else None)


def send(block, table):
    return lax.ppermute(block, ("dp", "mp"), table)


ACROSS_Y = routes(lambda z, y, x, c: (z, 1 - y, x, c))
ACROSS_X = routes(lambda z, y, x, c: (z, y, 1 - x, c))
ACROSS_C = routes(lambda z, y, x, c: (z, y, x, 1 - c))
UP = along_line({0: 1, 1: 2, 2: 3})
DOWN = along_line({1: 0, 2: 1, 3: 2})
MIX = [routes(lambda z, y, x, c, k=k: (z, y, x ^ (k >> 1), c ^ (k & 1))) for k in range(4)]


def line_gather(block):
    below = send(block, UP)
    above = send(block, DOWN)
    second = send(below, along_line({1: 2, 2: 3})) + send(above, along_line({1: 0, 2: 1}))
    third = send(second, along_line({1: 0, 2: 3}))
    return below, above, second, third


def line_reduce(first, second, third_up, third_down, own):
    far = send(first.astype(jnp.bfloat16), along_line({0: 1, 3: 2})).astype(jnp.float32)
    middle = (second + far).astype(jnp.bfloat16)
    climbed = send(middle, along_line({0: 1, 1: 2})).astype(jnp.float32)
    sunk = send(middle, along_line({3: 2, 2: 1})).astype(jnp.float32)
    from_below = send((third_up + climbed).astype(jnp.bfloat16), UP)
    from_above = send((third_down + sunk).astype(jnp.bfloat16), DOWN)
    return own + from_below.astype(jnp.float32) + from_above.astype(jnp.float32)


def full_window(prompts, responses, head_projection_matrix, positive):
    row_count = prompts.shape[0]
    depth, width = head_projection_matrix.shape
    factor = LOGIT_SCALE / math.sqrt(E)
    dp, mp = lax.axis_index("dp"), lax.axis_index("mp")
    z, y = dp // PAIR, dp % PAIR
    quarter = row_count // (SIDE * CORES)
    both = jnp.concatenate([prompts, responses], axis=0)

    def features(line, pair):
        line = line % LINE
        return lax.dynamic_slice_in_dim(both, (line * PAIR + pair) * depth, depth, axis=1)

    below, above, second, third = line_gather(head_projection_matrix)
    emb = jnp.zeros((2 * row_count, width), jnp.float32)
    for block, hop in ((head_projection_matrix, 0), (below, -1), (above, 1), (second, 2)):
        emb = emb + matmul(features(z + hop, y), block)
        emb = emb + matmul(features(z + hop, 1 - y), send(block, ACROSS_Y))
    emb = emb + matmul(features(LINE - 1 - z, y), third)
    third_table = routes(lambda z, y, x, c: (z, 1 - y, x, c) if z in (0, LINE - 1) else None)
    emb = emb + matmul(features(LINE - 1 - z, 1 - y), send(third, third_table))
    emb = emb.astype(jnp.bfloat16)
    prompt_emb, response_emb = emb[:row_count], emb[row_count:]

    pieces = []
    for k in range(SIDE * CORES):
        piece = lax.dynamic_slice_in_dim(response_emb, (mp ^ k) * quarter, quarter, axis=0)
        pieces.append(piece if k == 0 else send(piece, MIX[k]))
    response_rows = jnp.concatenate(pieces, axis=1)
    below, above, second, third = line_gather(response_rows)
    below = jnp.where(z == 0, third, below)
    above = jnp.where(z == LINE - 1, third, above)
    held = jnp.concatenate([response_rows, below, above, second], axis=0)

    plane = jnp.concatenate([prompt_emb, send(prompt_emb, ACROSS_Y)], axis=0)
    beside = send(plane, ACROSS_X)
    half = jnp.concatenate([plane, beside], axis=1)
    other = send(half, ACROSS_C)
    plane = jnp.concatenate([plane, other[:, :width], beside, other[:, width:]], axis=1)
    wanted = jnp.concatenate([positive, send(positive, ACROSS_Y)], axis=0)

    pair_scores = cross_cols(plane, held) * factor + LOGIT_BIAS
    lines = jnp.stack([z, (z + LINE - 1) % LINE, (z + 1) % LINE, (z + 2) % LINE])
    column_ids = ((lines * PAIR + y) * row_count + mp * quarter)[:, None] + lax.iota(
        jnp.int32, quarter
    )[None, :]
    column_ids = column_ids.reshape(-1)
    labels = jnp.where(wanted[:, None] == column_ids[None, :], 1.0, -1.0).astype(jnp.float32)
    margin = -labels * pair_scores
    losses = jnp.sum(jax.nn.softplus(margin), axis=1)
    weight = (-labels * jax.nn.sigmoid(margin) * (factor / row_count)).astype(jnp.bfloat16)

    parts = cross_rows(weight, plane)
    own, lower, upper, far = [parts[k * quarter : (k + 1) * quarter] for k in range(4)]
    grad = line_reduce(jnp.where(z == 0, lower, upper), far, upper, lower, own)
    grad = grad.astype(jnp.bfloat16)
    grad_response = jnp.zeros((row_count, width), jnp.bfloat16)
    for k in range(SIDE * CORES):
        piece = grad[:, k * width : (k + 1) * width]
        piece = piece if k == 0 else send(piece, MIX[k])
        grad_response = lax.dynamic_update_slice_in_dim(
            grad_response, piece, (mp ^ k) * quarter, axis=0
        )

    parts = matmul(weight, held)
    mine = jnp.concatenate([parts[:, :width], parts[:, 2 * width : 3 * width]], axis=1)
    away = jnp.concatenate([parts[:, width : 2 * width], parts[:, 3 * width :]], axis=1)
    mine = mine + send(away.astype(jnp.bfloat16), ACROSS_C).astype(jnp.float32)
    mine = mine[:, :width] + send(mine[:, width:].astype(jnp.bfloat16), ACROSS_X).astype(
        jnp.float32
    )
    grad_prompt = mine[:row_count] + send(
        mine[row_count:].astype(jnp.bfloat16), ACROSS_Y
    ).astype(jnp.float32)
    grads = jnp.concatenate([grad_prompt.astype(jnp.bfloat16), grad_response], axis=0)

    def head(line):
        away = cross_rows(features(line, 1 - y), grads).astype(jnp.bfloat16)
        return cross_rows(features(line, y), grads) + send(away, ACROSS_Y).astype(jnp.float32)

    lower_half = z < LINE // 2
    end_block = head(jnp.where(lower_half, z - 1, z + 1))
    far_block = head(z + 2)
    near_block = head(jnp.where(lower_half, z + 1, z - 1))
    own_block = head(z)
    head_grad = line_reduce(
        end_block,
        far_block,
        jnp.where(z == 2, end_block, near_block),
        jnp.where(z == 1, end_block, near_block),
        own_block,
    )

    losses = losses[:row_count] + send(losses[row_count:], ACROSS_Y)
    losses = losses + send(losses, ACROSS_X)
    losses = losses + send(losses, ACROSS_C)
    return (losses / row_count, head_grad)


def per_device(prompts, responses, head_projection_matrix, positive):
    whole = lax.axis_size("dp") == STEPS == LINE * PAIR
    whole = whole and lax.axis_size("mp") == SIDE * CORES
    step = full_window if whole else general
    return step(prompts, responses, head_projection_matrix, positive)


def solution(mesh):
    return jax.shard_map(
        per_device,
        mesh=mesh,
        in_specs=(P("dp", None), P("dp", None), P("dp", "mp"), P("dp")),
        out_specs=(P("dp"), P("dp", "mp")),
        check_vma=False,
    )
```

```python
import math

import jax
import jax.numpy as jnp
from jax import lax
from jax.sharding import PartitionSpec as P

E = 1024
STEPS = 8


LOGIT_SCALE = 3.0
LOGIT_BIAS = -3.0


def passed_along(block, axis, distance):
    devices = range(lax.axis_size(axis))
    route = [((i - distance) % len(devices), i) for i in devices]
    return lax.ppermute(block, axis, route)


def cross_rows(left_side, righthand_term):
    return lax.dot_general(
        left_side, righthand_term, (((0,), (0,)), ((), ())), preferred_element_type=jnp.float32
    )


def cross_cols(left_side, righthand_term):
    return lax.dot_general(
        left_side, righthand_term, (((1,), (1,)), ((), ())), preferred_element_type=jnp.float32
    )


def matmul(left_side, righthand_term):
    return jnp.dot(left_side, righthand_term, preferred_element_type=jnp.float32)


def general(prompts, responses, head_projection_matrix, positive):
    row_count = prompts.shape[0]
    col_count = head_projection_matrix.shape[1]
    factor = LOGIT_SCALE / math.sqrt(E)
    cycle_size = lax.axis_size("dp")
    position = lax.axis_index("dp")
    segment = lax.all_gather(head_projection_matrix, "dp", axis=0, tiled=True)
    prompt_emb = matmul(prompts, segment).astype(jnp.bfloat16)
    visiting = matmul(responses, segment).astype(jnp.bfloat16)
    local_ids = lax.iota(jnp.int32, row_count)
    prompt_gradient_total = jnp.zeros((row_count, col_count), jnp.float32)
    grad_response = jnp.zeros((row_count, col_count), jnp.float32)
    row_losses = jnp.zeros((row_count,), jnp.float32)
    for offset in range(STEPS):
        partial_logits = cross_cols(prompt_emb, visiting)
        pair_scores = lax.psum(partial_logits, "mp") * factor + LOGIT_BIAS
        anchor = (position - offset) % cycle_size
        column_ids = anchor * row_count + local_ids
        labels = jnp.where(positive[:, None] == column_ids[None, :], 1.0, -1.0).astype(jnp.float32)
        margin = -labels * pair_scores
        row_losses = row_losses + jnp.sum(jax.nn.softplus(margin), axis=1)
        pairwise_weight = (-labels * jax.nn.sigmoid(margin) * (factor / row_count)).astype(
            jnp.bfloat16
        )
        prompt_gradient_total = prompt_gradient_total + matmul(pairwise_weight, visiting)
        contribution = cross_rows(pairwise_weight, prompt_emb)
        if offset == 0:
            grad_response = contribution
        else:
            grad_response = grad_response + passed_along(contribution, "dp", -offset)
        if offset < STEPS - 1:
            visiting = passed_along(visiting, "dp", 1)
    grad_prompt_b = prompt_gradient_total.astype(jnp.bfloat16)
    grad_response_b = grad_response.astype(jnp.bfloat16)
    head_grad = lax.psum_scatter(
        cross_rows(prompts, grad_prompt_b) + cross_rows(responses, grad_response_b),
        "dp",
        scatter_dimension=0,
        tiled=True,
    )
    return (row_losses / row_count, head_grad)


LINE, PAIR, SIDE, CORES = 4, 2, 2, 2


def routes(move):
    table = []
    for z in range(LINE):
        for y in range(PAIR):
            for x in range(SIDE):
                for c in range(CORES):
                    goal = move(z, y, x, c)
                    if goal is not None:
                        gz, gy, gx, gc = goal
                        source = (z * PAIR + y) * SIDE * CORES + x * CORES + c
                        target = (gz * PAIR + gy) * SIDE * CORES + gx * CORES + gc
                        table.append((source, target))
    return table


def along_line(moves):
    return routes(lambda z, y, x, c: (moves[z], y, x, c) if z in moves else None)


def send(block, table):
    return lax.ppermute(block, ("dp", "mp"), table)


ACROSS_Y = routes(lambda z, y, x, c: (z, 1 - y, x, c))
ACROSS_X = routes(lambda z, y, x, c: (z, y, 1 - x, c))
ACROSS_XY = routes(lambda z, y, x, c: (z, 1 - y, 1 - x, c))
ACROSS_C = routes(lambda z, y, x, c: (z, y, x, 1 - c))
PAIRS = along_line({0: 1, 1: 0, 2: 3, 3: 2})
MIDDLE = along_line({1: 2, 2: 1})
OUTWARD = along_line({1: 0, 2: 3})
INWARD = along_line({0: 1, 3: 2})
TWO_OUT = along_line({1: 3, 2: 0})
TWO_IN = along_line({3: 1, 0: 2})
MIX = [routes(lambda z, y, x, c, k=k: (z, y, x ^ (k >> 1), c ^ (k & 1))) for k in range(4)]


def line_gather(block):
    first = send(block, PAIRS)
    middle = send(block, MIDDLE)
    second = send(first, MIDDLE) + send(middle, OUTWARD)
    third = middle + send(first, TWO_OUT)
    return first, second, third


def line_reduce(own, first, second, third):
    third_b, second_b = third.astype(jnp.bfloat16), second.astype(jnp.bfloat16)
    jumped = send(third_b, TWO_IN).astype(jnp.float32)
    inward = send(second_b, INWARD).astype(jnp.float32)
    across = send(second_b, MIDDLE).astype(jnp.float32)
    last = send((third + inward).astype(jnp.bfloat16), MIDDLE).astype(jnp.float32)
    paired = send((first + across + jumped).astype(jnp.bfloat16), PAIRS).astype(jnp.float32)
    return own + last + paired


def full_window(prompts, responses, head_projection_matrix, positive):
    row_count = prompts.shape[0]
    depth, width = head_projection_matrix.shape
    factor = LOGIT_SCALE / math.sqrt(E)
    dp, mp = lax.axis_index("dp"), lax.axis_index("mp")
    z, y = dp // PAIR, dp % PAIR
    quarter = row_count // (SIDE * CORES)
    both = jnp.concatenate([prompts, responses], axis=0)

    def features(line, pair):
        return lax.dynamic_slice_in_dim(both, (line * PAIR + pair) * depth, depth, axis=1)

    first, second, third = line_gather(head_projection_matrix)
    emb = jnp.zeros((2 * row_count, width), jnp.float32)
    for k, block in enumerate((head_projection_matrix, first, second, third)):
        emb = emb + matmul(features(z ^ k, y), block)
        emb = emb + matmul(features(z ^ k, 1 - y), send(block, ACROSS_Y))
    emb = emb.astype(jnp.bfloat16)
    prompt_emb, response_emb = emb[:row_count], emb[row_count:]

    pieces = []
    for k in range(SIDE * CORES):
        piece = lax.dynamic_slice_in_dim(response_emb, (mp ^ k) * quarter, quarter, axis=0)
        pieces.append(piece if k == 0 else send(piece, MIX[k]))
    response_rows = jnp.concatenate(pieces, axis=1)
    held = jnp.concatenate([response_rows, *line_gather(response_rows)], axis=0)

    near = jnp.concatenate([prompt_emb, send(prompt_emb, ACROSS_X)], axis=1)
    across = jnp.concatenate([send(prompt_emb, ACROSS_Y), send(prompt_emb, ACROSS_XY)], axis=1)
    half = jnp.concatenate([near, across], axis=0)
    other = send(half, ACROSS_C)
    plane = [half[:, :width], other[:, :width], half[:, width:], other[:, width:]]
    plane = jnp.concatenate(plane, axis=1)
    wanted = jnp.concatenate([positive, send(positive, ACROSS_Y)], axis=0)

    pair_scores = cross_cols(plane, held) * factor + LOGIT_BIAS
    lines = jnp.stack([z ^ k for k in range(LINE)])
    column_ids = ((lines * PAIR + y) * row_count + mp * quarter)[:, None] + lax.iota(
        jnp.int32, quarter
    )[None, :]
    column_ids = column_ids.reshape(-1)
    labels = jnp.where(wanted[:, None] == column_ids[None, :], 1.0, -1.0).astype(jnp.float32)
    margin = -labels * pair_scores
    losses = jnp.sum(jax.nn.softplus(margin), axis=1)
    weight = (-labels * jax.nn.sigmoid(margin) * (factor / row_count)).astype(jnp.bfloat16)

    parts = cross_rows(weight, plane)
    grad = line_reduce(*[parts[k * quarter : (k + 1) * quarter] for k in range(LINE)])
    grad = grad.astype(jnp.bfloat16)
    grad_response = jnp.zeros((row_count, width), jnp.bfloat16)
    for k in range(SIDE * CORES):
        piece = grad[:, k * width : (k + 1) * width]
        piece = piece if k == 0 else send(piece, MIX[k])
        grad_response = lax.dynamic_update_slice_in_dim(
            grad_response, piece, (mp ^ k) * quarter, axis=0
        )

    parts = matmul(weight, held)
    mine = jnp.concatenate([parts[:, :width], parts[:, 2 * width : 3 * width]], axis=1)
    away = jnp.concatenate([parts[:, width : 2 * width], parts[:, 3 * width :]], axis=1)
    mine = mine + send(away.astype(jnp.bfloat16), ACROSS_C).astype(jnp.float32)
    away = mine.astype(jnp.bfloat16)
    grad_prompt = (
        mine[:row_count, :width]
        + send(away[:row_count, width:], ACROSS_X).astype(jnp.float32)
        + send(away[row_count:, :width], ACROSS_Y).astype(jnp.float32)
        + send(away[row_count:, width:], ACROSS_XY).astype(jnp.float32)
    )
    grads = jnp.concatenate([grad_prompt.astype(jnp.bfloat16), grad_response], axis=0)

    def head(line):
        away = cross_rows(features(line, 1 - y), grads).astype(jnp.bfloat16)
        return cross_rows(features(line, y), grads) + send(away, ACROSS_Y).astype(jnp.float32)

    third, second, first, own = [head(z ^ k) for k in (3, 2, 1, 0)]
    head_grad = line_reduce(own, first, second, third)

    losses = losses[:row_count] + send(losses[row_count:], ACROSS_Y)
    losses = losses + send(losses, ACROSS_X)
    losses = losses + send(losses, ACROSS_C)
    return (losses / row_count, head_grad)


def per_device(prompts, responses, head_projection_matrix, positive):
    whole = lax.axis_size("dp") == STEPS == LINE * PAIR
    whole = whole and lax.axis_size("mp") == SIDE * CORES
    step = full_window if whole else general
    return step(prompts, responses, head_projection_matrix, positive)


def solution(mesh):
    return jax.shard_map(
        per_device,
        mesh=mesh,
        in_specs=(P("dp", None), P("dp", None), P("dp", "mp"), P("dp")),
        out_specs=(P("dp"), P("dp", "mp")),
        check_vma=False,
    )
```

```python
import math

import jax
import jax.numpy as jnp
from jax import lax
from jax.experimental import pallas as pl
from jax.experimental.pallas import tpu as pltpu
from jax.sharding import PartitionSpec as P

E = 1024
STEPS = 8


LOGIT_SCALE = 3.0
LOGIT_BIAS = -3.0


def passed_along(block, axis, distance):
    devices = range(lax.axis_size(axis))
    route = [((i - distance) % len(devices), i) for i in devices]
    return lax.ppermute(block, axis, route)


def cross_rows(left_side, righthand_term):
    return lax.dot_general(
        left_side, righthand_term, (((0,), (0,)), ((), ())), preferred_element_type=jnp.float32
    )


def cross_cols(left_side, righthand_term):
    return lax.dot_general(
        left_side, righthand_term, (((1,), (1,)), ((), ())), preferred_element_type=jnp.float32
    )


def matmul(left_side, righthand_term):
    return jnp.dot(left_side, righthand_term, preferred_element_type=jnp.float32)


def general(prompts, responses, head_projection_matrix, positive):
    row_count = prompts.shape[0]
    col_count = head_projection_matrix.shape[1]
    factor = LOGIT_SCALE / math.sqrt(E)
    cycle_size = lax.axis_size("dp")
    position = lax.axis_index("dp")
    segment = lax.all_gather(head_projection_matrix, "dp", axis=0, tiled=True)
    prompt_emb = matmul(prompts, segment).astype(jnp.bfloat16)
    visiting = matmul(responses, segment).astype(jnp.bfloat16)
    local_ids = lax.iota(jnp.int32, row_count)
    prompt_gradient_total = jnp.zeros((row_count, col_count), jnp.float32)
    grad_response = jnp.zeros((row_count, col_count), jnp.float32)
    row_losses = jnp.zeros((row_count,), jnp.float32)
    for offset in range(STEPS):
        partial_logits = cross_cols(prompt_emb, visiting)
        pair_scores = lax.psum(partial_logits, "mp") * factor + LOGIT_BIAS
        anchor = (position - offset) % cycle_size
        column_ids = anchor * row_count + local_ids
        labels = jnp.where(positive[:, None] == column_ids[None, :], 1.0, -1.0).astype(jnp.float32)
        margin = -labels * pair_scores
        row_losses = row_losses + jnp.sum(jax.nn.softplus(margin), axis=1)
        pairwise_weight = (-labels * jax.nn.sigmoid(margin) * (factor / row_count)).astype(
            jnp.bfloat16
        )
        prompt_gradient_total = prompt_gradient_total + matmul(pairwise_weight, visiting)
        contribution = cross_rows(pairwise_weight, prompt_emb)
        if offset == 0:
            grad_response = contribution
        else:
            grad_response = grad_response + passed_along(contribution, "dp", -offset)
        if offset < STEPS - 1:
            visiting = passed_along(visiting, "dp", 1)
    grad_prompt_b = prompt_gradient_total.astype(jnp.bfloat16)
    grad_response_b = grad_response.astype(jnp.bfloat16)
    head_grad = lax.psum_scatter(
        cross_rows(prompts, grad_prompt_b) + cross_rows(responses, grad_response_b),
        "dp",
        scatter_dimension=0,
        tiled=True,
    )
    return (row_losses / row_count, head_grad)


LINE, PAIR, SIDE, CORES = 4, 2, 2, 2


def routes(move):
    table = []
    for z in range(LINE):
        for y in range(PAIR):
            for x in range(SIDE):
                for c in range(CORES):
                    goal = move(z, y, x, c)
                    if goal is not None:
                        gz, gy, gx, gc = goal
                        source = (z * PAIR + y) * SIDE * CORES + x * CORES + c
                        target = (gz * PAIR + gy) * SIDE * CORES + gx * CORES + gc
                        table.append((source, target))
    return table


def along_line(moves):
    return routes(lambda z, y, x, c: (moves[z], y, x, c) if z in moves else None)


def send(block, table):
    return lax.ppermute(block, ("dp", "mp"), table)


ACROSS_Y = routes(lambda z, y, x, c: (z, 1 - y, x, c))
ACROSS_X = routes(lambda z, y, x, c: (z, y, 1 - x, c))
ACROSS_XY = routes(lambda z, y, x, c: (z, 1 - y, 1 - x, c))
ACROSS_C = routes(lambda z, y, x, c: (z, y, x, 1 - c))
PAIRS = along_line({0: 1, 1: 0, 2: 3, 3: 2})
MIDDLE = along_line({1: 2, 2: 1})
OUTWARD = along_line({1: 0, 2: 3})
INWARD = along_line({0: 1, 3: 2})
TWO_OUT = along_line({1: 3, 2: 0})
TWO_IN = along_line({3: 1, 0: 2})
MIX = [routes(lambda z, y, x, c, k=k: (z, y, x ^ (k >> 1), c ^ (k & 1))) for k in range(4)]


def line_gather(block):
    first = send(block, PAIRS)
    middle = send(block, MIDDLE)
    second = send(first, MIDDLE) + send(middle, OUTWARD)
    third = middle + send(first, TWO_OUT)
    return first, second, third


def line_reduce(own, first, second, third):
    third_b, second_b = third.astype(jnp.bfloat16), second.astype(jnp.bfloat16)
    jumped = send(third_b, TWO_IN).astype(jnp.float32)
    inward = send(second_b, INWARD).astype(jnp.float32)
    across = send(second_b, MIDDLE).astype(jnp.float32)
    last = send((third + inward).astype(jnp.bfloat16), MIDDLE).astype(jnp.float32)
    paired = send((first + across + jumped).astype(jnp.bfloat16), PAIRS).astype(jnp.float32)
    return own + last + paired


def project(prompts, responses, blocks, weights, total, kind):
    row_count = prompts.shape[0]
    depth, width = weights[0].shape
    count = len(weights)

    def kernel(block_ref, prompt_ref, response_ref, *refs):
        weight_refs, total_ref, out_ref, sum_ref = refs[:count], refs[count], refs[-2], refs[-1]
        step = pl.program_id(0)

        @pl.when(step == 0)
        def _():
            sum_ref[...] = total_ref[...] if total is not None else jnp.zeros_like(sum_ref)

        for k in range(count):

            @pl.when(step == k)
            def _(k=k):
                sum_ref[:row_count] += matmul(prompt_ref[...], weight_refs[k][...])
                sum_ref[row_count:] += matmul(response_ref[...], weight_refs[k][...])

        @pl.when(step == count - 1)
        def _():
            out_ref[...] = sum_ref[...].astype(out_ref.dtype)

    whole = pl.BlockSpec((2 * row_count, width), lambda i, block: (0, 0))
    piece = pl.BlockSpec((row_count, depth), lambda i, block: (0, block[i]))
    weight = pl.BlockSpec((depth, width), lambda i, block: (0, 0))
    operands = [prompts, responses, *weights] + ([total] if total is not None else [])
    return pl.pallas_call(
        kernel,
        grid_spec=pltpu.PrefetchScalarGridSpec(
            num_scalar_prefetch=1,
            grid=(count,),
            in_specs=[piece, piece] + [weight] * count + [whole] * (total is not None),
            out_specs=whole,
            scratch_shapes=[pltpu.VMEM((2 * row_count, width), jnp.float32)],
        ),
        out_shape=jax.ShapeDtypeStruct((2 * row_count, width), kind),
        compiler_params=pltpu.CompilerParams(vmem_limit_bytes=32 * 1024 * 1024),
        cost_estimate=pl.CostEstimate(
            flops=4 * count * row_count * depth * width,
            bytes_accessed=4 * count * row_count * depth + 2 * count * depth * width,
            transcendentals=0,
        ),
    )(jnp.stack(blocks).astype(jnp.int32), *operands)


def full_window(prompts, responses, head_projection_matrix, positive):
    row_count = prompts.shape[0]
    depth, width = head_projection_matrix.shape
    factor = LOGIT_SCALE / math.sqrt(E)
    dp, mp = lax.axis_index("dp"), lax.axis_index("mp")
    z, y, c = dp // PAIR, dp % PAIR, mp % CORES
    quarter = row_count // (SIDE * CORES)

    def features(array, line, pair):
        return lax.dynamic_slice_in_dim(array, (line * PAIR + pair) * depth, depth, axis=1)

    lines = [z ^ k for k in range(LINE)]
    own = head_projection_matrix
    own_y = send(own, ACROSS_Y)
    first, second, third = line_gather(own)
    first_y, second_y, third_y = [send(block, ACROSS_Y) for block in (first, second, third)]
    here = [line * PAIR + y for line in lines]
    there = [line * PAIR + 1 - y for line in lines]
    emb = project(
        prompts,
        responses,
        [here[0], there[0], here[1], there[1]],
        [own, own_y, first, first_y],
        None,
        jnp.float32,
    )
    emb = project(prompts, responses, [here[2], here[3]], [second, third], emb, jnp.float32)
    emb = project(prompts, responses, [there[2], there[3]], [second_y, third_y], emb, jnp.bfloat16)
    prompt_emb, response_emb = emb[:row_count], emb[row_count:]

    pieces = []
    for k in range(SIDE * CORES):
        piece = lax.dynamic_slice_in_dim(response_emb, (mp ^ k) * quarter, quarter, axis=0)
        pieces.append(piece if k == 0 else send(piece, MIX[k]))
    response_rows = jnp.concatenate(pieces, axis=1)
    held = jnp.concatenate([response_rows, *line_gather(response_rows)], axis=0)

    prompt_emb, response_rows = lax.optimization_barrier((prompt_emb, response_rows))
    near = jnp.concatenate([prompt_emb, send(prompt_emb, ACROSS_X)], axis=1)
    across = jnp.concatenate([send(prompt_emb, ACROSS_Y), send(prompt_emb, ACROSS_XY)], axis=1)
    half = jnp.concatenate([near, across], axis=0)
    other = send(half, ACROSS_C)
    plane = [half[:, :width], other[:, :width], half[:, width:], other[:, width:]]
    plane = jnp.concatenate(plane, axis=1)
    wanted = jnp.concatenate([positive, send(positive, ACROSS_Y)], axis=0)

    mine = jnp.where(c == 0, prompts, responses)
    mine = jnp.concatenate([features(mine, line, 1 - y) for line in lines], axis=1)
    mine, half = lax.optimization_barrier((mine, half))
    fetched = send(mine, ACROSS_Y)
    sibling = send(fetched, ACROSS_C)

    def turned(array):
        return [array[:, k * depth : (k + 1) * depth].T for k in range(LINE)]

    arrays = [[features(array, line, y).T for line in lines] for array in (prompts, responses)]
    arrays = arrays + [turned(fetched), turned(sibling)]
    columns = [jnp.concatenate([array[k] for array in arrays], axis=1) for k in range(LINE)]
    columns = lax.optimization_barrier(columns)

    pair_scores = cross_cols(plane, held) * factor + LOGIT_BIAS
    column_ids = ((jnp.stack(lines) * PAIR + y) * row_count + mp * quarter)[:, None] + lax.iota(
        jnp.int32, quarter
    )[None, :]
    column_ids = column_ids.reshape(-1)
    labels = jnp.where(wanted[:, None] == column_ids[None, :], 1.0, -1.0).astype(jnp.float32)
    margin = -labels * pair_scores
    losses = jnp.sum(jax.nn.softplus(margin), axis=1)
    weight = (-labels * jax.nn.sigmoid(margin) * (factor / row_count)).astype(jnp.bfloat16)

    parts = cross_rows(weight, plane)
    grad = line_reduce(*[parts[k * quarter : (k + 1) * quarter] for k in range(LINE)])
    grad = grad.astype(jnp.bfloat16)
    grad_response = jnp.zeros((row_count, width), jnp.bfloat16)
    for k in range(SIDE * CORES):
        piece = grad[:, k * width : (k + 1) * width]
        piece = piece if k == 0 else send(piece, MIX[k])
        grad_response = lax.dynamic_update_slice_in_dim(
            grad_response, piece, (mp ^ k) * quarter, axis=0
        )
    grad_response_y = send(grad_response, ACROSS_Y)

    parts = matmul(weight, held)
    mine = jnp.concatenate([parts[:, :width], parts[:, 2 * width : 3 * width]], axis=1)
    away = jnp.concatenate([parts[:, width : 2 * width], parts[:, 3 * width :]], axis=1)
    mine = mine + send(away.astype(jnp.bfloat16), ACROSS_C).astype(jnp.float32)
    mine = mine[:, :width] + send(mine[:, width:].astype(jnp.bfloat16), ACROSS_X).astype(
        jnp.float32
    )
    mine_y = send(mine.astype(jnp.bfloat16), ACROSS_Y).astype(jnp.float32)
    grad_prompt = (mine[:row_count] + mine_y[row_count:]).astype(jnp.bfloat16)
    grad_prompt_y = (mine[row_count:] + mine_y[:row_count]).astype(jnp.bfloat16)

    losses = losses[:row_count] + send(losses[row_count:], ACROSS_Y)
    losses = losses + send(losses, ACROSS_X)
    losses = losses + send(losses, ACROSS_C)
    losses, grad_response_y = lax.optimization_barrier((losses, grad_response_y))

    grads = [
        grad_prompt,
        grad_response,
        jnp.where(c == 0, grad_prompt_y, grad_response_y),
        jnp.where(c == 0, grad_response_y, grad_prompt_y),
    ]
    grads = jnp.concatenate(grads, axis=0)
    third, second, first, own = [matmul(columns[k], grads) for k in (3, 2, 1, 0)]
    head_grad = line_reduce(own, first, second, third)
    return (losses / row_count, head_grad)


def per_device(prompts, responses, head_projection_matrix, positive):
    whole = lax.axis_size("dp") == STEPS == LINE * PAIR
    whole = whole and lax.axis_size("mp") == SIDE * CORES
    step = full_window if whole else general
    return step(prompts, responses, head_projection_matrix, positive)


def solution(mesh):
    return jax.shard_map(
        per_device,
        mesh=mesh,
        in_specs=(P("dp", None), P("dp", None), P("dp", "mp"), P("dp")),
        out_specs=(P("dp"), P("dp", "mp")),
        check_vma=False,
    )
```

```python
import math

import jax
import jax.numpy as jnp
from jax import lax
from jax.experimental import pallas as pl
from jax.experimental.pallas import tpu as pltpu
from jax.sharding import PartitionSpec as P

E = 1024
STEPS = 8


LOGIT_SCALE = 3.0
LOGIT_BIAS = -3.0


def passed_along(block, axis, distance):
    devices = range(lax.axis_size(axis))
    route = [((i - distance) % len(devices), i) for i in devices]
    return lax.ppermute(block, axis, route)


def cross_rows(left_side, righthand_term):
    return lax.dot_general(
        left_side, righthand_term, (((0,), (0,)), ((), ())), preferred_element_type=jnp.float32
    )


def cross_cols(left_side, righthand_term):
    return lax.dot_general(
        left_side, righthand_term, (((1,), (1,)), ((), ())), preferred_element_type=jnp.float32
    )


def matmul(left_side, righthand_term):
    return jnp.dot(left_side, righthand_term, preferred_element_type=jnp.float32)


def general(prompts, responses, head_projection_matrix, positive):
    row_count = prompts.shape[0]
    col_count = head_projection_matrix.shape[1]
    factor = LOGIT_SCALE / math.sqrt(E)
    cycle_size = lax.axis_size("dp")
    position = lax.axis_index("dp")
    segment = lax.all_gather(head_projection_matrix, "dp", axis=0, tiled=True)
    prompt_emb = matmul(prompts, segment).astype(jnp.bfloat16)
    visiting = matmul(responses, segment).astype(jnp.bfloat16)
    local_ids = lax.iota(jnp.int32, row_count)
    prompt_gradient_total = jnp.zeros((row_count, col_count), jnp.float32)
    grad_response = jnp.zeros((row_count, col_count), jnp.float32)
    row_losses = jnp.zeros((row_count,), jnp.float32)
    for offset in range(STEPS):
        partial_logits = cross_cols(prompt_emb, visiting)
        pair_scores = lax.psum(partial_logits, "mp") * factor + LOGIT_BIAS
        anchor = (position - offset) % cycle_size
        column_ids = anchor * row_count + local_ids
        labels = jnp.where(positive[:, None] == column_ids[None, :], 1.0, -1.0).astype(jnp.float32)
        margin = -labels * pair_scores
        row_losses = row_losses + jnp.sum(jax.nn.softplus(margin), axis=1)
        pairwise_weight = (-labels * jax.nn.sigmoid(margin) * (factor / row_count)).astype(
            jnp.bfloat16
        )
        prompt_gradient_total = prompt_gradient_total + matmul(pairwise_weight, visiting)
        contribution = cross_rows(pairwise_weight, prompt_emb)
        if offset == 0:
            grad_response = contribution
        else:
            grad_response = grad_response + passed_along(contribution, "dp", -offset)
        if offset < STEPS - 1:
            visiting = passed_along(visiting, "dp", 1)
    grad_prompt_b = prompt_gradient_total.astype(jnp.bfloat16)
    grad_response_b = grad_response.astype(jnp.bfloat16)
    head_grad = lax.psum_scatter(
        cross_rows(prompts, grad_prompt_b) + cross_rows(responses, grad_response_b),
        "dp",
        scatter_dimension=0,
        tiled=True,
    )
    return (row_losses / row_count, head_grad)


LINE, PAIR, SIDE, CORES = 4, 2, 2, 2


def routes(move):
    table = []
    for z in range(LINE):
        for y in range(PAIR):
            for x in range(SIDE):
                for c in range(CORES):
                    goal = move(z, y, x, c)
                    if goal is not None:
                        gz, gy, gx, gc = goal
                        source = (z * PAIR + y) * SIDE * CORES + x * CORES + c
                        target = (gz * PAIR + gy) * SIDE * CORES + gx * CORES + gc
                        table.append((source, target))
    return table


def along_line(moves):
    return routes(lambda z, y, x, c: (moves[z], y, x, c) if z in moves else None)


def send(block, table):
    return lax.ppermute(block, ("dp", "mp"), table)


ACROSS_Y = routes(lambda z, y, x, c: (z, 1 - y, x, c))
ACROSS_X = routes(lambda z, y, x, c: (z, y, 1 - x, c))
ACROSS_XY = routes(lambda z, y, x, c: (z, 1 - y, 1 - x, c))
ACROSS_C = routes(lambda z, y, x, c: (z, y, x, 1 - c))
PAIRS = along_line({0: 1, 1: 0, 2: 3, 3: 2})
MIDDLE = along_line({1: 2, 2: 1})
OUTWARD = along_line({1: 0, 2: 3})
INWARD = along_line({0: 1, 3: 2})
TWO_OUT = along_line({1: 3, 2: 0})
TWO_IN = along_line({3: 1, 0: 2})
MIX = [routes(lambda z, y, x, c, k=k: (z, y, x ^ (k >> 1), c ^ (k & 1))) for k in range(4)]


def line_gather(block):
    first = send(block, PAIRS)
    middle = send(block, MIDDLE)
    second = send(first, MIDDLE) + send(middle, OUTWARD)
    third = middle + send(first, TWO_OUT)
    return first, second, third


def line_reduce(own, first, second, third):
    third_b, second_b = third.astype(jnp.bfloat16), second.astype(jnp.bfloat16)
    jumped, inward, across = lax.optimization_barrier(
        (send(third_b, TWO_IN), send(second_b, INWARD), send(second_b, MIDDLE))
    )
    jumped, inward, across = [block.astype(jnp.float32) for block in (jumped, inward, across)]
    last = send((third + inward).astype(jnp.bfloat16), MIDDLE).astype(jnp.float32)
    paired = send((first + across + jumped).astype(jnp.bfloat16), PAIRS).astype(jnp.float32)
    return own + last + paired


TAIL = 16


def with_tail(block, values):
    high = lax.reduce_precision(values, 8, 7)
    middle = lax.reduce_precision(values - high, 8, 7)
    terms = jnp.concatenate([high, middle, values - high - middle])
    rows = jnp.pad(terms, (0, TAIL * block.shape[1] - terms.size)).reshape(TAIL, -1)
    return jnp.concatenate([block.astype(jnp.bfloat16), rows.astype(jnp.bfloat16)], axis=0)


def tail_of(message, values):
    terms = message[-TAIL:].astype(jnp.float32).reshape(-1)[: 3 * values.size].reshape(3, -1)
    return terms[0] + terms[1] + terms[2]


def project(prompts, responses, blocks, weights, total, kind):
    row_count = prompts.shape[0]
    depth, width = weights[0].shape
    count = len(weights)

    def kernel(block_ref, prompt_ref, response_ref, *refs):
        weight_refs, total_ref, out_ref, sum_ref = refs[:count], refs[count], refs[-2], refs[-1]
        step = pl.program_id(0)

        @pl.when(step == 0)
        def _():
            sum_ref[...] = total_ref[...] if total is not None else jnp.zeros_like(sum_ref)

        for k in range(count):

            @pl.when(step == k)
            def _(k=k):
                sum_ref[:row_count] += matmul(prompt_ref[...], weight_refs[k][...])
                sum_ref[row_count:] += matmul(response_ref[...], weight_refs[k][...])

        @pl.when(step == count - 1)
        def _():
            out_ref[...] = sum_ref[...].astype(out_ref.dtype)

    whole = pl.BlockSpec((2 * row_count, width), lambda i, block: (0, 0))
    piece = pl.BlockSpec((row_count, depth), lambda i, block: (0, block[i]))
    weight = pl.BlockSpec((depth, width), lambda i, block: (0, 0))
    operands = [prompts, responses, *weights] + ([total] if total is not None else [])
    return pl.pallas_call(
        kernel,
        grid_spec=pltpu.PrefetchScalarGridSpec(
            num_scalar_prefetch=1,
            grid=(count,),
            in_specs=[piece, piece] + [weight] * count + [whole] * (total is not None),
            out_specs=whole,
            scratch_shapes=[pltpu.VMEM((2 * row_count, width), jnp.float32)],
        ),
        out_shape=jax.ShapeDtypeStruct((2 * row_count, width), kind),
        compiler_params=pltpu.CompilerParams(vmem_limit_bytes=32 * 1024 * 1024),
        cost_estimate=pl.CostEstimate(
            flops=4 * count * row_count * depth * width,
            bytes_accessed=4 * count * row_count * depth + 2 * count * depth * width,
            transcendentals=0,
        ),
    )(jnp.stack(blocks).astype(jnp.int32), *operands)


def full_window(prompts, responses, head_projection_matrix, positive):
    row_count = prompts.shape[0]
    depth, width = head_projection_matrix.shape
    factor = LOGIT_SCALE / math.sqrt(E)
    dp, mp = lax.axis_index("dp"), lax.axis_index("mp")
    z, y, c = dp // PAIR, dp % PAIR, mp % CORES
    quarter = row_count // (SIDE * CORES)

    def features(array, line, pair):
        return lax.dynamic_slice_in_dim(array, (line * PAIR + pair) * depth, depth, axis=1)

    lines = [z ^ k for k in range(LINE)]
    own = head_projection_matrix
    own_y = send(own, ACROSS_Y)
    first, second, third = line_gather(own)
    first_y, second_y, third_y = [send(block, ACROSS_Y) for block in (first, second, third)]
    here = [line * PAIR + y for line in lines]
    there = [line * PAIR + 1 - y for line in lines]
    emb = project(
        prompts,
        responses,
        [here[0], there[0], here[1], there[1]],
        [own, own_y, first, first_y],
        None,
        jnp.float32,
    )
    emb = project(prompts, responses, [here[2], here[3]], [second, third], emb, jnp.float32)
    emb = project(prompts, responses, [there[2], there[3]], [second_y, third_y], emb, jnp.bfloat16)
    prompt_emb, response_emb = emb[:row_count], emb[row_count:]

    pieces = []
    for k in range(SIDE * CORES):
        piece = lax.dynamic_slice_in_dim(response_emb, (mp ^ k) * quarter, quarter, axis=0)
        pieces.append(piece if k == 0 else send(piece, MIX[k]))
    response_rows = jnp.concatenate(pieces, axis=1)
    held = jnp.concatenate([response_rows, *line_gather(response_rows)], axis=0)

    near = jnp.concatenate([prompt_emb, send(prompt_emb, ACROSS_X)], axis=1)
    half = jnp.concatenate([near, send(near, ACROSS_Y)], axis=0)
    other = send(half, ACROSS_C)
    plane = [half[:, :width], other[:, :width], half[:, width:], other[:, width:]]
    plane = jnp.concatenate(plane, axis=1)
    wanted = jnp.concatenate([positive, send(positive, ACROSS_Y)], axis=0)

    mine = jnp.where(c == 0, prompts, responses)
    mine = jnp.concatenate([features(mine, line, 1 - y) for line in lines], axis=1)
    mine, half = lax.optimization_barrier((mine, half))
    fetched = send(mine, ACROSS_Y)
    sibling = send(fetched, ACROSS_C)

    def turned(array):
        return [array[:, k * depth : (k + 1) * depth].T for k in range(LINE)]

    arrays = [[features(array, line, y).T for line in lines] for array in (prompts, responses)]
    arrays = arrays + [turned(fetched), turned(sibling)]
    columns = [jnp.concatenate([array[k] for array in arrays], axis=1) for k in range(LINE)]
    columns = lax.optimization_barrier(columns)

    pair_scores = cross_cols(plane, held) * factor + LOGIT_BIAS
    column_ids = ((jnp.stack(lines) * PAIR + y) * row_count + mp * quarter)[:, None] + lax.iota(
        jnp.int32, quarter
    )[None, :]
    column_ids = column_ids.reshape(-1)
    labels = jnp.where(wanted[:, None] == column_ids[None, :], 1.0, -1.0).astype(jnp.float32)
    margin = -labels * pair_scores
    losses = jnp.sum(jax.nn.softplus(margin), axis=1)
    weight = (-labels * jax.nn.sigmoid(margin) * (factor / row_count)).astype(jnp.bfloat16)

    parts = cross_rows(weight, plane)
    grad = line_reduce(*[parts[k * quarter : (k + 1) * quarter] for k in range(LINE)])
    grad = grad.astype(jnp.bfloat16)

    parts = matmul(weight, held)
    mine = jnp.concatenate([parts[:, :width], parts[:, 2 * width : 3 * width]], axis=1)
    away = jnp.concatenate([parts[:, width : 2 * width], parts[:, 3 * width :]], axis=1)
    message = send(with_tail(away, losses), ACROSS_C)
    losses = losses + tail_of(message, losses)
    mine = mine + message[: 2 * row_count].astype(jnp.float32)
    message = send(with_tail(mine[:, width:], losses), ACROSS_X)
    losses = losses + tail_of(message, losses)
    mine = mine[:, :width] + message[: 2 * row_count].astype(jnp.float32)
    grad, mine, losses = lax.optimization_barrier((grad, mine, losses))
    message = send(with_tail(mine, losses), ACROSS_Y)
    losses = losses[:row_count] + tail_of(message, losses)[row_count:]
    mine_y = message[: 2 * row_count].astype(jnp.float32)
    grad_prompt = (mine[:row_count] + mine_y[row_count:]).astype(jnp.bfloat16)
    grad_prompt_y = (mine[row_count:] + mine_y[:row_count]).astype(jnp.bfloat16)

    grad_response = jnp.zeros((row_count, width), jnp.bfloat16)
    for k in range(SIDE * CORES):
        piece = grad[:, k * width : (k + 1) * width]
        piece = piece if k == 0 else send(piece, MIX[k])
        grad_response = lax.dynamic_update_slice_in_dim(
            grad_response, piece, (mp ^ k) * quarter, axis=0
        )
    grad_response_y = send(grad_response, ACROSS_Y)
    grads = [
        grad_prompt,
        grad_response,
        jnp.where(c == 0, grad_prompt_y, grad_response_y),
        jnp.where(c == 0, grad_response_y, grad_prompt_y),
    ]
    grads = jnp.concatenate(grads, axis=0)
    third, second, first, own = [matmul(columns[k], grads) for k in (3, 2, 1, 0)]
    head_grad = line_reduce(own, first, second, third)
    return (losses / row_count, head_grad)


def per_device(prompts, responses, head_projection_matrix, positive):
    whole = lax.axis_size("dp") == STEPS == LINE * PAIR
    whole = whole and lax.axis_size("mp") == SIDE * CORES
    step = full_window if whole else general
    return step(prompts, responses, head_projection_matrix, positive)


def solution(mesh):
    return jax.shard_map(
        per_device,
        mesh=mesh,
        in_specs=(P("dp", None), P("dp", None), P("dp", "mp"), P("dp")),
        out_specs=(P("dp"), P("dp", "mp")),
        check_vma=False,
    )
```

```python
import math

import jax
import jax.numpy as jnp
from jax import lax
from jax.experimental import pallas as pl
from jax.experimental.pallas import tpu as pltpu
from jax.sharding import PartitionSpec as P

E = 1024
STEPS = 8


LOGIT_SCALE = 3.0
LOGIT_BIAS = -3.0


def passed_along(block, axis, distance):
    devices = range(lax.axis_size(axis))
    route = [((i - distance) % len(devices), i) for i in devices]
    return lax.ppermute(block, axis, route)


def cross_rows(left_side, righthand_term):
    return lax.dot_general(
        left_side, righthand_term, (((0,), (0,)), ((), ())), preferred_element_type=jnp.float32
    )


def cross_cols(left_side, righthand_term):
    return lax.dot_general(
        left_side, righthand_term, (((1,), (1,)), ((), ())), preferred_element_type=jnp.float32
    )


def matmul(left_side, righthand_term):
    return jnp.dot(left_side, righthand_term, preferred_element_type=jnp.float32)


def general(prompts, responses, head_projection_matrix, positive):
    row_count = prompts.shape[0]
    col_count = head_projection_matrix.shape[1]
    factor = LOGIT_SCALE / math.sqrt(E)
    cycle_size = lax.axis_size("dp")
    position = lax.axis_index("dp")
    segment = lax.all_gather(head_projection_matrix, "dp", axis=0, tiled=True)
    prompt_emb = matmul(prompts, segment).astype(jnp.bfloat16)
    visiting = matmul(responses, segment).astype(jnp.bfloat16)
    local_ids = lax.iota(jnp.int32, row_count)
    prompt_gradient_total = jnp.zeros((row_count, col_count), jnp.float32)
    grad_response = jnp.zeros((row_count, col_count), jnp.float32)
    row_losses = jnp.zeros((row_count,), jnp.float32)
    for offset in range(STEPS):
        partial_logits = cross_cols(prompt_emb, visiting)
        pair_scores = lax.psum(partial_logits, "mp") * factor + LOGIT_BIAS
        anchor = (position - offset) % cycle_size
        column_ids = anchor * row_count + local_ids
        labels = jnp.where(positive[:, None] == column_ids[None, :], 1.0, -1.0).astype(jnp.float32)
        margin = -labels * pair_scores
        row_losses = row_losses + jnp.sum(jax.nn.softplus(margin), axis=1)
        pairwise_weight = (-labels * jax.nn.sigmoid(margin) * (factor / row_count)).astype(
            jnp.bfloat16
        )
        prompt_gradient_total = prompt_gradient_total + matmul(pairwise_weight, visiting)
        contribution = cross_rows(pairwise_weight, prompt_emb)
        if offset == 0:
            grad_response = contribution
        else:
            grad_response = grad_response + passed_along(contribution, "dp", -offset)
        if offset < STEPS - 1:
            visiting = passed_along(visiting, "dp", 1)
    grad_prompt_b = prompt_gradient_total.astype(jnp.bfloat16)
    grad_response_b = grad_response.astype(jnp.bfloat16)
    head_grad = lax.psum_scatter(
        cross_rows(prompts, grad_prompt_b) + cross_rows(responses, grad_response_b),
        "dp",
        scatter_dimension=0,
        tiled=True,
    )
    return (row_losses / row_count, head_grad)


LINE, PAIR, SIDE, CORES = 4, 2, 2, 2


def routes(move):
    table = []
    for z in range(LINE):
        for y in range(PAIR):
            for x in range(SIDE):
                for c in range(CORES):
                    goal = move(z, y, x, c)
                    if goal is not None:
                        gz, gy, gx, gc = goal
                        source = (z * PAIR + y) * SIDE * CORES + x * CORES + c
                        target = (gz * PAIR + gy) * SIDE * CORES + gx * CORES + gc
                        table.append((source, target))
    return table


def along_line(moves):
    return routes(lambda z, y, x, c: (moves[z], y, x, c) if z in moves else None)


def send(block, table):
    return lax.ppermute(block, ("dp", "mp"), table)


ACROSS_Y = routes(lambda z, y, x, c: (z, 1 - y, x, c))
ACROSS_X = routes(lambda z, y, x, c: (z, y, 1 - x, c))
ACROSS_XY = routes(lambda z, y, x, c: (z, 1 - y, 1 - x, c))
ACROSS_C = routes(lambda z, y, x, c: (z, y, x, 1 - c))
PAIRS = along_line({0: 1, 1: 0, 2: 3, 3: 2})
MIDDLE = along_line({1: 2, 2: 1})
OUTWARD = along_line({1: 0, 2: 3})
INWARD = along_line({0: 1, 3: 2})
TWO_OUT = along_line({1: 3, 2: 0})
TWO_IN = along_line({3: 1, 0: 2})
PLANE = [
    routes(lambda z, y, x, c, k=k: (z, y ^ (k >> 2), x ^ (k >> 1 & 1), c ^ (k & 1)))
    for k in range(PAIR * SIDE * CORES)
]


def line_gather(block):
    first = send(block, PAIRS)
    middle = send(block, MIDDLE)
    return first, (send(first, MIDDLE), send(middle, OUTWARD)), (middle, send(first, TWO_OUT))


def line_reduce(own, first, second, third, second_b, third_b, beside=(), later=()):
    jumped, inward, across = send(third_b, TWO_IN), send(second_b, INWARD), send(second_b, MIDDLE)
    jumped, inward, across, *beside = lax.optimization_barrier((jumped, inward, across, *beside))
    jumped, inward, across = [block.astype(jnp.float32) for block in (jumped, inward, across)]
    paired = send((first + across + jumped).astype(jnp.bfloat16), PAIRS)
    last = send((third + inward).astype(jnp.bfloat16), MIDDLE)
    later = later(*beside) if later else ()
    last, paired, *later = lax.optimization_barrier((last, paired, *later))
    return own + last.astype(jnp.float32) + paired.astype(jnp.float32), beside, later


def project(prompts, responses, blocks, weights, total, kind):
    row_count = prompts.shape[0]
    depth, width = weights[0][0].shape
    count = len(weights)
    terms = [term for weight in weights for term in weight]

    def kernel(block_ref, prompt_ref, response_ref, *refs):
        term_refs = list(refs[: len(terms)])
        total_ref, out_ref, sum_ref = refs[len(terms)], refs[-2], refs[-1]
        step = pl.program_id(0)

        @pl.when(step == 0)
        def _():
            sum_ref[...] = total_ref[...] if total is not None else jnp.zeros_like(sum_ref)

        for k, weight in enumerate(weights):
            mine = [term_refs.pop(0) for _ in weight]

            @pl.when(step == k)
            def _(mine=mine):
                block = mine[0][...]
                for ref in mine[1:]:
                    block = block + ref[...]
                sum_ref[:row_count] += matmul(prompt_ref[...], block)
                sum_ref[row_count:] += matmul(response_ref[...], block)

        @pl.when(step == count - 1)
        def _():
            out_ref[...] = sum_ref[...].astype(out_ref.dtype)

    whole = pl.BlockSpec((2 * row_count, width), lambda i, block: (0, 0))
    piece = pl.BlockSpec((row_count, depth), lambda i, block: (0, block[i]))
    term = pl.BlockSpec((depth, width), lambda i, block: (0, 0))
    operands = [prompts, responses, *terms] + ([total] if total is not None else [])
    return pl.pallas_call(
        kernel,
        grid_spec=pltpu.PrefetchScalarGridSpec(
            num_scalar_prefetch=1,
            grid=(count,),
            in_specs=[piece, piece] + [term] * len(terms) + [whole] * (total is not None),
            out_specs=whole,
            scratch_shapes=[pltpu.VMEM((2 * row_count, width), jnp.float32)],
        ),
        out_shape=jax.ShapeDtypeStruct((2 * row_count, width), kind),
        compiler_params=pltpu.CompilerParams(vmem_limit_bytes=32 * 1024 * 1024),
        cost_estimate=pl.CostEstimate(
            flops=4 * count * row_count * depth * width,
            bytes_accessed=4 * count * row_count * depth + 2 * len(terms) * depth * width,
            transcendentals=0,
        ),
    )(jnp.stack(blocks).astype(jnp.int32), *operands)


def compare(half, other, held, wanted, ids, row_count):
    prompt_rows, width = half.shape[0], half.shape[1] // 2
    quarter = held[0][0].shape[0]
    count = len(held) * quarter
    factor = LOGIT_SCALE / math.sqrt(E)
    terms = [term for block in held for term in block]

    def kernel(half_ref, other_ref, wanted_ref, ids_ref, *refs):
        term_refs, refs = list(refs[: len(terms)]), refs[len(terms) :]
        loss_ref, mine_ref, away_ref, parts_ref, second_ref, third_ref, rows_ref = refs
        for k, block in enumerate(held):
            mine = [term_refs.pop(0)[...] for _ in block]
            rows_ref[k * quarter : (k + 1) * quarter] = sum(mine[1:], mine[0])
        sources = [
            (half_ref, 0, mine_ref, 0),
            (other_ref, 0, away_ref, 0),
            (half_ref, 1, mine_ref, 1),
            (other_ref, 1, away_ref, 1),
        ]
        scores = jnp.zeros((prompt_rows, count), jnp.float32)
        for k, (ref, place, _, _) in enumerate(sources):
            scores += cross_cols(
                ref[:, place * width : (place + 1) * width],
                rows_ref[:, k * width : (k + 1) * width],
            )
        scores = scores * factor + LOGIT_BIAS
        match = wanted_ref[...] == ids_ref[...]
        margin = jnp.where(match, -scores, scores)
        small = jnp.exp(-jnp.abs(margin))
        loss_ref[...] = jnp.sum(
            jnp.maximum(margin, 0.0) + jnp.log1p(small), axis=1, keepdims=True
        )
        share = jnp.where(margin >= 0.0, 1.0, small) / (1.0 + small)
        share = share * (factor / row_count)
        weight = jnp.where(match, -share, share).astype(jnp.bfloat16)
        for k, (ref, place, out, goal) in enumerate(sources):
            columns = slice(k * width, (k + 1) * width)
            part = cross_rows(weight, ref[:, place * width : (place + 1) * width])
            parts_ref[:, columns] = part
            second_ref[:, columns] = part[2 * quarter : 3 * quarter].astype(jnp.bfloat16)
            third_ref[:, columns] = part[3 * quarter :].astype(jnp.bfloat16)
            part = matmul(weight, rows_ref[:, columns])
            out[:, goal * width : (goal + 1) * width] = part.astype(out.dtype)

    full = half.shape[1] * 2
    return pl.pallas_call(
        kernel,
        out_shape=[
            jax.ShapeDtypeStruct((prompt_rows, 1), jnp.float32),
            jax.ShapeDtypeStruct((prompt_rows, 2 * width), jnp.float32),
            jax.ShapeDtypeStruct((prompt_rows, 2 * width), jnp.bfloat16),
            jax.ShapeDtypeStruct((count, full), jnp.float32),
            jax.ShapeDtypeStruct((quarter, full), jnp.bfloat16),
            jax.ShapeDtypeStruct((quarter, full), jnp.bfloat16),
        ],
        scratch_shapes=[pltpu.VMEM((count, full), jnp.bfloat16)],
        compiler_params=pltpu.CompilerParams(vmem_limit_bytes=32 * 1024 * 1024),
        cost_estimate=pl.CostEstimate(
            flops=6 * prompt_rows * count * full,
            bytes_accessed=6 * prompt_rows * full + 6 * count * full,
            transcendentals=2 * prompt_rows * count,
        ),
    )(half, other, wanted, ids, *terms)


def full_window(prompts, responses, head_projection_matrix, positive):
    row_count = prompts.shape[0]
    depth, width = head_projection_matrix.shape
    dp, mp = lax.axis_index("dp"), lax.axis_index("mp")
    z, y, c = dp // PAIR, dp % PAIR, mp % CORES
    quarter = row_count // (SIDE * CORES)

    def features(array, line, pair):
        return lax.dynamic_slice_in_dim(array, (line * PAIR + pair) * depth, depth, axis=1)

    lines = [z ^ k for k in range(LINE)]
    here = [line * PAIR + y for line in lines]
    there = [line * PAIR + 1 - y for line in lines]
    own = head_projection_matrix
    first, middle = send(own, PAIRS), send(own, MIDDLE)
    inner, outer = send(first, MIDDLE), send(middle, OUTWARD)
    last = send(inner, OUTWARD)
    own_y, first_y, middle_y, inner_y, outer_y, last_y = [
        send(block, ACROSS_Y) for block in (own, first, middle, inner, outer, last)
    ]
    emb = project(
        prompts,
        responses,
        [here[0], there[0], here[1], there[1]],
        [(own,), (own_y,), (first,), (first_y,)],
        None,
        jnp.float32,
    )
    emb = project(
        prompts,
        responses,
        [here[2], there[2], here[3]],
        [(inner, outer), (inner_y, outer_y), (middle, last)],
        emb,
        jnp.float32,
    )
    emb = project(prompts, responses, [there[3]], [(middle_y, last_y)], emb, jnp.bfloat16)
    prompt_emb, response_emb = emb[:row_count], emb[row_count:]

    pieces = []
    for k in range(SIDE * CORES):
        piece = lax.dynamic_slice_in_dim(response_emb, (mp ^ k) * quarter, quarter, axis=0)
        pieces.append(piece if k == 0 else send(piece, PLANE[k]))
    prompt_emb, pieces[1] = lax.optimization_barrier((prompt_emb, pieces[1]))
    response_rows = jnp.concatenate(pieces, axis=1)
    first, second, third = line_gather(response_rows)
    held = [(response_rows,), (first,), second, third]

    near = jnp.concatenate([prompt_emb, send(prompt_emb, ACROSS_X)], axis=1)
    half = jnp.concatenate([near, send(near, ACROSS_Y)], axis=0)
    other = send(half, ACROSS_C)
    wanted = jnp.concatenate([positive, send(positive, ACROSS_Y)], axis=0)
    ids = ((jnp.stack(lines) * PAIR + y) * row_count + mp * quarter)[:, None] + lax.iota(
        jnp.int32, quarter
    )[None, :]

    mine = jnp.where(c == 0, prompts, responses)
    mine = jnp.concatenate([features(mine, line, 1 - y) for line in lines], axis=1)
    mine, half = lax.optimization_barrier((mine, half))
    fetched = send(mine, ACROSS_Y)
    sibling = send(fetched, ACROSS_C)

    def turned(array):
        return [array[:, k * depth : (k + 1) * depth].T for k in range(LINE)]

    arrays = [[features(array, line, y).T for line in lines] for array in (prompts, responses)]
    arrays = arrays + [turned(fetched), turned(sibling)]
    columns = [jnp.concatenate([array[k] for array in arrays], axis=1) for k in range(LINE)]
    columns = lax.optimization_barrier(columns)

    losses, mine, away, parts, second_b, third_b = compare(
        half, other, held, wanted[:, None], ids.reshape(1, -1), row_count
    )
    losses = losses[:, 0]
    losses = losses[:row_count], send(losses[row_count:], ACROSS_Y)

    mine = mine + send(away, ACROSS_C).astype(jnp.float32)
    aside = send(mine[:, width:].astype(jnp.bfloat16), ACROSS_X)

    def after(aside, loss):
        loss = losses[0] + loss
        return loss, send(loss, ACROSS_X)

    grad, (aside, _), losses = line_reduce(
        *[parts[k * quarter : (k + 1) * quarter] for k in range(LINE)],
        second_b,
        third_b,
        (aside, losses[1]),
        after,
    )
    mine = mine[:, :width] + aside.astype(jnp.float32)
    mine_y = send(mine.astype(jnp.bfloat16), ACROSS_Y).astype(jnp.float32)
    grad_prompt = (mine[:row_count] + mine_y[row_count:]).astype(jnp.bfloat16)
    grad_prompt_y = (mine[row_count:] + mine_y[:row_count]).astype(jnp.bfloat16)
    grad = grad.astype(jnp.bfloat16)
    gathered = [jnp.zeros((row_count, width), jnp.bfloat16)] * PAIR
    for k in range(PAIR * SIDE * CORES):
        pair, away = divmod(k, SIDE * CORES)
        piece = grad[:, away * width : (away + 1) * width]
        piece = piece if k == 0 else send(piece, PLANE[k])
        gathered[pair] = lax.dynamic_update_slice_in_dim(
            gathered[pair], piece, (mp ^ away) * quarter, axis=0
        )
    grad_response, grad_response_y = gathered
    losses = losses[0] + losses[1]
    losses = losses + send(losses, ACROSS_C)

    grads = [
        grad_prompt,
        grad_response,
        jnp.where(c == 0, grad_prompt_y, grad_response_y),
        jnp.where(c == 0, grad_response_y, grad_prompt_y),
    ]
    grads = jnp.concatenate(grads, axis=0)
    third = matmul(columns[3], grads)
    third_b, grads = lax.optimization_barrier((third.astype(jnp.bfloat16), grads))
    second, first, own = [matmul(columns[k], grads) for k in (2, 1, 0)]
    head_grad, _, _ = line_reduce(own, first, second, third, second.astype(jnp.bfloat16), third_b)
    return (losses / row_count, head_grad)


def per_device(prompts, responses, head_projection_matrix, positive):
    whole = lax.axis_size("dp") == STEPS == LINE * PAIR
    whole = whole and lax.axis_size("mp") == SIDE * CORES
    step = full_window if whole else general
    return step(prompts, responses, head_projection_matrix, positive)


def solution(mesh):
    return jax.shard_map(
        per_device,
        mesh=mesh,
        in_specs=(P("dp", None), P("dp", None), P("dp", "mp"), P("dp")),
        out_specs=(P("dp"), P("dp", "mp")),
        check_vma=False,
    )
```

```python
import math

import jax
import jax.numpy as jnp
from jax import lax
from jax.experimental import pallas as pl
from jax.experimental.pallas import tpu as pltpu
from jax.sharding import PartitionSpec as P

E = 1024
STEPS = 8


LOGIT_SCALE = 3.0
LOGIT_BIAS = -3.0


def passed_along(block, axis, distance):
    devices = range(lax.axis_size(axis))
    route = [((i - distance) % len(devices), i) for i in devices]
    return lax.ppermute(block, axis, route)


def cross_rows(left_side, righthand_term):
    return lax.dot_general(
        left_side, righthand_term, (((0,), (0,)), ((), ())), preferred_element_type=jnp.float32
    )


def cross_cols(left_side, righthand_term):
    return lax.dot_general(
        left_side, righthand_term, (((1,), (1,)), ((), ())), preferred_element_type=jnp.float32
    )


def matmul(left_side, righthand_term):
    return jnp.dot(left_side, righthand_term, preferred_element_type=jnp.float32)


def general(prompts, responses, head_projection_matrix, positive):
    row_count = prompts.shape[0]
    col_count = head_projection_matrix.shape[1]
    factor = LOGIT_SCALE / math.sqrt(E)
    cycle_size = lax.axis_size("dp")
    position = lax.axis_index("dp")
    segment = lax.all_gather(head_projection_matrix, "dp", axis=0, tiled=True)
    prompt_emb = matmul(prompts, segment).astype(jnp.bfloat16)
    visiting = matmul(responses, segment).astype(jnp.bfloat16)
    local_ids = lax.iota(jnp.int32, row_count)
    prompt_gradient_total = jnp.zeros((row_count, col_count), jnp.float32)
    grad_response = jnp.zeros((row_count, col_count), jnp.float32)
    row_losses = jnp.zeros((row_count,), jnp.float32)
    for offset in range(STEPS):
        partial_logits = cross_cols(prompt_emb, visiting)
        pair_scores = lax.psum(partial_logits, "mp") * factor + LOGIT_BIAS
        anchor = (position - offset) % cycle_size
        column_ids = anchor * row_count + local_ids
        labels = jnp.where(positive[:, None] == column_ids[None, :], 1.0, -1.0).astype(jnp.float32)
        margin = -labels * pair_scores
        row_losses = row_losses + jnp.sum(jax.nn.softplus(margin), axis=1)
        pairwise_weight = (-labels * jax.nn.sigmoid(margin) * (factor / row_count)).astype(
            jnp.bfloat16
        )
        prompt_gradient_total = prompt_gradient_total + matmul(pairwise_weight, visiting)
        contribution = cross_rows(pairwise_weight, prompt_emb)
        if offset == 0:
            grad_response = contribution
        else:
            grad_response = grad_response + passed_along(contribution, "dp", -offset)
        if offset < STEPS - 1:
            visiting = passed_along(visiting, "dp", 1)
    grad_prompt_b = prompt_gradient_total.astype(jnp.bfloat16)
    grad_response_b = grad_response.astype(jnp.bfloat16)
    head_grad = lax.psum_scatter(
        cross_rows(prompts, grad_prompt_b) + cross_rows(responses, grad_response_b),
        "dp",
        scatter_dimension=0,
        tiled=True,
    )
    return (row_losses / row_count, head_grad)


LINE, PAIR, SIDE, CORES = 4, 2, 2, 2


def routes(move):
    table = []
    for z in range(LINE):
        for y in range(PAIR):
            for x in range(SIDE):
                for c in range(CORES):
                    goal = move(z, y, x, c)
                    if goal is not None:
                        gz, gy, gx, gc = goal
                        source = (z * PAIR + y) * SIDE * CORES + x * CORES + c
                        target = (gz * PAIR + gy) * SIDE * CORES + gx * CORES + gc
                        table.append((source, target))
    return table


def along_line(moves):
    return routes(lambda z, y, x, c: (moves[z], y, x, c) if z in moves else None)


def send(block, table):
    return lax.ppermute(block, ("dp", "mp"), table)


ACROSS_Y = routes(lambda z, y, x, c: (z, 1 - y, x, c))
ACROSS_X = routes(lambda z, y, x, c: (z, y, 1 - x, c))
Y_ENDS = routes(lambda z, y, x, c: (z, 1 - y, x, c) if z in (0, 3) else None)
Y_MIDDLE = routes(lambda z, y, x, c: (z, 1 - y, x, c) if z in (1, 2) else None)
ACROSS_C = routes(lambda z, y, x, c: (z, y, x, 1 - c))
PAIRS = along_line({0: 1, 1: 0, 2: 3, 3: 2})
MIDDLE = along_line({1: 2, 2: 1})
OUTWARD = along_line({1: 0, 2: 3})
INWARD = along_line({0: 1, 3: 2})
TWO_OUT = along_line({1: 3, 2: 0})
TWO_IN = along_line({3: 1, 0: 2})
MIX = [routes(lambda z, y, x, c, k=k: (z, y, x ^ (k >> 1), c ^ (k & 1))) for k in range(4)]


def line_gather(block):
    first = send(block, PAIRS)
    middle = send(block, MIDDLE)
    return first, (send(first, MIDDLE), send(middle, OUTWARD)), (middle, send(first, TWO_OUT))


def line_reduce(own, first, second, third, second_b, third_b, beside=(), later=()):
    jumped, inward, across = send(third_b, TWO_IN), send(second_b, INWARD), send(second_b, MIDDLE)
    jumped, inward, across, *beside = lax.optimization_barrier((jumped, inward, across, *beside))
    jumped, inward, across = [block.astype(jnp.float32) for block in (jumped, inward, across)]
    paired = send((first + across + jumped).astype(jnp.bfloat16), PAIRS)
    last = send((third + inward).astype(jnp.bfloat16), MIDDLE)
    later = later(*beside) if later else ()
    last, paired, *later = lax.optimization_barrier((last, paired, *later))
    return own + last.astype(jnp.float32) + paired.astype(jnp.float32), beside, later


def place(buffer):
    return pltpu.VMEM(buffer.shape, buffer.dtype)


def project(prompts, responses, blocks, weights, total, kind):
    row_count = prompts.shape[0]
    depth, width = weights[0][0].shape
    count = len(weights)
    terms = [term for weight in weights for term in weight]

    def kernel(block_ref, *refs):
        arrays, term_refs, refs = refs[:2], refs[2 : 2 + len(terms)], refs[2 + len(terms) :]
        if total is not None:
            total_ref, *refs = refs
        out_ref, feature_buf, term_buf, sum_buf, out_buf, term_sem, feature_sem, sem = refs
        loads, weight_loads = [], []
        at = 0
        if total is not None:
            total_load = pltpu.make_async_copy(total_ref, sum_buf, sem.at[0])
            total_load.start()
        for k, weight in enumerate(weights):
            start = pl.multiple_of(block_ref[k] * depth, depth)
            for array in range(2):
                load = pltpu.make_async_copy(
                    arrays[array].at[:, pl.ds(start, depth)],
                    feature_buf.at[k, array],
                    feature_sem.at[k, array],
                )
                load.start()
                loads.append(load)
            weight_loads.append([])
            for _ in weight:
                load = pltpu.make_async_copy(term_refs[at], term_buf.at[at], term_sem.at[at])
                load.start()
                weight_loads[-1].append((load, at))
                at += 1
        if total is not None:
            total_load.wait()
        for k in range(count):
            block = None
            for load, at in weight_loads[k]:
                load.wait()
                block = term_buf[at] if block is None else block + term_buf[at]
            for array in range(2):
                loads[2 * k + array].wait()
                rows = slice(array * row_count, (array + 1) * row_count)
                part = matmul(feature_buf[k, array], block)
                if k == 0 and total is None:
                    sum_buf[rows] = part
                else:
                    sum_buf[rows] += part
        out_buf[...] = sum_buf[...].astype(out_buf.dtype)
        store = pltpu.make_async_copy(out_buf, out_ref, sem.at[1])
        store.start()
        store.wait()

    anywhere = pl.BlockSpec(memory_space=pl.ANY)
    operands = [prompts, responses, *terms] + ([total] if total is not None else [])
    return pl.pallas_call(
        kernel,
        in_specs=[pl.BlockSpec(memory_space=pltpu.SMEM)] + [anywhere] * len(operands),
        out_specs=anywhere,
        scratch_shapes=[
            pltpu.VMEM((count, 2, row_count, depth), jnp.bfloat16),
            pltpu.VMEM((len(terms), depth, width), jnp.bfloat16),
            pltpu.VMEM((2 * row_count, width), jnp.float32),
            pltpu.VMEM((2 * row_count, width), kind),
            pltpu.SemaphoreType.DMA((len(terms),)),
            pltpu.SemaphoreType.DMA((count, 2)),
            pltpu.SemaphoreType.DMA((2,)),
        ],
        out_shape=jax.ShapeDtypeStruct((2 * row_count, width), kind),
        compiler_params=pltpu.CompilerParams(vmem_limit_bytes=16 * 1024 * 1024),
        cost_estimate=pl.CostEstimate(
            flops=4 * count * row_count * depth * width,
            bytes_accessed=4 * count * row_count * depth + 2 * len(terms) * depth * width,
            transcendentals=0,
        ),
    )(jnp.stack(blocks).astype(jnp.int32), *operands)


def compare(half, other, held, wanted, ids, row_count):
    prompt_rows, width = half.shape[0], half.shape[1] // 2
    quarter = held[0][0].shape[0]
    count, full = len(held) * quarter, 4 * width
    factor = LOGIT_SCALE / math.sqrt(E)
    operands = [wanted, ids, half, other] + [term for block in held for term in block]
    results = [
        jax.ShapeDtypeStruct((prompt_rows, 1), jnp.float32),
        jax.ShapeDtypeStruct((prompt_rows, 2 * width), jnp.float32),
        jax.ShapeDtypeStruct((prompt_rows, 2 * width), jnp.bfloat16),
        jax.ShapeDtypeStruct((count, full), jnp.float32),
        jax.ShapeDtypeStruct((quarter, full), jnp.bfloat16),
        jax.ShapeDtypeStruct((quarter, full), jnp.bfloat16),
    ]

    def kernel(*refs):
        sources, refs = refs[: len(operands)], refs[len(operands) :]
        goals, refs = refs[: len(results)], refs[len(results) :]
        buffers, refs = refs[: len(operands)], refs[len(operands) :]
        outs, (rows_buf, load_sem, store_sem) = refs[: len(results)], refs[len(results) :]
        loads = [
            pltpu.make_async_copy(source, buffer, load_sem.at[k])
            for k, (source, buffer) in enumerate(zip(sources, buffers))
        ]
        stores = [
            pltpu.make_async_copy(out, goal, store_sem.at[k])
            for k, (out, goal) in enumerate(zip(outs, goals))
        ]
        for load in loads:
            load.start()
        for load in loads:
            load.wait()
        wanted_buf, ids_buf, half_buf, other_buf, *term_bufs = buffers
        loss_buf, mine_buf, away_buf, parts_buf, second_buf, third_buf = outs
        for k, block in enumerate(held):
            mine = [term_bufs.pop(0)[...] for _ in block]
            rows_buf[k * quarter : (k + 1) * quarter] = sum(mine[1:], mine[0])
        places = [
            (half_buf, 0, mine_buf),
            (other_buf, 0, away_buf),
            (half_buf, 1, mine_buf),
            (other_buf, 1, away_buf),
        ]
        scores = jnp.zeros((prompt_rows, count), jnp.float32)
        for k, (buffer, at, _) in enumerate(places):
            scores += cross_cols(
                buffer[:, at * width : (at + 1) * width], rows_buf[:, k * width : (k + 1) * width]
            )
        scores = scores * factor + LOGIT_BIAS
        match = wanted_buf[...] == ids_buf[...]
        margin = jnp.where(match, -scores, scores)
        small = jnp.exp(-jnp.abs(margin))
        share = jnp.where(margin >= 0.0, 1.0, small) / (1.0 + small)
        share = share * (factor / row_count)
        weight = jnp.where(match, -share, share).astype(jnp.bfloat16)
        for k, (buffer, at, _) in enumerate(places):
            columns = slice(k * width, (k + 1) * width)
            part = cross_rows(weight, buffer[:, at * width : (at + 1) * width])
            parts_buf[:, columns] = part
            second_buf[:, columns] = part[2 * quarter : 3 * quarter].astype(jnp.bfloat16)
            third_buf[:, columns] = part[3 * quarter :].astype(jnp.bfloat16)
        for store in stores[3:]:
            store.start()
        for k, (_, at, out) in enumerate(places):
            part = matmul(weight, rows_buf[:, k * width : (k + 1) * width])
            out[:, at * width : (at + 1) * width] = part.astype(out.dtype)
        for store in stores[1:3]:
            store.start()
        loss_buf[...] = jnp.sum(
            jnp.maximum(margin, 0.0) + jnp.log1p(small), axis=1, keepdims=True
        )
        stores[0].start()
        for store in stores:
            store.wait()

    anywhere = pl.BlockSpec(memory_space=pl.ANY)
    return pl.pallas_call(
        kernel,
        in_specs=[anywhere] * len(operands),
        out_specs=[anywhere] * len(results),
        out_shape=results,
        scratch_shapes=[place(array) for array in operands + results]
        + [
            pltpu.VMEM((count, full), jnp.bfloat16),
            pltpu.SemaphoreType.DMA((len(operands),)),
            pltpu.SemaphoreType.DMA((len(results),)),
        ],
        compiler_params=pltpu.CompilerParams(vmem_limit_bytes=24 * 1024 * 1024),
        cost_estimate=pl.CostEstimate(
            flops=6 * prompt_rows * count * full,
            bytes_accessed=6 * prompt_rows * full + 6 * count * full,
            transcendentals=2 * prompt_rows * count,
        ),
    )(*operands)


def full_window(prompts, responses, head_projection_matrix, positive):
    row_count = prompts.shape[0]
    depth, width = head_projection_matrix.shape
    dp, mp = lax.axis_index("dp"), lax.axis_index("mp")
    z, y, c = dp // PAIR, dp % PAIR, mp % CORES
    quarter = row_count // (SIDE * CORES)

    def features(array, line, pair):
        return lax.dynamic_slice_in_dim(array, (line * PAIR + pair) * depth, depth, axis=1)

    lines = [z ^ k for k in range(LINE)]
    here = [line * PAIR + y for line in lines]
    there = [line * PAIR + 1 - y for line in lines]
    own = head_projection_matrix
    first, middle, own_y, wanted = lax.optimization_barrier(
        (
            send(own, PAIRS),
            send(own, MIDDLE),
            send(own, ACROSS_Y),
            jnp.concatenate([positive, send(positive, ACROSS_Y)], axis=0)[:, None],
        )
    )
    inner, outer, first_y = lax.optimization_barrier(
        (send(first, MIDDLE), send(middle, OUTWARD), send(first, ACROSS_Y))
    )
    last, middle_y, inner_y, outer_y = lax.optimization_barrier(
        (
            send(inner, OUTWARD),
            send(middle, Y_MIDDLE),
            send(inner, Y_MIDDLE),
            send(outer, Y_ENDS),
        )
    )
    last_y = send(last, Y_ENDS)
    emb = project(
        prompts,
        responses,
        [here[0], there[0], here[1], there[1]],
        [(own,), (own_y,), (first,), (first_y,)],
        None,
        jnp.float32,
    )
    emb = project(
        prompts,
        responses,
        [here[2], there[2], here[3]],
        [(inner, outer), (inner_y, outer_y), (middle, last)],
        emb,
        jnp.float32,
    )
    emb = project(prompts, responses, [there[3]], [(middle_y, last_y)], emb, jnp.bfloat16)
    prompt_emb, response_emb = emb[:row_count], emb[row_count:]

    pieces = []
    for k in range(SIDE * CORES):
        piece = lax.dynamic_slice_in_dim(response_emb, (mp ^ k) * quarter, quarter, axis=0)
        pieces.append(piece if k == 0 else send(piece, MIX[k]))
    response_rows = jnp.concatenate(pieces, axis=1)
    prompt_emb, response_rows = lax.optimization_barrier((prompt_emb, response_rows))
    first, second, third = line_gather(response_rows)
    held = [(response_rows,), (first,), second, third]

    near = jnp.concatenate([prompt_emb, send(prompt_emb, ACROSS_X)], axis=1)
    half = jnp.concatenate([near, send(near, ACROSS_Y)], axis=0)
    other = send(half, ACROSS_C)
    ids = ((jnp.stack(lines) * PAIR + y) * row_count + mp * quarter)[:, None] + lax.iota(
        jnp.int32, quarter
    )[None, :]

    mine = jnp.where(c == 0, prompts, responses)
    mine = jnp.concatenate([features(mine, line, 1 - y) for line in lines], axis=1)
    mine, half = lax.optimization_barrier((mine, half))
    fetched = send(mine, ACROSS_Y)
    sibling = send(fetched, ACROSS_C)

    def turned(array):
        return [array[:, k * depth : (k + 1) * depth].T for k in range(LINE)]

    arrays = [[features(array, line, y).T for line in lines] for array in (prompts, responses)]
    arrays = arrays + [turned(fetched), turned(sibling)]
    columns = [jnp.concatenate([array[k] for array in arrays], axis=1) for k in range(LINE)]
    columns = lax.optimization_barrier(columns)

    losses, mine, away, parts, second_b, third_b = compare(
        half, other, held, wanted, ids.reshape(1, -1), row_count
    )
    losses = losses[:, 0]
    losses = losses[:row_count], send(losses[row_count:], ACROSS_Y)

    mine = mine + send(away, ACROSS_C).astype(jnp.float32)
    aside = send(mine[:, width:].astype(jnp.bfloat16), ACROSS_X)

    def after(aside, loss):
        loss = losses[0] + loss
        return loss, send(loss, ACROSS_X)

    grad, (aside, _), losses = line_reduce(
        *[parts[k * quarter : (k + 1) * quarter] for k in range(LINE)],
        second_b,
        third_b,
        (aside, losses[1]),
        after,
    )
    mine = mine[:, :width] + aside.astype(jnp.float32)
    mine_y = send(mine.astype(jnp.bfloat16), ACROSS_Y).astype(jnp.float32)
    grad_prompt = (mine[:row_count] + mine_y[row_count:]).astype(jnp.bfloat16)
    grad_prompt_y = (mine[row_count:] + mine_y[:row_count]).astype(jnp.bfloat16)
    grad = grad.astype(jnp.bfloat16)
    grad_response = jnp.zeros((row_count, width), jnp.bfloat16)
    for k in range(SIDE * CORES):
        piece = grad[:, k * width : (k + 1) * width]
        piece = piece if k == 0 else send(piece, MIX[k])
        grad_response = lax.dynamic_update_slice_in_dim(
            grad_response, piece, (mp ^ k) * quarter, axis=0
        )
    grad_response_y = send(grad_response, ACROSS_Y)
    losses = losses[0] + losses[1]
    losses = losses + send(losses, ACROSS_C)

    grads = [
        grad_prompt,
        grad_response,
        jnp.where(c == 0, grad_prompt_y, grad_response_y),
        jnp.where(c == 0, grad_response_y, grad_prompt_y),
    ]
    grads = jnp.concatenate(grads, axis=0)
    third = matmul(columns[3], grads)
    third_b, grads = lax.optimization_barrier((third.astype(jnp.bfloat16), grads))
    second, first, own = [matmul(columns[k], grads) for k in (2, 1, 0)]
    head_grad, _, _ = line_reduce(own, first, second, third, second.astype(jnp.bfloat16), third_b)
    return (losses / row_count, head_grad)


def per_device(prompts, responses, head_projection_matrix, positive):
    whole = lax.axis_size("dp") == STEPS == LINE * PAIR
    whole = whole and lax.axis_size("mp") == SIDE * CORES
    step = full_window if whole else general
    return step(prompts, responses, head_projection_matrix, positive)


def solution(mesh):
    return jax.shard_map(
        per_device,
        mesh=mesh,
        in_specs=(P("dp", None), P("dp", None), P("dp", "mp"), P("dp")),
        out_specs=(P("dp"), P("dp", "mp")),
        check_vma=False,
    )
```

```python
import math

import jax
import jax.numpy as jnp
from jax import lax
from jax.experimental import pallas as pl
from jax.experimental.pallas import tpu as pltpu
from jax.sharding import PartitionSpec as P

E = 1024
STEPS = 8


LOGIT_SCALE = 3.0
LOGIT_BIAS = -3.0


def passed_along(block, axis, distance):
    devices = range(lax.axis_size(axis))
    route = [((i - distance) % len(devices), i) for i in devices]
    return lax.ppermute(block, axis, route)


def cross_rows(left_side, righthand_term):
    return lax.dot_general(
        left_side, righthand_term, (((0,), (0,)), ((), ())), preferred_element_type=jnp.float32
    )


def cross_cols(left_side, righthand_term):
    return lax.dot_general(
        left_side, righthand_term, (((1,), (1,)), ((), ())), preferred_element_type=jnp.float32
    )


def matmul(left_side, righthand_term):
    return jnp.dot(left_side, righthand_term, preferred_element_type=jnp.float32)


def general(prompts, responses, head_projection_matrix, positive):
    row_count = prompts.shape[0]
    col_count = head_projection_matrix.shape[1]
    factor = LOGIT_SCALE / math.sqrt(E)
    cycle_size = lax.axis_size("dp")
    position = lax.axis_index("dp")
    segment = lax.all_gather(head_projection_matrix, "dp", axis=0, tiled=True)
    prompt_emb = matmul(prompts, segment).astype(jnp.bfloat16)
    visiting = matmul(responses, segment).astype(jnp.bfloat16)
    local_ids = lax.iota(jnp.int32, row_count)
    prompt_gradient_total = jnp.zeros((row_count, col_count), jnp.float32)
    grad_response = jnp.zeros((row_count, col_count), jnp.float32)
    row_losses = jnp.zeros((row_count,), jnp.float32)
    for offset in range(STEPS):
        partial_logits = cross_cols(prompt_emb, visiting)
        pair_scores = lax.psum(partial_logits, "mp") * factor + LOGIT_BIAS
        anchor = (position - offset) % cycle_size
        column_ids = anchor * row_count + local_ids
        labels = jnp.where(positive[:, None] == column_ids[None, :], 1.0, -1.0).astype(jnp.float32)
        margin = -labels * pair_scores
        row_losses = row_losses + jnp.sum(jax.nn.softplus(margin), axis=1)
        pairwise_weight = (-labels * jax.nn.sigmoid(margin) * (factor / row_count)).astype(
            jnp.bfloat16
        )
        prompt_gradient_total = prompt_gradient_total + matmul(pairwise_weight, visiting)
        contribution = cross_rows(pairwise_weight, prompt_emb)
        if offset == 0:
            grad_response = contribution
        else:
            grad_response = grad_response + passed_along(contribution, "dp", -offset)
        if offset < STEPS - 1:
            visiting = passed_along(visiting, "dp", 1)
    grad_prompt_b = prompt_gradient_total.astype(jnp.bfloat16)
    grad_response_b = grad_response.astype(jnp.bfloat16)
    head_grad = lax.psum_scatter(
        cross_rows(prompts, grad_prompt_b) + cross_rows(responses, grad_response_b),
        "dp",
        scatter_dimension=0,
        tiled=True,
    )
    return (row_losses / row_count, head_grad)


LINE, PAIR, SIDE, CORES = 4, 2, 2, 2


def routes(move):
    table = []
    for z in range(LINE):
        for y in range(PAIR):
            for x in range(SIDE):
                for c in range(CORES):
                    goal = move(z, y, x, c)
                    if goal is not None:
                        gz, gy, gx, gc = goal
                        source = (z * PAIR + y) * SIDE * CORES + x * CORES + c
                        target = (gz * PAIR + gy) * SIDE * CORES + gx * CORES + gc
                        table.append((source, target))
    return table


def along_line(moves):
    return routes(lambda z, y, x, c: (moves[z], y, x, c) if z in moves else None)


def send(block, table):
    return lax.ppermute(block, ("dp", "mp"), table)


ACROSS_Y = routes(lambda z, y, x, c: (z, 1 - y, x, c))
ACROSS_X = routes(lambda z, y, x, c: (z, y, 1 - x, c))
Y_ENDS = routes(lambda z, y, x, c: (z, 1 - y, x, c) if z in (0, 3) else None)
Y_MIDDLE = routes(lambda z, y, x, c: (z, 1 - y, x, c) if z in (1, 2) else None)
ACROSS_C = routes(lambda z, y, x, c: (z, y, x, 1 - c))
PAIRS = along_line({0: 1, 1: 0, 2: 3, 3: 2})
MIDDLE = along_line({1: 2, 2: 1})
OUTWARD = along_line({1: 0, 2: 3})
INWARD = along_line({0: 1, 3: 2})
TWO_OUT = along_line({1: 3, 2: 0})
TWO_IN = along_line({3: 1, 0: 2})
FAR = along_line({0: 2, 1: 3, 2: 0, 3: 1})
FAR_Y = routes(lambda z, y, x, c: (z ^ 2, 1 - y, x, c))
PAIRS_X = routes(lambda z, y, x, c: (z ^ 1, y, 1 - x, c))
MIX = [routes(lambda z, y, x, c, k=k: (z, y, x ^ (k >> 1), c ^ (k & 1))) for k in range(4)]


def line_reduce(own, first, second, third, second_b, third_b, own_y, first_y):
    jumped, inward, across, first_y = lax.optimization_barrier(
        (
            send(third_b, TWO_IN),
            send(second_b, INWARD),
            send(second_b, MIDDLE),
            send(first_y, ACROSS_Y),
        )
    )
    jumped, inward, across, first_y = [
        block.astype(jnp.float32) for block in (jumped, inward, across, first_y)
    ]
    paired = send((first + first_y + across + jumped).astype(jnp.bfloat16), PAIRS)
    last = send((third + inward).astype(jnp.bfloat16), MIDDLE)
    own = own + send(own_y, ACROSS_Y).astype(jnp.float32)
    return own + last.astype(jnp.float32) + paired.astype(jnp.float32)


def project(prompts, responses, blocks, weights, total, kind):
    row_count = prompts.shape[0]
    depth, width = weights[0][0].shape
    count = len(weights)
    terms = [term for weight in weights for term in weight]

    def kernel(block_ref, *refs):
        arrays, term_refs, refs = refs[:2], list(refs[2 : 2 + len(terms)]), refs[2 + len(terms) :]
        if total is not None:
            total_ref, *refs = refs
        out_ref, feature_buf, sum_buf, sem = refs
        loads = []
        for k in range(count):
            start = pl.multiple_of(block_ref[k] * depth, depth)
            for array in range(2):
                load = pltpu.make_async_copy(
                    arrays[array].at[:, pl.ds(start, depth)],
                    feature_buf.at[k, array],
                    sem.at[k, array],
                )
                load.start()
                loads.append(load)
        for k, weight in enumerate(weights):
            block = term_refs.pop(0)[...]
            for _ in weight[1:]:
                block = block + term_refs.pop(0)[...]
            for array in range(2):
                loads[2 * k + array].wait()
                rows = slice(array * row_count, (array + 1) * row_count)
                part = matmul(feature_buf[k, array], block)
                if k > 0:
                    part += sum_buf[rows]
                elif total is not None:
                    part += total_ref[rows]
                if k < count - 1:
                    sum_buf[rows] = part
                else:
                    out_ref[rows] = part.astype(out_ref.dtype)

    inside = pl.BlockSpec(memory_space=pltpu.VMEM)
    operands = terms + ([total] if total is not None else [])
    return pl.pallas_call(
        kernel,
        in_specs=[pl.BlockSpec(memory_space=pltpu.SMEM)]
        + [pl.BlockSpec(memory_space=pltpu.HBM)] * 2
        + [inside] * len(operands),
        out_specs=inside,
        scratch_shapes=[
            pltpu.VMEM((count, 2, row_count, depth), jnp.bfloat16),
            pltpu.VMEM((2 * row_count, width), jnp.float32),
            pltpu.SemaphoreType.DMA((count, 2)),
        ],
        out_shape=jax.ShapeDtypeStruct((2 * row_count, width), kind),
        compiler_params=pltpu.CompilerParams(vmem_limit_bytes=12 * 1024 * 1024),
        cost_estimate=pl.CostEstimate(
            flops=4 * count * row_count * depth * width,
            bytes_accessed=4 * count * row_count * depth + 2 * len(terms) * depth * width,
            transcendentals=0,
        ),
    )(blocks, prompts, responses, *operands)


def compare(half, other, held, wanted, ids, row_count):
    prompt_rows, width = half.shape[0], half.shape[1] // 2
    quarter = held[0].shape[0]
    count, full = len(held) * quarter, 4 * width
    factor = LOGIT_SCALE / math.sqrt(E)

    def kernel(wanted_ref, ids_ref, half_ref, other_ref, *refs):
        held_refs, refs = refs[: len(held)], refs[len(held) :]
        loss_ref, mine_ref, away_ref, *part_refs, rows_ref = refs
        for k, ref in enumerate(held_refs):
            rows_ref[k * quarter : (k + 1) * quarter] = ref[...]
        places = [
            (half_ref, 0, mine_ref),
            (other_ref, 0, away_ref),
            (half_ref, 1, mine_ref),
            (other_ref, 1, away_ref),
        ]
        scores = jnp.zeros((count, prompt_rows), jnp.float32)
        for k, (ref, at, _) in enumerate(places):
            scores += cross_cols(
                rows_ref[:, k * width : (k + 1) * width], ref[:, at * width : (at + 1) * width]
            )
        scores = scores * factor + LOGIT_BIAS
        match = wanted_ref[...] == ids_ref[...]
        margin = jnp.where(match, -scores, scores)
        small = jnp.exp(-jnp.abs(margin))
        loss_ref[...] = jnp.sum(
            jnp.maximum(margin, 0.0) + jnp.log1p(small), axis=0, keepdims=True
        )
        share = jnp.where(margin >= 0.0, 1.0, small) / (1.0 + small)
        share = share * (factor / row_count)
        weight = jnp.where(match, -share, share).astype(jnp.bfloat16)
        for k, (ref, at, out) in enumerate(places):
            columns, goal = slice(k * width, (k + 1) * width), slice(at * width, (at + 1) * width)
            part = matmul(weight, ref[:, goal])
            for block, part_ref in enumerate(part_refs):
                rows = part[block * quarter : (block + 1) * quarter]
                part_ref[:, columns] = rows.astype(part_ref.dtype)
            out[:, goal] = cross_rows(weight, rows_ref[:, columns]).astype(out.dtype)

    return pl.pallas_call(
        kernel,
        in_specs=[pl.BlockSpec(memory_space=pltpu.VMEM)] * (4 + len(held)),
        out_specs=[pl.BlockSpec(memory_space=pltpu.VMEM)] * (3 + len(held)),
        out_shape=[
            jax.ShapeDtypeStruct((1, prompt_rows), jnp.float32),
            jax.ShapeDtypeStruct((prompt_rows, 2 * width), jnp.float32),
            jax.ShapeDtypeStruct((prompt_rows, 2 * width), jnp.bfloat16),
            jax.ShapeDtypeStruct((quarter, full), jnp.float32),
        ]
        + [jax.ShapeDtypeStruct((quarter, full), jnp.bfloat16)] * (len(held) - 1),
        scratch_shapes=[pltpu.VMEM((count, full), jnp.bfloat16)],
        compiler_params=pltpu.CompilerParams(vmem_limit_bytes=16 * 1024 * 1024),
        cost_estimate=pl.CostEstimate(
            flops=6 * prompt_rows * count * full,
            bytes_accessed=6 * prompt_rows * full + 6 * count * full,
            transcendentals=2 * prompt_rows * count,
        ),
    )(wanted, ids, half, other, *held)


def full_window(prompts, responses, head_projection_matrix, positive):
    row_count = prompts.shape[0]
    depth, width = head_projection_matrix.shape
    dp, mp = lax.axis_index("dp"), lax.axis_index("mp")
    z, y = dp // PAIR, dp % PAIR
    quarter = row_count // (SIDE * CORES)
    tie = lax.optimization_barrier

    here = [(z ^ k) * PAIR + y for k in range(LINE)]
    there = [(z ^ k) * PAIR + 1 - y for k in range(LINE)]
    orders = [here[0], there[0], here[1], there[1]], [here[2], there[2], here[3]], [there[3]]
    ids = jnp.stack([here[0], here[2], there[0], there[2]]) * row_count + mp * quarter
    ids = (ids[:, None] + lax.iota(jnp.int32, quarter)).reshape(-1, 1)
    own, orders, here, there, places, even, left, ids = tie(
        (
            head_projection_matrix,
            [jnp.stack(order).astype(jnp.int32) for order in orders],
            [(index * depth).astype(jnp.uint32) for index in here],
            [(index * depth).astype(jnp.uint32) for index in there],
            [((mp ^ k) * quarter).astype(jnp.uint32) for k in range(SIDE * CORES)],
            mp % CORES == 0,
            mp < CORES,
            ids,
        )
    )
    zero = jnp.uint32(0)

    def features(array, start):
        return lax.dynamic_slice(array, (zero, start), (row_count, depth))

    first, middle, own_y, positive_z = tie(
        (
            send(own, PAIRS),
            send(own, MIDDLE),
            send(own, ACROSS_Y),
            send(positive, PAIRS),
        )
    )
    wanted = jnp.concatenate([positive, positive_z], axis=0)[None, :]
    columns = [
        jnp.concatenate([features(prompts, start).T, features(responses, start).T], axis=1)
        for start in here + there[:2]
    ]
    mine = jnp.concatenate(
        [jnp.where(even, features(prompts, f), features(responses, f)) for f in there[2:]], axis=1
    )
    inner, outer, first_y, wanted, columns, mine = tie(
        (send(first, MIDDLE), send(middle, OUTWARD), send(first, ACROSS_Y), wanted, columns, mine)
    )
    emb = project(
        prompts,
        responses,
        orders[0],
        [(own,), (own_y,), (first,), (first_y,)],
        None,
        jnp.float32,
    )
    last, inner_y, outer_y, emb = tie(
        (send(inner, OUTWARD), send(inner, Y_MIDDLE), send(outer, Y_ENDS), emb)
    )
    emb = project(
        prompts,
        responses,
        orders[1],
        [(inner, outer), (inner_y, outer_y), (middle, last)],
        emb,
        jnp.float32,
    )
    middle_y, last_y, emb = tie((send(middle, Y_MIDDLE), send(last, Y_ENDS), emb))
    emb = project(prompts, responses, orders[2], [(middle_y, last_y)], emb, jnp.bfloat16)
    prompt_emb, response_emb = emb[:row_count], emb[row_count:]

    pieces = []
    for k in range(SIDE * CORES):
        piece = lax.dynamic_slice(response_emb, (places[k], zero), (quarter, width))
        pieces.append(piece if k == 0 else send(piece, MIX[k]))
    response_rows = jnp.concatenate(pieces, axis=1)

    response_rows, mine = tie((response_rows, mine))
    held = [send(response_rows, table) for table in (FAR, ACROSS_Y, FAR_Y)]
    near = jnp.concatenate([prompt_emb, send(prompt_emb, PAIRS)], axis=0)
    near_c = send(near, ACROSS_C)
    held, beside = tie((held, send(near, ACROSS_X)))
    half = jnp.concatenate([near, beside], axis=1)
    other = jnp.concatenate([near_c, send(beside, ACROSS_C)], axis=1)
    fetched = send(mine, ACROSS_Y)
    losses, mine, away, *parts = compare(
        half, other, [response_rows, *held], wanted, ids, row_count
    )

    back = [send(part, table) for part, table in zip(parts[1:], (FAR, ACROSS_Y, FAR_Y))]
    losses = losses[0]
    losses = losses + send(losses, ACROSS_C)
    mine = mine + send(away, ACROSS_C).astype(jnp.float32)
    aside = send(mine[:, width:].astype(jnp.bfloat16), ACROSS_X)
    back, aside, fetched = tie((back, aside, fetched))
    grad = parts[0] + sum(part.astype(jnp.float32) for part in back)
    grad = grad.astype(jnp.bfloat16)
    mine = mine[:, :width] + aside.astype(jnp.float32)
    far = send(mine[row_count:].astype(jnp.bfloat16), PAIRS)
    sibling = send(fetched, ACROSS_C)

    pieces = [grad[:, k * width : (k + 1) * width] for k in range(SIDE * CORES)]
    pieces = [pieces[0]] + [send(pieces[k], MIX[k]) for k in range(1, SIDE * CORES)]
    pieces, far, sibling = tie((pieces, far, sibling))
    swapped = [jnp.where(even, pieces[k], pieces[k ^ 1]) for k in range(SIDE * CORES)]
    swapped = [jnp.where(left, swapped[k], swapped[k ^ 2]) for k in range(SIDE * CORES)]
    grad_response = jnp.concatenate(swapped, axis=0)
    grad_response_y = send(grad_response, ACROSS_Y)
    grad_prompt = (mine[:row_count] + far.astype(jnp.float32)).astype(jnp.bfloat16)
    grad_prompt_y = send(grad_prompt, ACROSS_Y)
    losses_x = send(losses[:row_count], ACROSS_X)
    losses_z = send(losses[row_count:], PAIRS)
    losses_xz = send(losses[row_count:], PAIRS_X)
    columns_y = [
        jnp.concatenate(
            [array[:, k * depth : (k + 1) * depth].T for array in (fetched, sibling)], axis=1
        )
        for k in range(2)
    ]
    grad_response_y, grad_prompt_y, losses_x, losses_z, losses_xz, columns_y = tie(
        (grad_response_y, grad_prompt_y, losses_x, losses_z, losses_xz, columns_y)
    )
    losses = (losses[:row_count] + losses_x) + (losses_z + losses_xz)

    grads = jnp.concatenate([grad_prompt, grad_response], axis=0)
    grads_y = jnp.concatenate(
        [
            jnp.where(even, grad_prompt_y, grad_response_y),
            jnp.where(even, grad_response_y, grad_prompt_y),
        ],
        axis=0,
    )
    third = matmul(columns[3], grads) + matmul(columns_y[1], grads_y)
    third_b, grads = tie((third.astype(jnp.bfloat16), grads))
    second = matmul(columns[2], grads) + matmul(columns_y[0], grads_y)
    second_b, grads = tie((second.astype(jnp.bfloat16), grads))
    first_y, own_y = [matmul(columns[k], grads).astype(jnp.bfloat16) for k in (5, 4)]
    first, own = [matmul(columns[k], grads) for k in (1, 0)]
    head_grad = line_reduce(own, first, second, third, second_b, third_b, own_y, first_y)
    return (losses / row_count, head_grad)


def per_device(prompts, responses, head_projection_matrix, positive):
    whole = lax.axis_size("dp") == STEPS == LINE * PAIR
    whole = whole and lax.axis_size("mp") == SIDE * CORES
    step = full_window if whole else general
    return step(prompts, responses, head_projection_matrix, positive)


def solution(mesh):
    return jax.shard_map(
        per_device,
        mesh=mesh,
        in_specs=(P("dp", None), P("dp", None), P("dp", "mp"), P("dp")),
        out_specs=(P("dp"), P("dp", "mp")),
        check_vma=False,
    )
```

```python
import math

import jax
import jax.numpy as jnp
from jax import lax
from jax.experimental import pallas as pl
from jax.experimental.pallas import tpu as pltpu
from jax.sharding import PartitionSpec as P

E = 1024
STEPS = 8


LOGIT_SCALE = 3.0
LOGIT_BIAS = -3.0


def passed_along(block, axis, distance):
    devices = range(lax.axis_size(axis))
    route = [((i - distance) % len(devices), i) for i in devices]
    return lax.ppermute(block, axis, route)


def cross_rows(left_side, righthand_term):
    return lax.dot_general(
        left_side, righthand_term, (((0,), (0,)), ((), ())), preferred_element_type=jnp.float32
    )


def cross_cols(left_side, righthand_term):
    return lax.dot_general(
        left_side, righthand_term, (((1,), (1,)), ((), ())), preferred_element_type=jnp.float32
    )


def matmul(left_side, righthand_term):
    return jnp.dot(left_side, righthand_term, preferred_element_type=jnp.float32)


def general(prompts, responses, head_projection_matrix, positive):
    row_count = prompts.shape[0]
    col_count = head_projection_matrix.shape[1]
    factor = LOGIT_SCALE / math.sqrt(E)
    cycle_size = lax.axis_size("dp")
    position = lax.axis_index("dp")
    segment = lax.all_gather(head_projection_matrix, "dp", axis=0, tiled=True)
    prompt_emb = matmul(prompts, segment).astype(jnp.bfloat16)
    visiting = matmul(responses, segment).astype(jnp.bfloat16)
    local_ids = lax.iota(jnp.int32, row_count)
    prompt_gradient_total = jnp.zeros((row_count, col_count), jnp.float32)
    grad_response = jnp.zeros((row_count, col_count), jnp.float32)
    row_losses = jnp.zeros((row_count,), jnp.float32)
    for offset in range(STEPS):
        partial_logits = cross_cols(prompt_emb, visiting)
        pair_scores = lax.psum(partial_logits, "mp") * factor + LOGIT_BIAS
        anchor = (position - offset) % cycle_size
        column_ids = anchor * row_count + local_ids
        labels = jnp.where(positive[:, None] == column_ids[None, :], 1.0, -1.0).astype(jnp.float32)
        margin = -labels * pair_scores
        row_losses = row_losses + jnp.sum(jax.nn.softplus(margin), axis=1)
        pairwise_weight = (-labels * jax.nn.sigmoid(margin) * (factor / row_count)).astype(
            jnp.bfloat16
        )
        prompt_gradient_total = prompt_gradient_total + matmul(pairwise_weight, visiting)
        contribution = cross_rows(pairwise_weight, prompt_emb)
        if offset == 0:
            grad_response = contribution
        else:
            grad_response = grad_response + passed_along(contribution, "dp", -offset)
        if offset < STEPS - 1:
            visiting = passed_along(visiting, "dp", 1)
    grad_prompt_b = prompt_gradient_total.astype(jnp.bfloat16)
    grad_response_b = grad_response.astype(jnp.bfloat16)
    head_grad = lax.psum_scatter(
        cross_rows(prompts, grad_prompt_b) + cross_rows(responses, grad_response_b),
        "dp",
        scatter_dimension=0,
        tiled=True,
    )
    return (row_losses / row_count, head_grad)


LINE, PAIR, SIDE, CORES = 4, 2, 2, 2


def routes(move):
    table = []
    for z in range(LINE):
        for y in range(PAIR):
            for x in range(SIDE):
                for c in range(CORES):
                    goal = move(z, y, x, c)
                    if goal is not None:
                        gz, gy, gx, gc = goal
                        source = (z * PAIR + y) * SIDE * CORES + x * CORES + c
                        target = (gz * PAIR + gy) * SIDE * CORES + gx * CORES + gc
                        table.append((source, target))
    return table


def along_line(moves):
    return routes(lambda z, y, x, c: (moves[z], y, x, c) if z in moves else None)


def send(block, table):
    return lax.ppermute(block, ("dp", "mp"), table)


ACROSS_Y = routes(lambda z, y, x, c: (z, 1 - y, x, c))
ACROSS_X = routes(lambda z, y, x, c: (z, y, 1 - x, c))
Y_ENDS = routes(lambda z, y, x, c: (z, 1 - y, x, c) if z in (0, 3) else None)
Y_MIDDLE = routes(lambda z, y, x, c: (z, 1 - y, x, c) if z in (1, 2) else None)
ACROSS_C = routes(lambda z, y, x, c: (z, y, x, 1 - c))
PAIRS = along_line({0: 1, 1: 0, 2: 3, 3: 2})
MIDDLE = along_line({1: 2, 2: 1})
OUTWARD = along_line({1: 0, 2: 3})
INWARD = along_line({0: 1, 3: 2})
TWO_OUT = along_line({1: 3, 2: 0})
TWO_IN = along_line({3: 1, 0: 2})
FAR = along_line({0: 2, 1: 3, 2: 0, 3: 1})
FAR_Y = routes(lambda z, y, x, c: (z ^ 2, 1 - y, x, c))
MIX = [routes(lambda z, y, x, c, k=k: (z, y, x ^ (k >> 1), c ^ (k & 1))) for k in range(4)]


def line_reduce(own, first, second, third, second_b, third_b, own_y, first_y):
    jumped, inward, across, first_y = lax.optimization_barrier(
        (
            send(third_b, TWO_IN),
            send(second_b, INWARD),
            send(second_b, MIDDLE),
            send(first_y, ACROSS_Y),
        )
    )
    jumped, inward, across, first_y = [
        block.astype(jnp.float32) for block in (jumped, inward, across, first_y)
    ]
    paired = send((first + first_y + across + jumped).astype(jnp.bfloat16), PAIRS)
    last = send((third + inward).astype(jnp.bfloat16), MIDDLE)
    own = own + send(own_y, ACROSS_Y).astype(jnp.float32)
    return own + last.astype(jnp.float32) + paired.astype(jnp.float32)


TAIL = 16


def tail_rows(rows):
    terms = []
    for row in rows:
        for _ in range(3):
            term = row.astype(jnp.bfloat16).astype(jnp.float32)
            terms.append(term)
            row = row - term
    terms.append(jnp.zeros((TAIL - len(terms), rows[0].shape[1]), jnp.float32))
    return jnp.concatenate(terms, axis=0).astype(jnp.bfloat16)


def tail_of(message, row):
    terms = message[-TAIL:].astype(jnp.float32)[3 * row : 3 * row + 3]
    return terms[0:1] + terms[1:2] + terms[2:3]


def in_vmem(kernel, results, *operands):
    inside = pl.BlockSpec(memory_space=pltpu.VMEM)
    size = sum(array.size * array.dtype.itemsize for array in (*operands, *results))
    return pl.pallas_call(
        kernel,
        in_specs=[inside] * len(operands),
        out_specs=[inside] * len(results),
        out_shape=results,
        compiler_params=pltpu.CompilerParams(vmem_limit_bytes=12 * 1024 * 1024),
        cost_estimate=pl.CostEstimate(flops=size, bytes_accessed=size, transcendentals=0),
    )(*operands)


def after_cores(mine, message, loss):
    rows, width = mine.shape[0], mine.shape[1] // 2
    half = rows // 2

    def kernel(mine_ref, message_ref, loss_ref, kept_ref, out_ref, total_ref):
        kept_ref[...] = mine_ref[:, :width] + message_ref[:rows, :width].astype(jnp.float32)
        sent = mine_ref[:, width:] + message_ref[:rows, width:].astype(jnp.float32)
        out_ref[:rows] = sent.astype(jnp.bfloat16)
        total = loss_ref[...] + tail_of(message_ref, 0)
        total_ref[...] = total
        out_ref[rows:] = tail_rows([total[:, :half], total[:, half:]])

    results = [
        jax.ShapeDtypeStruct((rows, width), jnp.float32),
        jax.ShapeDtypeStruct((rows + TAIL, width), jnp.bfloat16),
        jax.ShapeDtypeStruct((1, rows), jnp.float32),
    ]
    return in_vmem(kernel, results, mine, message, loss)


def after_sides(kept, message, loss):
    rows, width = kept.shape[0] // 2, kept.shape[1]

    def kernel(kept_ref, message_ref, loss_ref, own_ref, out_ref, total_ref):
        own_ref[...] = kept_ref[:rows] + message_ref[:rows].astype(jnp.float32)
        sent = kept_ref[rows:] + message_ref[rows : 2 * rows].astype(jnp.float32)
        out_ref[:rows] = sent.astype(jnp.bfloat16)
        total_ref[...] = loss_ref[:, :rows] + tail_of(message_ref, 0)
        out_ref[rows:] = tail_rows([loss_ref[:, rows:] + tail_of(message_ref, 1)])

    results = [
        jax.ShapeDtypeStruct((rows, width), jnp.float32),
        jax.ShapeDtypeStruct((rows + TAIL, width), jnp.bfloat16),
        jax.ShapeDtypeStruct((1, rows), jnp.float32),
    ]
    return in_vmem(kernel, results, kept, message, loss)


def after_line(own, message, loss):
    rows, width = own.shape

    def kernel(own_ref, message_ref, loss_ref, out_ref, total_ref):
        total = own_ref[...] + message_ref[:rows].astype(jnp.float32)
        out_ref[...] = total.astype(jnp.bfloat16)
        total_ref[...] = loss_ref[...] + tail_of(message_ref, 0)

    results = [
        jax.ShapeDtypeStruct((rows, width), jnp.bfloat16),
        jax.ShapeDtypeStruct((1, rows), jnp.float32),
    ]
    return in_vmem(kernel, results, own, message, loss)


def project(prompts, responses, blocks, weights, total, kind):
    row_count = prompts.shape[0]
    depth, width = weights[0][0].shape
    count = len(weights)
    terms = [term for weight in weights for term in weight]

    def kernel(block_ref, *refs):
        arrays, term_refs, refs = refs[:2], list(refs[2 : 2 + len(terms)]), refs[2 + len(terms) :]
        if total is not None:
            total_ref, *refs = refs
        out_ref, feature_buf, sum_buf, sem = refs
        loads = []
        for k in range(count):
            start = pl.multiple_of(block_ref[k] * depth, depth)
            for array in range(2):
                load = pltpu.make_async_copy(
                    arrays[array].at[:, pl.ds(start, depth)],
                    feature_buf.at[k, array],
                    sem.at[k, array],
                )
                load.start()
                loads.append(load)
        for k, weight in enumerate(weights):
            block = term_refs.pop(0)[...]
            for _ in weight[1:]:
                block = block + term_refs.pop(0)[...]
            for array in range(2):
                loads[2 * k + array].wait()
                rows = slice(array * row_count, (array + 1) * row_count)
                part = matmul(feature_buf[k, array], block)
                if k > 0:
                    part += sum_buf[rows]
                elif total is not None:
                    part += total_ref[rows]
                if k < count - 1:
                    sum_buf[rows] = part
                else:
                    out_ref[rows] = part.astype(out_ref.dtype)

    inside = pl.BlockSpec(memory_space=pltpu.VMEM)
    operands = terms + ([total] if total is not None else [])
    return pl.pallas_call(
        kernel,
        in_specs=[pl.BlockSpec(memory_space=pltpu.SMEM)]
        + [pl.BlockSpec(memory_space=pltpu.HBM)] * 2
        + [inside] * len(operands),
        out_specs=inside,
        scratch_shapes=[
            pltpu.VMEM((count, 2, row_count, depth), jnp.bfloat16),
            pltpu.VMEM((2 * row_count, width), jnp.float32),
            pltpu.SemaphoreType.DMA((count, 2)),
        ],
        out_shape=jax.ShapeDtypeStruct((2 * row_count, width), kind),
        compiler_params=pltpu.CompilerParams(vmem_limit_bytes=12 * 1024 * 1024),
        cost_estimate=pl.CostEstimate(
            flops=4 * count * row_count * depth * width,
            bytes_accessed=4 * count * row_count * depth + 2 * len(terms) * depth * width,
            transcendentals=0,
        ),
    )(blocks, prompts, responses, *operands)


def compare(groups, held, wanted, ids, row_count):
    rows, width = groups[0][0].shape
    prompt_rows, across = rows * len(groups), len(groups[0])
    quarter = held[0].shape[0]
    count, full = len(held) * quarter, across * width
    factor = LOGIT_SCALE / math.sqrt(E)
    operands = [wanted, ids, *[piece for group in groups for piece in group], *held]

    def kernel(wanted_ref, ids_ref, *refs):
        group_refs = [refs[g * across : (g + 1) * across] for g in range(len(groups))]
        refs = refs[len(groups) * across :]
        held_refs, refs = refs[: len(held)], refs[len(held) :]
        loss_ref, mine_ref, away_ref, *part_refs, rows_ref = refs
        for k, ref in enumerate(held_refs):
            rows_ref[k * quarter : (k + 1) * quarter] = ref[...]
        weights, losses = [], []
        for g, pieces in enumerate(group_refs):
            scores = jnp.zeros((count, rows), jnp.float32)
            for k, ref in enumerate(pieces):
                scores += cross_cols(rows_ref[:, k * width : (k + 1) * width], ref[...])
            scores = scores * factor + LOGIT_BIAS
            match = wanted_ref[:, g * rows : (g + 1) * rows] == ids_ref[...]
            margin = jnp.where(match, -scores, scores)
            small = jnp.exp(-jnp.abs(margin))
            soft = jnp.maximum(margin, 0.0) + jnp.log1p(small)
            losses.append(jnp.sum(soft, axis=0, keepdims=True))
            share = jnp.where(margin >= 0.0, 1.0, small) / (1.0 + small)
            share = share * (factor / row_count)
            weights.append(jnp.where(match, -share, share).astype(jnp.bfloat16))
        for k in range(across):
            columns = slice(k * width, (k + 1) * width)
            part = sum(matmul(weight, pieces[k][...]) for weight, pieces in zip(weights, group_refs))
            for block, part_ref in enumerate(part_refs):
                part_rows = part[block * quarter : (block + 1) * quarter]
                part_ref[:, columns] = part_rows.astype(part_ref.dtype)
        for k in range(across):
            out, goal = (mine_ref, away_ref)[k % 2], slice(k // 2 * width, (k // 2 + 1) * width)
            for g, weight in enumerate(weights):
                part = cross_rows(weight, rows_ref[:, k * width : (k + 1) * width])
                out[g * rows : (g + 1) * rows, goal] = part.astype(out.dtype)
        loss = jnp.concatenate(losses, axis=1)
        loss_ref[...] = loss
        away_ref[prompt_rows:] = tail_rows([loss])

    return pl.pallas_call(
        kernel,
        in_specs=[pl.BlockSpec(memory_space=pltpu.VMEM)] * len(operands),
        out_specs=[pl.BlockSpec(memory_space=pltpu.VMEM)] * (3 + len(held)),
        out_shape=[
            jax.ShapeDtypeStruct((1, prompt_rows), jnp.float32),
            jax.ShapeDtypeStruct((prompt_rows, full // 2), jnp.float32),
            jax.ShapeDtypeStruct((prompt_rows + TAIL, full // 2), jnp.bfloat16),
            jax.ShapeDtypeStruct((quarter, full), jnp.float32),
        ]
        + [jax.ShapeDtypeStruct((quarter, full), jnp.bfloat16)] * (len(held) - 1),
        scratch_shapes=[pltpu.VMEM((count, full), jnp.bfloat16)],
        compiler_params=pltpu.CompilerParams(vmem_limit_bytes=16 * 1024 * 1024),
        cost_estimate=pl.CostEstimate(
            flops=6 * prompt_rows * count * full,
            bytes_accessed=6 * prompt_rows * full + 6 * count * full,
            transcendentals=2 * prompt_rows * count,
        ),
    )(*operands)


def full_window(prompts, responses, head_projection_matrix, positive):
    row_count = prompts.shape[0]
    depth, width = head_projection_matrix.shape
    dp, mp = lax.axis_index("dp"), lax.axis_index("mp")
    z, y = dp // PAIR, dp % PAIR
    quarter = row_count // (SIDE * CORES)
    tie = lax.optimization_barrier

    here = [(z ^ k) * PAIR + y for k in range(LINE)]
    there = [(z ^ k) * PAIR + 1 - y for k in range(LINE)]
    orders = here[:1] + there[:1] + here[1:2], [there[1], here[2], there[2], here[3]], [there[3]]
    ids = jnp.stack([here[0], here[2], there[0], there[2]]) * row_count + mp * quarter
    ids = (ids[:, None] + lax.iota(jnp.int32, quarter)).reshape(-1, 1)
    own, orders, here, there, places, even, left, ids = tie(
        (
            head_projection_matrix,
            [jnp.stack(order).astype(jnp.int32) for order in orders],
            [(index * depth).astype(jnp.uint32) for index in here],
            [(index * depth).astype(jnp.uint32) for index in there],
            [((mp ^ k) * quarter).astype(jnp.uint32) for k in range(SIDE * CORES)],
            mp % CORES == 0,
            mp < CORES,
            ids,
        )
    )
    zero = jnp.uint32(0)

    def features(array, start):
        return lax.dynamic_slice(array, (zero, start), (row_count, depth))

    own_y = send(own, ACROSS_Y)
    first, middle = send(own, PAIRS), send(own, MIDDLE)
    wanted = jnp.concatenate([positive, send(positive, PAIRS)], axis=0)[None, :]
    inner, outer, first_y = send(first, MIDDLE), send(middle, OUTWARD), send(first, ACROSS_Y)
    last = send(inner, OUTWARD)
    emb = project(
        prompts, responses, orders[0], [(own,), (own_y,), (first,)], None, jnp.float32
    )
    inner_late, middle_late, emb = tie((inner, middle, emb))
    inner_y, outer_y = send(inner_late, Y_MIDDLE), send(outer, Y_ENDS)
    columns = [
        jnp.concatenate([features(prompts, start).T, features(responses, start).T], axis=1)
        for start in here + there[:2]
    ]
    mine = jnp.concatenate(
        [jnp.where(even, features(prompts, f), features(responses, f)) for f in there[2:]], axis=1
    )
    emb, columns, wanted, mine = tie((emb, columns, wanted, mine))
    emb = project(
        prompts,
        responses,
        orders[1],
        [(first_y,), (inner, outer), (inner_y, outer_y), (middle, last)],
        emb,
        jnp.float32,
    )
    middle_y, last_y, emb = tie((send(middle_late, Y_MIDDLE), send(last, Y_ENDS), emb))
    emb = project(prompts, responses, orders[2], [(middle_y, last_y)], emb, jnp.bfloat16)
    prompt_emb, response_emb = emb[:row_count], emb[row_count:]

    pieces = []
    for k in range(SIDE * CORES):
        piece = lax.dynamic_slice(response_emb, (places[k], zero), (quarter, width))
        pieces.append(piece if k == 0 else send(piece, MIX[k]))
    pieces[1], mine, prompt_emb = tie((pieces[1], mine, prompt_emb))
    fetched = send(mine, ACROSS_Y)
    prompt_pair = send(prompt_emb, PAIRS)
    response_rows = jnp.concatenate(pieces, axis=1)
    response_rows, prompt_emb = tie((response_rows, prompt_emb))

    held = [send(response_rows, table) for table in (FAR, ACROSS_Y, FAR_Y)]
    groups = [prompt_emb, prompt_pair]
    groups = [[block, send(block, ACROSS_C), send(block, ACROSS_X)] for block in groups]
    held, fetched, *beside = tie((held, fetched, *[group[2] for group in groups]))
    groups = [[*group[:2], x, send(x, ACROSS_C)] for group, x in zip(groups, beside)]
    sibling = send(fetched, ACROSS_C)
    losses, mine, away, *parts = compare(groups, [response_rows, *held], wanted, ids, row_count)

    back = [send(part, table) for part, table in zip(parts[1:], (FAR, ACROSS_Y, FAR_Y))]
    mine, aside, losses = after_cores(mine, send(away, ACROSS_C), losses)
    columns_y = [
        jnp.concatenate(
            [array[:, k * depth : (k + 1) * depth].T for array in (fetched, sibling)], axis=1
        )
        for k in range(2)
    ]
    back, aside, columns_y = tie((back, send(aside, ACROSS_X), columns_y))
    grad = parts[0] + sum(part.astype(jnp.float32) for part in back)
    grad = grad.astype(jnp.bfloat16)
    mine, far, losses = after_sides(mine, aside, losses)

    pieces = [grad[:, k * width : (k + 1) * width] for k in range(SIDE * CORES)]
    pieces = [pieces[0]] + [send(pieces[k], MIX[k]) for k in range(1, SIDE * CORES)]
    pieces, far = tie((pieces, send(far, PAIRS)))
    swapped = [jnp.where(even, pieces[k], pieces[k ^ 1]) for k in range(SIDE * CORES)]
    swapped = [jnp.where(left, swapped[k], swapped[k ^ 2]) for k in range(SIDE * CORES)]
    grad_response = jnp.concatenate(swapped, axis=0)
    grad_response_y = send(grad_response, ACROSS_Y)
    grad_prompt, losses = after_line(mine, far, losses)
    grad_prompt_y = send(grad_prompt, ACROSS_Y)
    grad_response_y, grad_prompt_y = tie((grad_response_y, grad_prompt_y))

    grads = jnp.concatenate([grad_prompt, grad_response], axis=0)
    grads_y = jnp.concatenate(
        [
            jnp.where(even, grad_prompt_y, grad_response_y),
            jnp.where(even, grad_response_y, grad_prompt_y),
        ],
        axis=0,
    )
    third = matmul(columns[3], grads) + matmul(columns_y[1], grads_y)
    third_b, grads = tie((third.astype(jnp.bfloat16), grads))
    second = matmul(columns[2], grads) + matmul(columns_y[0], grads_y)
    second_b, grads = tie((second.astype(jnp.bfloat16), grads))
    first_y, own_y = [matmul(columns[k], grads).astype(jnp.bfloat16) for k in (5, 4)]
    first, own = [matmul(columns[k], grads) for k in (1, 0)]
    head_grad = line_reduce(own, first, second, third, second_b, third_b, own_y, first_y)
    return (losses[0] / row_count, head_grad)


def per_device(prompts, responses, head_projection_matrix, positive):
    whole = lax.axis_size("dp") == STEPS == LINE * PAIR
    whole = whole and lax.axis_size("mp") == SIDE * CORES
    step = full_window if whole else general
    return step(prompts, responses, head_projection_matrix, positive)


def solution(mesh):
    return jax.shard_map(
        per_device,
        mesh=mesh,
        in_specs=(P("dp", None), P("dp", None), P("dp", "mp"), P("dp")),
        out_specs=(P("dp"), P("dp", "mp")),
        check_vma=False,
    )
```

```python
import math

import jax
import jax.numpy as jnp
from jax import lax
from jax.experimental import pallas as pl
from jax.experimental.pallas import tpu as pltpu
from jax.sharding import PartitionSpec as P

E = 1024
STEPS = 8


LOGIT_SCALE = 3.0
LOGIT_BIAS = -3.0


def passed_along(block, axis, distance):
    devices = range(lax.axis_size(axis))
    route = [((i - distance) % len(devices), i) for i in devices]
    return lax.ppermute(block, axis, route)


def cross_rows(left_side, righthand_term):
    return lax.dot_general(
        left_side, righthand_term, (((0,), (0,)), ((), ())), preferred_element_type=jnp.float32
    )


def cross_cols(left_side, righthand_term):
    return lax.dot_general(
        left_side, righthand_term, (((1,), (1,)), ((), ())), preferred_element_type=jnp.float32
    )


def matmul(left_side, righthand_term):
    return jnp.dot(left_side, righthand_term, preferred_element_type=jnp.float32)


def general(prompts, responses, head_projection_matrix, positive):
    row_count = prompts.shape[0]
    col_count = head_projection_matrix.shape[1]
    factor = LOGIT_SCALE / math.sqrt(E)
    cycle_size = lax.axis_size("dp")
    position = lax.axis_index("dp")
    segment = lax.all_gather(head_projection_matrix, "dp", axis=0, tiled=True)
    prompt_emb = matmul(prompts, segment).astype(jnp.bfloat16)
    visiting = matmul(responses, segment).astype(jnp.bfloat16)
    local_ids = lax.iota(jnp.int32, row_count)
    prompt_gradient_total = jnp.zeros((row_count, col_count), jnp.float32)
    grad_response = jnp.zeros((row_count, col_count), jnp.float32)
    row_losses = jnp.zeros((row_count,), jnp.float32)
    for offset in range(STEPS):
        partial_logits = cross_cols(prompt_emb, visiting)
        pair_scores = lax.psum(partial_logits, "mp") * factor + LOGIT_BIAS
        anchor = (position - offset) % cycle_size
        column_ids = anchor * row_count + local_ids
        labels = jnp.where(positive[:, None] == column_ids[None, :], 1.0, -1.0).astype(jnp.float32)
        margin = -labels * pair_scores
        row_losses = row_losses + jnp.sum(jax.nn.softplus(margin), axis=1)
        pairwise_weight = (-labels * jax.nn.sigmoid(margin) * (factor / row_count)).astype(
            jnp.bfloat16
        )
        prompt_gradient_total = prompt_gradient_total + matmul(pairwise_weight, visiting)
        contribution = cross_rows(pairwise_weight, prompt_emb)
        if offset == 0:
            grad_response = contribution
        else:
            grad_response = grad_response + passed_along(contribution, "dp", -offset)
        if offset < STEPS - 1:
            visiting = passed_along(visiting, "dp", 1)
    grad_prompt_b = prompt_gradient_total.astype(jnp.bfloat16)
    grad_response_b = grad_response.astype(jnp.bfloat16)
    head_grad = lax.psum_scatter(
        cross_rows(prompts, grad_prompt_b) + cross_rows(responses, grad_response_b),
        "dp",
        scatter_dimension=0,
        tiled=True,
    )
    return (row_losses / row_count, head_grad)


LINE, PAIR, SIDE, CORES = 4, 2, 2, 2


def routes(move):
    table = []
    for z in range(LINE):
        for y in range(PAIR):
            for x in range(SIDE):
                for c in range(CORES):
                    goal = move(z, y, x, c)
                    if goal is not None:
                        gz, gy, gx, gc = goal
                        source = (z * PAIR + y) * SIDE * CORES + x * CORES + c
                        target = (gz * PAIR + gy) * SIDE * CORES + gx * CORES + gc
                        table.append((source, target))
    return table


def along_line(moves):
    return routes(lambda z, y, x, c: (moves[z], y, x, c) if z in moves else None)


def send(block, table):
    return lax.ppermute(block, ("dp", "mp"), table)


ACROSS_Y = routes(lambda z, y, x, c: (z, 1 - y, x, c))
ACROSS_X = routes(lambda z, y, x, c: (z, y, 1 - x, c))
Y_ENDS = routes(lambda z, y, x, c: (z, 1 - y, x, c) if z in (0, 3) else None)
Y_MIDDLE = routes(lambda z, y, x, c: (z, 1 - y, x, c) if z in (1, 2) else None)
ACROSS_C = routes(lambda z, y, x, c: (z, y, x, 1 - c))
PAIRS = along_line({0: 1, 1: 0, 2: 3, 3: 2})
MIDDLE = along_line({1: 2, 2: 1})
OUTWARD = along_line({1: 0, 2: 3})
INWARD = along_line({0: 1, 3: 2})
TWO_OUT = along_line({1: 3, 2: 0})
TWO_IN = along_line({3: 1, 0: 2})
FAR = along_line({0: 2, 1: 3, 2: 0, 3: 1})
FAR_Y = routes(lambda z, y, x, c: (z ^ 2, 1 - y, x, c))
MIX = [routes(lambda z, y, x, c, k=k: (z, y, x ^ (k >> 1), c ^ (k & 1))) for k in range(4)]


def line_reduce(own, first, second, third, second_b, third_b, own_y, first_y):
    jumped, inward, across, first_y = lax.optimization_barrier(
        (
            send(third_b, TWO_IN),
            send(second_b, INWARD),
            send(second_b, MIDDLE),
            first_y,
        )
    )
    paired, last = second_round((first, first_y, across, jumped), (third, inward))
    return own, own_y, send(paired, PAIRS), send(last, MIDDLE)


TAIL = 16
DIGIT_BITS = 8


def cost(microseconds):
    return pl.CostEstimate(flops=int(microseconds * 1e9), bytes_accessed=0, transcendentals=0)


def tail_rows(rows):
    terms = []
    for row in rows:
        for _ in range(3):
            term = row.astype(jnp.bfloat16).astype(jnp.float32)
            terms.append(term)
            row = row - term
    terms.append(jnp.zeros((TAIL - len(terms), rows[0].shape[1]), jnp.float32))
    return jnp.concatenate(terms, axis=0).astype(jnp.bfloat16)


def tail_of(message, row):
    terms = message[-TAIL:].astype(jnp.float32)[3 * row : 3 * row + 3]
    return terms[0:1] + terms[1:2] + terms[2:3]


def in_vmem(kernel, results, *operands, time):
    inside = pl.BlockSpec(memory_space=pltpu.VMEM)
    return pl.pallas_call(
        kernel,
        in_specs=[inside] * len(operands),
        out_specs=[inside] * len(results),
        out_shape=results,
        compiler_params=pltpu.CompilerParams(vmem_limit_bytes=12 * 1024 * 1024),
        cost_estimate=cost(time),
    )(*operands)


def after_cores(mine, message, loss):
    rows, width = mine.shape[0], mine.shape[1] // 2
    half = rows // 2

    def kernel(mine_ref, message_ref, loss_ref, kept_ref, out_ref, total_ref):
        kept_ref[...] = mine_ref[:, :width] + message_ref[:rows, :width].astype(jnp.float32)
        sent = mine_ref[:, width:] + message_ref[:rows, width:].astype(jnp.float32)
        out_ref[:rows] = sent.astype(jnp.bfloat16)
        total = loss_ref[...] + tail_of(message_ref, 0)
        total_ref[...] = total
        out_ref[rows:] = tail_rows([total[:, :half], total[:, half:]])

    results = [
        jax.ShapeDtypeStruct((rows, width), jnp.float32),
        jax.ShapeDtypeStruct((rows + TAIL, width), jnp.bfloat16),
        jax.ShapeDtypeStruct((1, rows), jnp.float32),
    ]
    return in_vmem(kernel, results, mine, message, loss, time=0.5)


def after_sides(kept, message, loss):
    rows, width = kept.shape[0] // 2, kept.shape[1]

    def kernel(kept_ref, message_ref, loss_ref, own_ref, out_ref, total_ref):
        own_ref[...] = kept_ref[:rows] + message_ref[:rows].astype(jnp.float32)
        sent = kept_ref[rows:] + message_ref[rows : 2 * rows].astype(jnp.float32)
        out_ref[:rows] = sent.astype(jnp.bfloat16)
        total_ref[...] = loss_ref[:, :rows] + tail_of(message_ref, 0)
        out_ref[rows:] = tail_rows([loss_ref[:, rows:] + tail_of(message_ref, 1)])

    results = [
        jax.ShapeDtypeStruct((rows, width), jnp.float32),
        jax.ShapeDtypeStruct((rows + TAIL, width), jnp.bfloat16),
        jax.ShapeDtypeStruct((1, rows), jnp.float32),
    ]
    return in_vmem(kernel, results, kept, message, loss, time=0.5)


def after_line(own, message, loss):
    rows, width = own.shape

    def kernel(own_ref, message_ref, loss_ref, out_ref, total_ref):
        total = own_ref[...] + message_ref[:rows].astype(jnp.float32)
        out_ref[...] = total.astype(jnp.bfloat16)
        total_ref[...] = loss_ref[...] + tail_of(message_ref, 0)

    results = [
        jax.ShapeDtypeStruct((rows, width), jnp.bfloat16),
        jax.ShapeDtypeStruct((1, rows), jnp.float32),
    ]
    return in_vmem(kernel, results, own, message, loss, time=0.5)


def project(prompts, responses, blocks, weights, total, kind, time, digits=None):
    row_count = prompts.shape[0]
    depth, width = weights[0][0].shape
    count = len(weights)
    terms = [term for weight in weights for term in weight]
    operands = terms + ([total] if total is not None else [])
    operands += [digits] if digits is not None else []

    def kernel(block_ref, *refs):
        arrays, term_refs, refs = refs[:2], list(refs[2 : 2 + len(terms)]), refs[2 + len(terms) :]
        if total is not None:
            total_ref, *refs = refs
        if digits is not None:
            digit_ref, *refs = refs
        *out_refs, feature_buf, sum_buf, sem = refs

        def columns(array, k):
            start = pl.multiple_of(block_ref[k] * depth, depth)
            return arrays[array].at[:, pl.ds(start, depth)]

        loads = []
        for k in range(count):
            for array in range(2):
                load = pltpu.make_async_copy(
                    columns(array, k), feature_buf.at[k, array], sem.at[k, array]
                )
                load.start()
                loads.append(load)
        for k, weight in enumerate(weights):
            block = term_refs.pop(0)[...]
            for _ in weight[1:]:
                block = block + term_refs.pop(0)[...]
            for array in range(2):
                loads[2 * k + array].wait()
                rows = slice(array * row_count, (array + 1) * row_count)
                part = matmul(feature_buf[k, array], block)
                if k > 0:
                    part += sum_buf[rows]
                elif total is not None:
                    part += total_ref[rows]
                if k < count - 1:
                    sum_buf[rows] = part
                elif digits is not None:
                    out_refs[array][:row_count] = part.astype(kind)
                else:
                    out_refs[0][rows] = part.astype(kind)
        if digits is not None:
            wanted = digit_ref[...]
            high = wanted >> DIGIT_BITS
            low = wanted - (high << DIGIT_BITS)
            rows = [high.astype(jnp.float32), low.astype(jnp.float32)]
            rows.append(jnp.zeros((TAIL - 2, wanted.shape[1]), jnp.float32))
            out_refs[0][row_count:] = jnp.concatenate(rows, axis=0).astype(kind)

    results = [(2 * row_count, width)]
    if digits is not None:
        results = [(row_count + TAIL, width), (row_count, width)]
    results = [jax.ShapeDtypeStruct(shape, kind) for shape in results]
    inside = pl.BlockSpec(memory_space=pltpu.VMEM)
    return pl.pallas_call(
        kernel,
        in_specs=[pl.BlockSpec(memory_space=pltpu.SMEM)]
        + [pl.BlockSpec(memory_space=pltpu.HBM)] * 2
        + [inside] * len(operands),
        out_specs=[inside] * len(results),
        scratch_shapes=[
            pltpu.VMEM((count, 2, row_count, depth), jnp.bfloat16),
            pltpu.VMEM((2 * row_count, width), jnp.float32),
            pltpu.SemaphoreType.DMA((count, 2)),
        ],
        out_shape=results,
        compiler_params=pltpu.CompilerParams(vmem_limit_bytes=12 * 1024 * 1024),
        cost_estimate=cost(time),
    )(blocks, prompts, responses, *operands)


def pick(prompts, responses, order, depth):
    half = prompts.shape[0] // 2

    def kernel(order_ref, prompt_ref, response_ref, out_ref, sem):
        rows = pl.ds(pl.multiple_of(order_ref[3] * half, half), half)
        for array, ref in enumerate((prompt_ref, response_ref)):

            @pl.when(order_ref[2] == 1 - array)
            def _(ref=ref):
                copies = []
                for k in range(2):
                    start = pl.multiple_of(order_ref[k] * depth, depth)
                    copy = pltpu.make_async_copy(
                        ref.at[rows, pl.ds(start, depth)],
                        out_ref.at[:, k * depth : (k + 1) * depth],
                        sem.at[k],
                    )
                    copy.start()
                    copies.append(copy)
                for copy in copies:
                    copy.wait()

    return pl.pallas_call(
        kernel,
        in_specs=[pl.BlockSpec(memory_space=pltpu.SMEM)]
        + [pl.BlockSpec(memory_space=pltpu.HBM)] * 2,
        out_specs=pl.BlockSpec(memory_space=pltpu.VMEM),
        out_shape=jax.ShapeDtypeStruct((half, 2 * depth), prompts.dtype),
        scratch_shapes=[pltpu.SemaphoreType.DMA((2,))],
        compiler_params=pltpu.CompilerParams(vmem_limit_bytes=4 * 1024 * 1024),
        cost_estimate=cost(1),
    )(order, prompts, responses)


def slices(prompts, responses, blocks, depth):
    count = blocks.shape[0]

    def kernel(block_ref, prompt_ref, response_ref, *refs):
        outs, sem = refs[:-1], refs[-1]
        copies = []
        for k in range(count):
            start = pl.multiple_of(block_ref[k] * depth, depth)
            for array, ref in enumerate((prompt_ref, response_ref)):
                copy = pltpu.make_async_copy(
                    ref.at[:, pl.ds(start, depth)], outs[array * count + k], sem.at[array, k]
                )
                copy.start()
                copies.append(copy)
        for copy in copies:
            copy.wait()

    shape = jax.ShapeDtypeStruct((prompts.shape[0], depth), prompts.dtype)
    return pl.pallas_call(
        kernel,
        in_specs=[pl.BlockSpec(memory_space=pltpu.SMEM)]
        + [pl.BlockSpec(memory_space=pltpu.HBM)] * 2,
        out_specs=[pl.BlockSpec(memory_space=pltpu.VMEM)] * (2 * count),
        out_shape=[shape] * (2 * count),
        scratch_shapes=[pltpu.SemaphoreType.DMA((2, count))],
        compiler_params=pltpu.CompilerParams(vmem_limit_bytes=8 * 1024 * 1024),
        cost_estimate=cost(1),
    )(blocks, prompts, responses)


def own_products(features, grads):
    rows, width = grads[0].shape
    depth = features[0][0].shape[1]
    kinds = [jnp.bfloat16] * 2 + [jnp.float32] * 4

    def kernel(*refs):
        grad_refs, refs = refs[:2], refs[2:]
        for k, kind in enumerate(kinds):
            total = cross_rows(grad_refs[0][...], refs[2 * k][...])
            total += cross_rows(grad_refs[1][...], refs[2 * k + 1][...])
            refs[2 * len(kinds) + k][...] = total.astype(kind)

    results = [jax.ShapeDtypeStruct((width, depth), kind) for kind in kinds]
    arrays = [array for block in features for array in block]
    return in_vmem(kernel, results, *grads, *arrays, time=1)


def in_order(order, fetched):
    half, columns = fetched[0].shape

    def kernel(order_ref, *refs):
        place = order_ref[1] * half
        start = (1 - order_ref[0]) * 2 * half
        for part, ref in enumerate(refs[:-1]):
            first = start if part < 2 else 2 * half - start
            row = first + (place if part % 2 == 0 else half - place)
            refs[-1][pl.ds(pl.multiple_of(row, half), half)] = ref[...]

    inside = pl.BlockSpec(memory_space=pltpu.VMEM)
    return pl.pallas_call(
        kernel,
        in_specs=[pl.BlockSpec(memory_space=pltpu.SMEM)] + [inside] * 4,
        out_specs=inside,
        out_shape=jax.ShapeDtypeStruct((4 * half, columns), fetched[0].dtype),
        compiler_params=pltpu.CompilerParams(vmem_limit_bytes=8 * 1024 * 1024),
        cost_estimate=cost(0.5),
    )(order, *fetched)


def far_products(totals, features, grads):
    (width, depth), rows = totals[0].shape, grads[0].shape[0]

    def kernel(first_ref, second_ref, prompt_ref, response_ref, feature_ref, *outs):
        for k, ref in ((1, second_ref), (0, first_ref)):
            columns = slice(k * depth, (k + 1) * depth)
            total = ref[...] + cross_rows(prompt_ref[...], feature_ref[:rows, columns])
            total += cross_rows(response_ref[...], feature_ref[rows:, columns])
            outs[k][...] = total
            outs[2 + k][...] = total.astype(jnp.bfloat16)

    results = [jax.ShapeDtypeStruct((width, depth), jnp.float32)] * 2
    results += [jax.ShapeDtypeStruct((width, depth), jnp.bfloat16)] * 2
    return in_vmem(kernel, results, *totals, *grads, features, time=2)


def second_round(*sums):
    def kernel(*refs):
        refs = list(refs)
        for terms, out in zip(sums, refs[-len(sums) :]):
            total = refs.pop(0)[...].astype(jnp.float32)
            for _ in terms[1:]:
                total += refs.pop(0)[...].astype(jnp.float32)
            out[...] = total.astype(jnp.bfloat16)

    shape = jax.ShapeDtypeStruct(sums[0][0].shape, jnp.bfloat16)
    arrays = [term for terms in sums for term in terms]
    return in_vmem(kernel, [shape] * len(sums), *arrays, time=0.5)


def turned_sum(*terms):
    def kernel(*refs):
        total = refs[0][...].astype(jnp.float32)
        for ref in refs[1:-1]:
            total += ref[...].astype(jnp.float32)
        refs[-1][...] = total.T

    shape = terms[0].shape[::-1]
    return in_vmem(kernel, [jax.ShapeDtypeStruct(shape, jnp.float32)], *terms, time=1)[0]


def stacked(blocks):
    rows, width = blocks[0].shape

    def kernel(*refs):
        for k, ref in enumerate(refs[:-1]):
            refs[-1][k * rows : (k + 1) * rows] = ref[...]

    result = jax.ShapeDtypeStruct((len(blocks) * rows, width), blocks[0].dtype)
    return in_vmem(kernel, [result], *blocks, time=0.1)[0]


def summed(terms, count):
    rows, width = terms[0].shape[0], terms[0].shape[1] // count

    def kernel(*refs):
        for k, out in enumerate(refs[len(terms) :]):
            columns = slice(k * width, (k + 1) * width)
            total = refs[0][:, columns]
            for ref in refs[1 : len(terms)]:
                total += ref[:, columns].astype(jnp.float32)
            out[...] = total.astype(jnp.bfloat16)

    result = jax.ShapeDtypeStruct((rows, width), jnp.bfloat16)
    return in_vmem(kernel, [result] * count, *terms, time=5)


def compare(groups, held, wanted, starts, row_count, blocks):
    rows, width = row_count, groups[0][0].shape[1]
    prompt_rows, across = rows * len(groups), len(groups[0])
    count, full = held.shape
    quarter = count // blocks
    factor = LOGIT_SCALE / math.sqrt(E)
    operands = [wanted, *[piece for group in groups for piece in group], held]

    def kernel(start_ref, wanted_ref, *refs):
        group_refs = [refs[g * across : (g + 1) * across] for g in range(len(groups))]
        refs = refs[len(groups) * across :]
        rows_ref, loss_ref, mine_ref, away_ref, *part_refs = refs
        count_up = lax.broadcasted_iota(jnp.int32, (quarter, 1), 0)
        ids = jnp.concatenate([count_up + start_ref[k] for k in range(blocks)], axis=0)
        weights, losses = [], []
        for g, pieces in enumerate(group_refs):
            scores = jnp.zeros((count, rows), jnp.float32)
            for k, ref in enumerate(pieces):
                scores += cross_cols(rows_ref[:, k * width : (k + 1) * width], ref[:rows])
            scores = scores * factor + LOGIT_BIAS
            target = wanted_ref[...]
            if g > 0:
                tail = pieces[0][rows:].astype(jnp.float32)
                target = (tail[0:1] * 2.0**DIGIT_BITS + tail[1:2]).astype(jnp.int32)
            match = target == ids
            margin = jnp.where(match, -scores, scores)
            small = jnp.exp(-jnp.abs(margin))
            soft = jnp.maximum(margin, 0.0) + jnp.log1p(small)
            losses.append(jnp.sum(soft, axis=0, keepdims=True))
            share = jnp.where(margin >= 0.0, 1.0, small) / (1.0 + small)
            share = share * (factor / row_count)
            weights.append(jnp.where(match, -share, share).astype(jnp.bfloat16))
        for k in range(across):
            columns = slice(k * width, (k + 1) * width)
            part = sum(
                matmul(weight, pieces[k][:rows]) for weight, pieces in zip(weights, group_refs)
            )
            for block, part_ref in enumerate(part_refs):
                part_rows = part[block * quarter : (block + 1) * quarter]
                part_ref[:, columns] = part_rows.astype(part_ref.dtype)
        for k in range(across):
            out, goal = (mine_ref, away_ref)[k % 2], slice(k // 2 * width, (k // 2 + 1) * width)
            for g, weight in enumerate(weights):
                part = cross_rows(weight, rows_ref[:, k * width : (k + 1) * width])
                out[g * rows : (g + 1) * rows, goal] = part.astype(out.dtype)
        loss = jnp.concatenate(losses, axis=1)
        loss_ref[...] = loss
        away_ref[prompt_rows:] = tail_rows([loss])

    return pl.pallas_call(
        kernel,
        in_specs=[pl.BlockSpec(memory_space=pltpu.SMEM)]
        + [pl.BlockSpec(memory_space=pltpu.VMEM)] * len(operands),
        out_specs=[pl.BlockSpec(memory_space=pltpu.VMEM)] * (3 + blocks),
        out_shape=[
            jax.ShapeDtypeStruct((1, prompt_rows), jnp.float32),
            jax.ShapeDtypeStruct((prompt_rows, full // 2), jnp.float32),
            jax.ShapeDtypeStruct((prompt_rows + TAIL, full // 2), jnp.bfloat16),
            jax.ShapeDtypeStruct((quarter, full), jnp.float32),
        ]
        + [jax.ShapeDtypeStruct((quarter, full), jnp.bfloat16)] * (blocks - 1),
        compiler_params=pltpu.CompilerParams(vmem_limit_bytes=16 * 1024 * 1024),
        cost_estimate=cost(2),
    )(starts, *operands)


def full_window(prompts, responses, head_projection_matrix, positive):
    row_count = prompts.shape[0]
    depth, width = head_projection_matrix.shape
    dp, mp = lax.axis_index("dp"), lax.axis_index("mp")
    z, y = dp // PAIR, dp % PAIR
    quarter = row_count // (SIDE * CORES)
    tie = lax.optimization_barrier

    here = [(z ^ k) * PAIR + y for k in range(LINE)]
    there = [(z ^ k) * PAIR + 1 - y for k in range(LINE)]
    even = (mp % CORES == 0).astype(jnp.int32)
    orders = (
        [there[2], there[3], even, mp // CORES],
        [here[0], there[0], here[1]],
        [there[1], here[2], there[2], here[3]],
        [there[3]],
        there[:2] + here,
        [even, mp // CORES],
    )
    starts = jnp.stack([here[0], here[2], there[0], there[2]]) * row_count + mp * quarter
    own, orders, places, swap, left, starts = tie(
        (
            head_projection_matrix,
            [jnp.stack(order).astype(jnp.int32) for order in orders],
            [((mp ^ k) * quarter).astype(jnp.uint32) for k in range(SIDE * CORES)],
            even == 1,
            mp < CORES,
            starts.astype(jnp.int32),
        )
    )

    picked = pick(prompts, responses, orders[0], depth)
    own_y = send(own, ACROSS_Y)
    first, middle, picked = tie(
        (send(own, PAIRS), send(own, MIDDLE), picked)
    )
    inner, outer, first_y = send(first, MIDDLE), send(middle, OUTWARD), send(first, ACROSS_Y)
    inner, own_y = tie((inner, own_y))
    last = send(inner, OUTWARD)
    (emb,) = project(
        prompts, responses, orders[1], [(own,), (own_y,), (first,)], None, jnp.float32, 2
    )
    inner_late, middle_late, emb = tie((inner, middle, emb))
    inner_y, outer_y = send(inner_late, Y_MIDDLE), send(outer, Y_ENDS)
    (emb,) = project(
        prompts,
        responses,
        orders[2],
        [(first_y,), (inner, outer), (inner_y, outer_y), (middle, last)],
        emb,
        jnp.float32,
        2.4,
    )
    middle_y, last_y, emb = tie(
        (send(middle_late, Y_MIDDLE), send(last, Y_ENDS), emb)
    )
    prompt_emb, response_emb = project(
        prompts, responses, orders[3], [(middle_y, last_y)], emb, jnp.bfloat16, 0.7, positive[None, :]
    )

    pieces = []
    for k in range(SIDE * CORES):
        piece = lax.dynamic_slice(response_emb, (places[k], jnp.uint32(0)), (quarter, width))
        pieces.append(piece if k == 0 else send(piece, MIX[k]))
    emb_done, picked = tie((prompt_emb, picked))
    fetched = send(picked, ACROSS_Y)
    prompt_pair = send(prompt_emb, PAIRS)
    response_rows = jnp.concatenate(pieces, axis=1)

    held = [send(response_rows, FAR), send(response_rows, FAR_Y), send(response_rows, ACROSS_Y)]
    groups = [
        [block, send(block, ACROSS_C), send(block, ACROSS_X)] for block in (prompt_emb, prompt_pair)
    ]
    beside = [group[2] for group in groups]
    held = [held[0], held[2], held[1]]
    held = stacked([response_rows, *held])
    fetched_x = send(fetched, ACROSS_X)
    features = slices(prompts, responses, tie((orders[4], prompt_emb))[0], depth)
    cross = [send(x, ACROSS_C) for x in beside]
    held, features, cross_tied, fetched_x = tie((held, features, cross, fetched_x))
    cross = cross_tied
    features = list(zip(features[:6], features[6:]))
    groups = [[*group[:2], x, across] for group, x, across in zip(groups, beside, cross)]
    losses, mine, away, *parts = compare(
        groups, held, positive[None, :], starts, row_count, LINE
    )

    mine, aside, losses = after_cores(mine, send(away, ACROSS_C), losses)
    back = [send(parts[1], FAR), send(parts[3], FAR_Y), send(parts[2], ACROSS_Y)]
    pieces = summed([parts[0], *back], SIDE * CORES)
    pieces, aside = tie((pieces, send(aside, ACROSS_X)))
    sibling, sibling_x = send(fetched, ACROSS_C), send(fetched_x, ACROSS_C)
    mine, far, losses = after_sides(mine, aside, losses)

    pieces = [pieces[0]] + [send(pieces[k], MIX[k]) for k in range(1, SIDE * CORES)]
    pieces, far = tie((pieces, send(far, PAIRS)))
    swapped = [jnp.where(swap, pieces[k], pieces[k ^ 1]) for k in range(SIDE * CORES)]
    swapped = [jnp.where(left, swapped[k], swapped[k ^ 2]) for k in range(SIDE * CORES)]
    grad_response = jnp.concatenate(swapped, axis=0)
    grad_prompt, losses = after_line(mine, far, losses)
    grads_y = [send(grad_prompt, ACROSS_Y), send(grad_response, ACROSS_Y)]

    own_y, first_y, own, first, second, third = own_products(
        features, (grad_prompt, grad_response)
    )
    far_features = in_order(orders[5], (fetched, fetched_x, sibling, sibling_x))
    grads_y, own, first, second, third, far_features = tie(
        (grads_y, own, first, second, third, far_features)
    )
    own_y, first_y = send(own_y, ACROSS_Y), send(first_y, ACROSS_Y)
    second, third, second_b, third_b = far_products(
        (second, third), far_features, grads_y
    )
    terms = line_reduce(own, first, second, third, second_b, third_b, own_y, first_y)
    return (losses[0] / row_count, turned_sum(*terms))


def per_device(prompts, responses, head_projection_matrix, positive):
    whole = lax.axis_size("dp") == STEPS == LINE * PAIR
    whole = whole and lax.axis_size("mp") == SIDE * CORES
    step = full_window if whole else general
    return step(prompts, responses, head_projection_matrix, positive)


def solution(mesh):
    return jax.shard_map(
        per_device,
        mesh=mesh,
        in_specs=(P("dp", None), P("dp", None), P("dp", "mp"), P("dp")),
        out_specs=(P("dp"), P("dp", "mp")),
        check_vma=False,
    )
```

```python
import math

import jax
import jax.numpy as jnp
from jax import lax
from jax.experimental import pallas as pl
from jax.experimental.pallas import tpu as pltpu
from jax.sharding import PartitionSpec as P

E = 1024
STEPS = 8


LOGIT_SCALE = 3.0
LOGIT_BIAS = -3.0


def passed_along(block, axis, distance):
    devices = range(lax.axis_size(axis))
    route = [((i - distance) % len(devices), i) for i in devices]
    return lax.ppermute(block, axis, route)


def cross_rows(left_side, righthand_term):
    return lax.dot_general(
        left_side, righthand_term, (((0,), (0,)), ((), ())), preferred_element_type=jnp.float32
    )


def cross_cols(left_side, righthand_term):
    return lax.dot_general(
        left_side, righthand_term, (((1,), (1,)), ((), ())), preferred_element_type=jnp.float32
    )


def matmul(left_side, righthand_term):
    return jnp.dot(left_side, righthand_term, preferred_element_type=jnp.float32)


def general(prompts, responses, head_projection_matrix, positive):
    row_count = prompts.shape[0]
    col_count = head_projection_matrix.shape[1]
    factor = LOGIT_SCALE / math.sqrt(E)
    cycle_size = lax.axis_size("dp")
    position = lax.axis_index("dp")
    segment = lax.all_gather(head_projection_matrix, "dp", axis=0, tiled=True)
    prompt_emb = matmul(prompts, segment).astype(jnp.bfloat16)
    visiting = matmul(responses, segment).astype(jnp.bfloat16)
    local_ids = lax.iota(jnp.int32, row_count)
    prompt_gradient_total = jnp.zeros((row_count, col_count), jnp.float32)
    grad_response = jnp.zeros((row_count, col_count), jnp.float32)
    row_losses = jnp.zeros((row_count,), jnp.float32)
    for offset in range(STEPS):
        partial_logits = cross_cols(prompt_emb, visiting)
        pair_scores = lax.psum(partial_logits, "mp") * factor + LOGIT_BIAS
        anchor = (position - offset) % cycle_size
        column_ids = anchor * row_count + local_ids
        labels = jnp.where(positive[:, None] == column_ids[None, :], 1.0, -1.0).astype(jnp.float32)
        margin = -labels * pair_scores
        row_losses = row_losses + jnp.sum(jax.nn.softplus(margin), axis=1)
        pairwise_weight = (-labels * jax.nn.sigmoid(margin) * (factor / row_count)).astype(
            jnp.bfloat16
        )
        prompt_gradient_total = prompt_gradient_total + matmul(pairwise_weight, visiting)
        contribution = cross_rows(pairwise_weight, prompt_emb)
        if offset == 0:
            grad_response = contribution
        else:
            grad_response = grad_response + passed_along(contribution, "dp", -offset)
        if offset < STEPS - 1:
            visiting = passed_along(visiting, "dp", 1)
    grad_prompt_b = prompt_gradient_total.astype(jnp.bfloat16)
    grad_response_b = grad_response.astype(jnp.bfloat16)
    head_grad = lax.psum_scatter(
        cross_rows(prompts, grad_prompt_b) + cross_rows(responses, grad_response_b),
        "dp",
        scatter_dimension=0,
        tiled=True,
    )
    return (row_losses / row_count, head_grad)


LINE, PAIR, SIDE, CORES = 4, 2, 2, 2


def routes(move):
    table = []
    for z in range(LINE):
        for y in range(PAIR):
            for x in range(SIDE):
                for c in range(CORES):
                    goal = move(z, y, x, c)
                    if goal is not None:
                        gz, gy, gx, gc = goal
                        source = (z * PAIR + y) * SIDE * CORES + x * CORES + c
                        target = (gz * PAIR + gy) * SIDE * CORES + gx * CORES + gc
                        table.append((source, target))
    return table


def along_line(moves):
    return routes(lambda z, y, x, c: (moves[z], y, x, c) if z in moves else None)


def send(block, table):
    return lax.ppermute(block, ("dp", "mp"), table)


ACROSS_Y = routes(lambda z, y, x, c: (z, 1 - y, x, c))
ACROSS_X = routes(lambda z, y, x, c: (z, y, 1 - x, c))
Y_ENDS = routes(lambda z, y, x, c: (z, 1 - y, x, c) if z in (0, 3) else None)
Y_MIDDLE = routes(lambda z, y, x, c: (z, 1 - y, x, c) if z in (1, 2) else None)
ACROSS_C = routes(lambda z, y, x, c: (z, y, x, 1 - c))
PAIRS = along_line({0: 1, 1: 0, 2: 3, 3: 2})
MIDDLE = along_line({1: 2, 2: 1})
OUTWARD = along_line({1: 0, 2: 3})
INWARD = along_line({0: 1, 3: 2})
TWO_OUT = along_line({1: 3, 2: 0})
TWO_IN = along_line({3: 1, 0: 2})
FAR = along_line({0: 2, 1: 3, 2: 0, 3: 1})
FAR_X = routes(lambda z, y, x, c: (z ^ 2, y, 1 - x, c))
PAIRS_Y = routes(lambda z, y, x, c: (z ^ 1, 1 - y, x, c))
MIX = [routes(lambda z, y, x, c, k=k: (z, y, x ^ (k >> 1), c ^ (k & 1))) for k in range(4)]


def line_reduce(own, first, second, third, second_b, third_b, own_y, first_y):
    jumped, inward, across, first_y = lax.optimization_barrier(
        (
            send(third_b, TWO_IN),
            send(second_b, INWARD),
            send(second_b, MIDDLE),
            first_y,
        )
    )
    paired, last = second_round((first, first_y, across, jumped), (third, inward))
    return own, own_y, send(paired, PAIRS), send(last, MIDDLE)


TAIL = 16
DIGIT_BITS = 8


def cost(microseconds):
    return pl.CostEstimate(flops=int(microseconds * 1e9), bytes_accessed=0, transcendentals=0)


def tail_rows(rows):
    terms = []
    for row in rows:
        for _ in range(3):
            term = row.astype(jnp.bfloat16).astype(jnp.float32)
            terms.append(term)
            row = row - term
    terms.append(jnp.zeros((TAIL - len(terms), rows[0].shape[1]), jnp.float32))
    return jnp.concatenate(terms, axis=0).astype(jnp.bfloat16)


def tail_of(message, row):
    terms = message.astype(jnp.float32)[3 * row : 3 * row + 3]
    return terms[0:1] + terms[1:2] + terms[2:3]


def in_vmem(kernel, results, *operands, time):
    inside = pl.BlockSpec(memory_space=pltpu.VMEM)
    return pl.pallas_call(
        kernel,
        in_specs=[inside] * len(operands),
        out_specs=[inside] * len(results),
        out_shape=results,
        compiler_params=pltpu.CompilerParams(vmem_limit_bytes=12 * 1024 * 1024),
        cost_estimate=cost(time),
    )(*operands)


def after_cores(mine, message, loss, fetched):
    rows, width = mine.shape[0] // 2, mine.shape[1] // 2

    below, blocks = fetched.shape[0], fetched.shape[1] // width

    def kernel(
        mine_ref, message_ref, loss_ref, fetched_ref, kept_ref, far_ref, far_x_ref, x_ref, total_ref
    ):
        total = loss_ref[...] + tail_of(message_ref[2 * rows :], 0)
        total_ref[...] = total[:, :rows]
        tails = [tail_rows([total[:, :rows]]), tail_rows([total[:, rows:]])]
        for k, ref in enumerate((kept_ref, x_ref, far_ref, far_x_ref)):
            place = slice(k // 2 * rows, (k // 2 + 1) * rows)
            columns = slice(k % 2 * width, (k % 2 + 1) * width)
            part = mine_ref[place, columns] + message_ref[place, columns].astype(jnp.float32)
            ref[:rows] = part.astype(ref.dtype)
            if k > 0:
                ref[rows : rows + TAIL] = tails[k // 2]
        for k in range(blocks):
            place = slice(rows + TAIL + k * below, rows + TAIL + (k + 1) * below)
            x_ref[place] = fetched_ref[:, k * width : (k + 1) * width]

    results = [jax.ShapeDtypeStruct((rows, width), jnp.float32)]
    heights = [rows + TAIL] * 2 + [rows + TAIL + below * blocks]
    results += [jax.ShapeDtypeStruct((height, width), jnp.bfloat16) for height in heights]
    results += [jax.ShapeDtypeStruct((1, rows), jnp.float32)]
    return in_vmem(kernel, results, mine, message, loss, fetched, time=0.5)


def after_line(own, messages, loss):
    rows, width = own.shape

    def kernel(own_ref, far_ref, far_x_ref, x_ref, loss_ref, out_ref, total_ref):
        total = own_ref[...]
        for ref in (x_ref, far_ref, far_x_ref):
            total += ref[:rows].astype(jnp.float32)
        out_ref[...] = total.astype(jnp.bfloat16)
        far = tail_of(far_ref[rows:], 0) + tail_of(far_x_ref[rows:], 0)
        total_ref[...] = (loss_ref[...] + tail_of(x_ref[rows : rows + TAIL], 0)) + far

    results = [
        jax.ShapeDtypeStruct((rows, width), jnp.bfloat16),
        jax.ShapeDtypeStruct((1, rows), jnp.float32),
    ]
    return in_vmem(kernel, results, own, *messages, loss, time=0.5)


def project(prompts, responses, blocks, weights, total, kind, time, digits=None):
    row_count = prompts.shape[0]
    depth, width = weights[0][0].shape
    count = len(weights)
    terms = [term for weight in weights for term in weight]
    operands = terms + ([total] if total is not None else [])
    operands += [digits] if digits is not None else []

    def kernel(block_ref, *refs):
        arrays, term_refs, refs = refs[:2], list(refs[2 : 2 + len(terms)]), refs[2 + len(terms) :]
        if total is not None:
            total_ref, *refs = refs
        if digits is not None:
            digit_ref, *refs = refs
        *out_refs, feature_buf, sum_buf, sem = refs

        def columns(array, k):
            start = pl.multiple_of(block_ref[k] * depth, depth)
            return arrays[array].at[:, pl.ds(start, depth)]

        loads = []
        for k in range(count):
            for array in range(2):
                load = pltpu.make_async_copy(
                    columns(array, k), feature_buf.at[k, array], sem.at[k, array]
                )
                load.start()
                loads.append(load)
        for k, weight in enumerate(weights):
            block = term_refs.pop(0)[...]
            for _ in weight[1:]:
                block = block + term_refs.pop(0)[...]
            for array in range(2):
                loads[2 * k + array].wait()
                rows = slice(array * row_count, (array + 1) * row_count)
                part = matmul(feature_buf[k, array], block)
                if k > 0:
                    part += sum_buf[rows]
                elif total is not None:
                    part += total_ref[rows]
                if k < count - 1:
                    sum_buf[rows] = part
                elif digits is not None:
                    out_refs[array][:row_count] = part.astype(kind)
                else:
                    out_refs[0][rows] = part.astype(kind)
        if digits is not None:
            wanted = digit_ref[...]
            high = wanted >> DIGIT_BITS
            low = wanted - (high << DIGIT_BITS)
            rows = [high.astype(jnp.float32), low.astype(jnp.float32)]
            rows.append(jnp.zeros((TAIL - 2, wanted.shape[1]), jnp.float32))
            out_refs[0][row_count:] = jnp.concatenate(rows, axis=0).astype(kind)

    results = [(2 * row_count, width)]
    if digits is not None:
        results = [(row_count + TAIL, width), (row_count, width)]
    results = [jax.ShapeDtypeStruct(shape, kind) for shape in results]
    inside = pl.BlockSpec(memory_space=pltpu.VMEM)
    return pl.pallas_call(
        kernel,
        in_specs=[pl.BlockSpec(memory_space=pltpu.SMEM)]
        + [pl.BlockSpec(memory_space=pltpu.HBM)] * 2
        + [inside] * len(operands),
        out_specs=[inside] * len(results),
        scratch_shapes=[
            pltpu.VMEM((count, 2, row_count, depth), jnp.bfloat16),
            pltpu.VMEM((2 * row_count, width), jnp.float32),
            pltpu.SemaphoreType.DMA((count, 2)),
        ],
        out_shape=results,
        compiler_params=pltpu.CompilerParams(vmem_limit_bytes=12 * 1024 * 1024),
        cost_estimate=cost(time),
    )(blocks, prompts, responses, *operands)


def pick(prompts, responses, order, depth):
    half = prompts.shape[0] // 2

    def kernel(order_ref, prompt_ref, response_ref, out_ref, sem):
        rows = pl.ds(pl.multiple_of(order_ref[3] * half, half), half)
        for array, ref in enumerate((prompt_ref, response_ref)):

            @pl.when(order_ref[2] == 1 - array)
            def _(ref=ref):
                copies = []
                for k in range(2):
                    start = pl.multiple_of(order_ref[k] * depth, depth)
                    copy = pltpu.make_async_copy(
                        ref.at[rows, pl.ds(start, depth)],
                        out_ref.at[:, k * depth : (k + 1) * depth],
                        sem.at[k],
                    )
                    copy.start()
                    copies.append(copy)
                for copy in copies:
                    copy.wait()

    return pl.pallas_call(
        kernel,
        in_specs=[pl.BlockSpec(memory_space=pltpu.SMEM)]
        + [pl.BlockSpec(memory_space=pltpu.HBM)] * 2,
        out_specs=pl.BlockSpec(memory_space=pltpu.VMEM),
        out_shape=jax.ShapeDtypeStruct((half, 2 * depth), prompts.dtype),
        scratch_shapes=[pltpu.SemaphoreType.DMA((2,))],
        compiler_params=pltpu.CompilerParams(vmem_limit_bytes=4 * 1024 * 1024),
        cost_estimate=cost(1),
    )(order, prompts, responses)


def slices(prompts, responses, blocks, depth):
    count = blocks.shape[0]

    def kernel(block_ref, prompt_ref, response_ref, *refs):
        outs, sem = refs[:-1], refs[-1]
        copies = []
        for k in range(count):
            start = pl.multiple_of(block_ref[k] * depth, depth)
            for array, ref in enumerate((prompt_ref, response_ref)):
                copy = pltpu.make_async_copy(
                    ref.at[:, pl.ds(start, depth)], outs[array * count + k], sem.at[array, k]
                )
                copy.start()
                copies.append(copy)
        for copy in copies:
            copy.wait()

    shape = jax.ShapeDtypeStruct((prompts.shape[0], depth), prompts.dtype)
    return pl.pallas_call(
        kernel,
        in_specs=[pl.BlockSpec(memory_space=pltpu.SMEM)]
        + [pl.BlockSpec(memory_space=pltpu.HBM)] * 2,
        out_specs=[pl.BlockSpec(memory_space=pltpu.VMEM)] * (2 * count),
        out_shape=[shape] * (2 * count),
        scratch_shapes=[pltpu.SemaphoreType.DMA((2, count))],
        compiler_params=pltpu.CompilerParams(vmem_limit_bytes=8 * 1024 * 1024),
        cost_estimate=cost(1),
    )(blocks, prompts, responses)


def own_products(features, grads):
    rows, width = grads[0].shape
    depth = features[0][0].shape[1]
    kinds = [jnp.bfloat16] * 2 + [jnp.float32] * 4

    def kernel(*refs):
        grad_refs, refs = refs[:2], refs[2:]
        for k, kind in enumerate(kinds):
            total = cross_rows(grad_refs[0][...], refs[2 * k][...])
            total += cross_rows(grad_refs[1][...], refs[2 * k + 1][...])
            refs[2 * len(kinds) + k][...] = total.astype(kind)

    results = [jax.ShapeDtypeStruct((width, depth), kind) for kind in kinds]
    arrays = [array for block in features for array in block]
    return in_vmem(kernel, results, *grads, *arrays, time=1)


def in_order(order, fetched, messages):
    half, columns = fetched[0].shape
    height, width = messages[0].shape
    blocks = columns // width

    def kernel(order_ref, *refs):
        for k in range(2):
            for array in range(2):

                @pl.when(order_ref[0] == (array if k else 1 - array))
                def _(ref=refs[k], message=refs[2 + k], out=refs[4 + array]):
                    place = pl.multiple_of(order_ref[1] * half, half)
                    out[pl.ds(place, half)] = ref[...]
                    place = pl.multiple_of((1 - order_ref[1]) * half, half)
                    for block in range(blocks):
                        start = height - (blocks - block) * half
                        columns = slice(block * width, (block + 1) * width)
                        out[pl.ds(place, half), columns] = message[start : start + half]

    inside = pl.BlockSpec(memory_space=pltpu.VMEM)
    return pl.pallas_call(
        kernel,
        in_specs=[pl.BlockSpec(memory_space=pltpu.SMEM)] + [inside] * 4,
        out_specs=[inside] * 2,
        out_shape=[jax.ShapeDtypeStruct((2 * half, columns), fetched[0].dtype)] * 2,
        compiler_params=pltpu.CompilerParams(vmem_limit_bytes=8 * 1024 * 1024),
        cost_estimate=cost(0.5),
    )(order, *fetched, *messages)


def far_products(totals, features, grad, time, last=False):
    width, depth = totals[0].shape

    def kernel(first_ref, second_ref, grad_ref, feature_ref, *outs):
        for k, ref in ((1, second_ref), (0, first_ref)):
            columns = slice(k * depth, (k + 1) * depth)
            total = ref[...] + cross_rows(grad_ref[...], feature_ref[:, columns])
            outs[k][...] = total
            if last:
                outs[2 + k][...] = total.astype(jnp.bfloat16)

    results = [jax.ShapeDtypeStruct((width, depth), jnp.float32)] * 2
    results += [jax.ShapeDtypeStruct((width, depth), jnp.bfloat16)] * 2 * last
    return in_vmem(kernel, results, *totals, grad, features, time=time)


def second_round(*sums):
    def kernel(*refs):
        refs = list(refs)
        for terms, out in zip(sums, refs[-len(sums) :]):
            total = refs.pop(0)[...].astype(jnp.float32)
            for _ in terms[1:]:
                total += refs.pop(0)[...].astype(jnp.float32)
            out[...] = total.astype(jnp.bfloat16)

    shape = jax.ShapeDtypeStruct(sums[0][0].shape, jnp.bfloat16)
    arrays = [term for terms in sums for term in terms]
    return in_vmem(kernel, [shape] * len(sums), *arrays, time=0.5)


def turned_sum(*terms):
    def kernel(*refs):
        total = refs[0][...].astype(jnp.float32)
        for ref in refs[1:-1]:
            total += ref[...].astype(jnp.float32)
        refs[-1][...] = total.T

    shape = terms[0].shape[::-1]
    return in_vmem(kernel, [jax.ShapeDtypeStruct(shape, jnp.float32)], *terms, time=1)[0]


def stacked(blocks):
    rows, width = blocks[0].shape

    def kernel(*refs):
        for k, ref in enumerate(refs[:-1]):
            refs[-1][k * rows : (k + 1) * rows] = ref[...]

    result = jax.ShapeDtypeStruct((len(blocks) * rows, width), blocks[0].dtype)
    return in_vmem(kernel, [result], *blocks, time=0.1)[0]


def summed(terms, count):
    rows, width = terms[0].shape[0], terms[0].shape[1] // count

    def kernel(*refs):
        for k, out in enumerate(refs[len(terms) :]):
            columns = slice(k * width, (k + 1) * width)
            total = refs[0][:, columns]
            for ref in refs[1 : len(terms)]:
                total += ref[:, columns].astype(jnp.float32)
            out[...] = total.astype(jnp.bfloat16)

    result = jax.ShapeDtypeStruct((rows, width), jnp.bfloat16)
    return in_vmem(kernel, [result] * count, *terms, time=5)


def compare(groups, held, wanted, starts, row_count, blocks):
    rows, width = row_count, groups[0][0].shape[1]
    prompt_rows, across = rows * len(groups), len(groups[0])
    count, full = held.shape
    quarter = count // blocks
    factor = LOGIT_SCALE / math.sqrt(E)
    operands = [wanted, *[piece for group in groups for piece in group], held]

    def kernel(start_ref, wanted_ref, *refs):
        group_refs = [refs[g * across : (g + 1) * across] for g in range(len(groups))]
        refs = refs[len(groups) * across :]
        rows_ref, loss_ref, mine_ref, away_ref, *part_refs = refs
        count_up = lax.broadcasted_iota(jnp.int32, (quarter, 1), 0)
        ids = jnp.concatenate([count_up + start_ref[k] for k in range(blocks)], axis=0)
        weights, losses = [], []
        for g, pieces in enumerate(group_refs):
            scores = jnp.zeros((count, rows), jnp.float32)
            for k, ref in enumerate(pieces):
                scores += cross_cols(rows_ref[:, k * width : (k + 1) * width], ref[:rows])
            scores = scores * factor + LOGIT_BIAS
            target = wanted_ref[...]
            if g > 0:
                tail = pieces[0][rows:].astype(jnp.float32)
                target = (tail[0:1] * 2.0**DIGIT_BITS + tail[1:2]).astype(jnp.int32)
            match = target == ids
            margin = jnp.where(match, -scores, scores)
            small = jnp.exp(-jnp.abs(margin))
            soft = jnp.maximum(margin, 0.0) + jnp.log1p(small)
            losses.append(jnp.sum(soft, axis=0, keepdims=True))
            share = jnp.where(margin >= 0.0, 1.0, small) / (1.0 + small)
            share = share * (factor / row_count)
            weights.append(jnp.where(match, -share, share).astype(jnp.bfloat16))
        for k in range(across):
            columns = slice(k * width, (k + 1) * width)
            part = sum(
                matmul(weight, pieces[k][:rows]) for weight, pieces in zip(weights, group_refs)
            )
            for block, part_ref in enumerate(part_refs):
                part_rows = part[block * quarter : (block + 1) * quarter]
                part_ref[:, columns] = part_rows.astype(part_ref.dtype)
        for k in range(across):
            out, goal = (mine_ref, away_ref)[k % 2], slice(k // 2 * width, (k // 2 + 1) * width)
            for g, weight in enumerate(weights):
                part = cross_rows(weight, rows_ref[:, k * width : (k + 1) * width])
                out[g * rows : (g + 1) * rows, goal] = part.astype(out.dtype)
        loss = jnp.concatenate(losses, axis=1)
        loss_ref[...] = loss
        away_ref[prompt_rows:] = tail_rows([loss])

    return pl.pallas_call(
        kernel,
        in_specs=[pl.BlockSpec(memory_space=pltpu.SMEM)]
        + [pl.BlockSpec(memory_space=pltpu.VMEM)] * len(operands),
        out_specs=[pl.BlockSpec(memory_space=pltpu.VMEM)] * (3 + blocks),
        out_shape=[
            jax.ShapeDtypeStruct((1, prompt_rows), jnp.float32),
            jax.ShapeDtypeStruct((prompt_rows, full // 2), jnp.float32),
            jax.ShapeDtypeStruct((prompt_rows + TAIL, full // 2), jnp.bfloat16),
            jax.ShapeDtypeStruct((quarter, full), jnp.float32),
        ]
        + [jax.ShapeDtypeStruct((quarter, full), jnp.bfloat16)] * (blocks - 1),
        compiler_params=pltpu.CompilerParams(vmem_limit_bytes=16 * 1024 * 1024),
        cost_estimate=cost(2),
    )(starts, *operands)


def full_window(prompts, responses, head_projection_matrix, positive):
    row_count = prompts.shape[0]
    depth, width = head_projection_matrix.shape
    dp, mp = lax.axis_index("dp"), lax.axis_index("mp")
    z, y = dp // PAIR, dp % PAIR
    quarter = row_count // (SIDE * CORES)
    tie = lax.optimization_barrier

    here = [(z ^ k) * PAIR + y for k in range(LINE)]
    there = [(z ^ k) * PAIR + 1 - y for k in range(LINE)]
    even = (mp % CORES == 0).astype(jnp.int32)
    orders = (
        [there[2], there[3], even, mp // CORES],
        [here[0], there[0], here[1]],
        [there[1], here[2], there[2], here[3]],
        [there[3]],
        there[:2] + here,
        [even, mp // CORES],
    )
    starts = jnp.stack([here[0], here[1], there[1], there[0]]) * row_count + mp * quarter
    own, orders, places, swap, left, starts = tie(
        (
            head_projection_matrix,
            [jnp.stack(order).astype(jnp.int32) for order in orders],
            [((mp ^ k) * quarter).astype(jnp.uint32) for k in range(SIDE * CORES)],
            even == 1,
            mp < CORES,
            starts.astype(jnp.int32),
        )
    )

    picked = pick(prompts, responses, orders[0], depth)
    own_y = send(own, ACROSS_Y)
    first, middle, picked = tie(
        (send(own, PAIRS), send(own, MIDDLE), picked)
    )
    inner, outer, first_y = send(first, MIDDLE), send(middle, OUTWARD), send(first, ACROSS_Y)
    inner, own_y = tie((inner, own_y))
    last = send(inner, OUTWARD)
    (emb,) = project(
        prompts, responses, orders[1], [(own,), (own_y,), (first,)], None, jnp.float32, 2
    )
    inner_late, middle_late, emb = tie((inner, middle, emb))
    inner_y, outer_y = send(inner_late, Y_MIDDLE), send(outer, Y_ENDS)
    (emb,) = project(
        prompts,
        responses,
        orders[2],
        [(first_y,), (inner, outer), (inner_y, outer_y), (middle, last)],
        emb,
        jnp.float32,
        2.4,
    )
    middle_y, last_y, emb = tie(
        (send(middle_late, Y_MIDDLE), send(last, Y_ENDS), emb)
    )
    prompt_emb, response_emb = project(
        prompts, responses, orders[3], [(middle_y, last_y)], emb, jnp.bfloat16, 0.7, positive[None, :]
    )

    pieces = []
    for k in range(SIDE * CORES):
        piece = lax.dynamic_slice(response_emb, (places[k], jnp.uint32(0)), (quarter, width))
        pieces.append(piece if k == 0 else send(piece, MIX[k]))
    prompt_emb, picked = tie((prompt_emb, picked))
    fetched = send(picked, ACROSS_Y)
    prompt_far, prompt_far_x = send(prompt_emb, FAR), send(prompt_emb, FAR_X)
    beside = [send(prompt_emb, ACROSS_X), prompt_far_x]
    response_rows = jnp.concatenate(pieces, axis=1)

    rows_late, fetched = tie((response_rows, fetched))
    held = [send(response_rows, PAIRS), send(response_rows, PAIRS_Y), send(rows_late, ACROSS_Y)]
    held = stacked([response_rows, *held])
    groups = [[block, send(block, ACROSS_C)] for block in (prompt_emb, prompt_far)]
    sibling = send(fetched, ACROSS_C)
    features = slices(prompts, responses, tie((orders[4], response_rows))[0], depth)
    cross = [send(x, ACROSS_C) for x in beside]
    held, features, cross_tied, fetched = tie((held, features, cross, fetched))
    cross = cross_tied
    features = list(zip(features[:6], features[6:]))
    groups = [[*group, x, across] for group, x, across in zip(groups, beside, cross)]
    losses, mine, away, *parts = compare(
        groups, held, positive[None, :], starts, row_count, LINE
    )

    back = [send(part, table) for part, table in zip(parts[1:], (PAIRS, PAIRS_Y, ACROSS_Y))]
    mine, *messages, losses = after_cores(mine, send(away, ACROSS_C), losses, fetched)
    messages = [send(part, table) for part, table in zip(messages, (FAR, FAR_X, ACROSS_X))]
    pieces = summed([parts[0], *back], SIDE * CORES)

    pieces = [pieces[0]] + [send(pieces[k], MIX[k]) for k in range(1, SIDE * CORES)]
    pieces, messages = tie((pieces, messages))
    swapped = [jnp.where(swap, pieces[k], pieces[k ^ 1]) for k in range(SIDE * CORES)]
    swapped = [jnp.where(left, swapped[k], swapped[k ^ 2]) for k in range(SIDE * CORES)]
    grad_response = jnp.concatenate(swapped, axis=0)
    grad_prompt, losses = after_line(mine, messages, losses)
    grads_y = [send(grad_prompt, ACROSS_Y), send(grad_response, ACROSS_Y)]

    own_y, first_y, own, first, second, third = own_products(
        features, (grad_prompt, grad_response)
    )
    far_features = in_order(
        orders[5], (fetched, sibling), (messages[2], send(messages[2], ACROSS_C))
    )
    own, first, second, third, far_features = tie((own, first, second, third, far_features))
    second, third = far_products((second, third), far_features[1], grads_y[1], 4)
    own_y, first_y = send(own_y, ACROSS_Y), send(first_y, ACROSS_Y)
    second, third, second_b, third_b = far_products(
        (second, third), far_features[0], grads_y[0], 1, last=True
    )
    terms = line_reduce(own, first, second, third, second_b, third_b, own_y, first_y)
    return (losses[0] / row_count, turned_sum(*terms))


def per_device(prompts, responses, head_projection_matrix, positive):
    whole = lax.axis_size("dp") == STEPS == LINE * PAIR
    whole = whole and lax.axis_size("mp") == SIDE * CORES
    step = full_window if whole else general
    return step(prompts, responses, head_projection_matrix, positive)


def solution(mesh):
    return jax.shard_map(
        per_device,
        mesh=mesh,
        in_specs=(P("dp", None), P("dp", None), P("dp", "mp"), P("dp")),
        out_specs=(P("dp"), P("dp", "mp")),
        check_vma=False,
    )
```

```python
import math

import jax
import jax.numpy as jnp
from jax import lax
from jax.experimental import pallas as pl
from jax.experimental.pallas import tpu as pltpu
from jax.sharding import PartitionSpec as P

E = 1024
STEPS = 8


LOGIT_SCALE = 3.0
LOGIT_BIAS = -3.0


def passed_along(block, axis, distance):
    devices = range(lax.axis_size(axis))
    route = [((i - distance) % len(devices), i) for i in devices]
    return lax.ppermute(block, axis, route)


def cross_rows(left_side, righthand_term):
    return lax.dot_general(
        left_side, righthand_term, (((0,), (0,)), ((), ())), preferred_element_type=jnp.float32
    )


def cross_cols(left_side, righthand_term):
    return lax.dot_general(
        left_side, righthand_term, (((1,), (1,)), ((), ())), preferred_element_type=jnp.float32
    )


def matmul(left_side, righthand_term):
    return jnp.dot(left_side, righthand_term, preferred_element_type=jnp.float32)


def general(prompts, responses, head_projection_matrix, positive):
    row_count = prompts.shape[0]
    col_count = head_projection_matrix.shape[1]
    factor = LOGIT_SCALE / math.sqrt(E)
    cycle_size = lax.axis_size("dp")
    position = lax.axis_index("dp")
    segment = lax.all_gather(head_projection_matrix, "dp", axis=0, tiled=True)
    prompt_emb = matmul(prompts, segment).astype(jnp.bfloat16)
    visiting = matmul(responses, segment).astype(jnp.bfloat16)
    local_ids = lax.iota(jnp.int32, row_count)
    prompt_gradient_total = jnp.zeros((row_count, col_count), jnp.float32)
    grad_response = jnp.zeros((row_count, col_count), jnp.float32)
    row_losses = jnp.zeros((row_count,), jnp.float32)
    for offset in range(STEPS):
        partial_logits = cross_cols(prompt_emb, visiting)
        pair_scores = lax.psum(partial_logits, "mp") * factor + LOGIT_BIAS
        anchor = (position - offset) % cycle_size
        column_ids = anchor * row_count + local_ids
        labels = jnp.where(positive[:, None] == column_ids[None, :], 1.0, -1.0).astype(jnp.float32)
        margin = -labels * pair_scores
        row_losses = row_losses + jnp.sum(jax.nn.softplus(margin), axis=1)
        pairwise_weight = (-labels * jax.nn.sigmoid(margin) * (factor / row_count)).astype(
            jnp.bfloat16
        )
        prompt_gradient_total = prompt_gradient_total + matmul(pairwise_weight, visiting)
        contribution = cross_rows(pairwise_weight, prompt_emb)
        if offset == 0:
            grad_response = contribution
        else:
            grad_response = grad_response + passed_along(contribution, "dp", -offset)
        if offset < STEPS - 1:
            visiting = passed_along(visiting, "dp", 1)
    grad_prompt_b = prompt_gradient_total.astype(jnp.bfloat16)
    grad_response_b = grad_response.astype(jnp.bfloat16)
    head_grad = lax.psum_scatter(
        cross_rows(prompts, grad_prompt_b) + cross_rows(responses, grad_response_b),
        "dp",
        scatter_dimension=0,
        tiled=True,
    )
    return (row_losses / row_count, head_grad)


LINE, PAIR, SIDE, CORES = 4, 2, 2, 2


def routes(move):
    table = []
    for z in range(LINE):
        for y in range(PAIR):
            for x in range(SIDE):
                for c in range(CORES):
                    goal = move(z, y, x, c)
                    if goal is not None:
                        gz, gy, gx, gc = goal
                        source = (z * PAIR + y) * SIDE * CORES + x * CORES + c
                        target = (gz * PAIR + gy) * SIDE * CORES + gx * CORES + gc
                        table.append((source, target))
    return table


def along_line(moves):
    return routes(lambda z, y, x, c: (moves[z], y, x, c) if z in moves else None)


def send(block, table):
    return lax.ppermute(block, ("dp", "mp"), table)


ACROSS_Y = routes(lambda z, y, x, c: (z, 1 - y, x, c))
ACROSS_X = routes(lambda z, y, x, c: (z, y, 1 - x, c))
ACROSS_C = routes(lambda z, y, x, c: (z, y, x, 1 - c))
PAIRS = along_line({0: 1, 1: 0, 2: 3, 3: 2})
MIDDLE = along_line({1: 2, 2: 1})
INWARD = along_line({0: 1, 3: 2})
TWO_IN = along_line({3: 1, 0: 2})
OPPOSITE = along_line({0: 3, 1: 2, 2: 1, 3: 0})
FAR = along_line({0: 2, 1: 3, 2: 0, 3: 1})
FAR_X = routes(lambda z, y, x, c: (z ^ 2, y, 1 - x, c))
PAIRS_Y = routes(lambda z, y, x, c: (z ^ 1, 1 - y, x, c))
MIX = [routes(lambda z, y, x, c, k=k: (z, y, x ^ (k >> 1), c ^ (k & 1))) for k in range(4)]


def line_reduce(own, first, second, third, second_b, third_b, own_y, first_y):
    jumped, inward, across, first_y = lax.optimization_barrier(
        (
            send(third_b, TWO_IN),
            send(second_b, INWARD),
            send(second_b, MIDDLE),
            first_y,
        )
    )
    paired, last = second_round((first, first_y, across, jumped), (third, inward))
    return own, own_y, send(paired, PAIRS), send(last, MIDDLE)


TAIL = 16
DIGIT_BITS = 8
LANES = 128


def cost(microseconds):
    return pl.CostEstimate(flops=int(microseconds * 1e9), bytes_accessed=0, transcendentals=0)


def tail_rows(rows):
    terms = []
    for row in rows:
        for _ in range(3):
            term = row.astype(jnp.bfloat16).astype(jnp.float32)
            terms.append(term)
            row = row - term
    terms.append(jnp.zeros((TAIL - len(terms), rows[0].shape[1]), jnp.float32))
    return jnp.concatenate(terms, axis=0).astype(jnp.bfloat16)


def tail_of(message, row):
    terms = message.astype(jnp.float32)[3 * row : 3 * row + 3]
    return terms[0:1] + terms[1:2] + terms[2:3]


def in_vmem(kernel, results, *operands, time):
    inside = pl.BlockSpec(memory_space=pltpu.VMEM)
    return pl.pallas_call(
        kernel,
        in_specs=[inside] * len(operands),
        out_specs=[inside] * len(results),
        out_shape=results,
        compiler_params=pltpu.CompilerParams(vmem_limit_bytes=12 * 1024 * 1024),
        cost_estimate=cost(time),
    )(*operands)


def after_cores(mine, message, loss, fetched):
    rows, width = mine.shape[0] // 2, mine.shape[1] // 2

    below, blocks = fetched.shape[0], fetched.shape[1] // width

    def kernel(
        mine_ref, message_ref, loss_ref, fetched_ref, kept_ref, far_ref, far_x_ref, x_ref, total_ref
    ):
        total = loss_ref[...] + tail_of(message_ref[2 * rows :], 0)
        total_ref[...] = total[:, :rows]
        tails = [tail_rows([total[:, :rows]]), tail_rows([total[:, rows:]])]
        for k, ref in enumerate((kept_ref, x_ref, far_ref, far_x_ref)):
            place = slice(k // 2 * rows, (k // 2 + 1) * rows)
            columns = slice(k % 2 * width, (k % 2 + 1) * width)
            part = mine_ref[place, columns] + message_ref[place, columns].astype(jnp.float32)
            ref[:rows] = part.astype(ref.dtype)
            if k > 0:
                ref[rows : rows + TAIL] = tails[k // 2]
        for k in range(blocks):
            place = slice(rows + TAIL + k * below, rows + TAIL + (k + 1) * below)
            x_ref[place] = fetched_ref[:, k * width : (k + 1) * width]

    results = [jax.ShapeDtypeStruct((rows, width), jnp.float32)]
    heights = [rows + TAIL] * 2 + [rows + TAIL + below * blocks]
    results += [jax.ShapeDtypeStruct((height, width), jnp.bfloat16) for height in heights]
    results += [jax.ShapeDtypeStruct((1, rows), jnp.float32)]
    return in_vmem(kernel, results, mine, message, loss, fetched, time=0.5)


def after_line(own, messages, loss):
    rows, width = own.shape

    def kernel(own_ref, far_ref, far_x_ref, x_ref, loss_ref, out_ref, total_ref):
        total = own_ref[...]
        for ref in (x_ref, far_ref, far_x_ref):
            total += ref[:rows].astype(jnp.float32)
        out_ref[...] = total.astype(jnp.bfloat16)
        far = tail_of(far_ref[rows:], 0) + tail_of(far_x_ref[rows:], 0)
        total_ref[...] = (loss_ref[...] + tail_of(x_ref[rows : rows + TAIL], 0)) + far

    results = [
        jax.ShapeDtypeStruct((rows, width), jnp.bfloat16),
        jax.ShapeDtypeStruct((1, rows), jnp.float32),
    ]
    return in_vmem(kernel, results, own, *messages, loss, time=0.5)


def project(prompts, responses, blocks, weights, total, kind, time, digits=None):
    row_count = prompts.shape[0]
    depth, width = weights[0][0].shape
    count = len(weights)
    terms = [term for weight in weights for term in weight]
    operands = terms + ([total] if total is not None else [])
    operands += [digits] if digits is not None else []

    def kernel(block_ref, *refs):
        arrays, term_refs, refs = refs[:2], list(refs[2 : 2 + len(terms)]), refs[2 + len(terms) :]
        if total is not None:
            total_ref, *refs = refs
        if digits is not None:
            digit_ref, *refs = refs
        *out_refs, feature_buf, sum_buf, sem = refs

        def columns(array, k):
            start = pl.multiple_of(block_ref[k] * depth, depth)
            return arrays[array].at[:, pl.ds(start, depth)]

        loads = []
        for k in range(count):
            for array in range(2):
                load = pltpu.make_async_copy(
                    columns(array, k), feature_buf.at[k, array], sem.at[k, array]
                )
                load.start()
                loads.append(load)
        for k, weight in enumerate(weights):
            block = term_refs.pop(0)[...]
            for _ in weight[1:]:
                block = block + term_refs.pop(0)[...]
            for array in range(2):
                loads[2 * k + array].wait()
                rows = slice(array * row_count, (array + 1) * row_count)
                part = matmul(feature_buf[k, array], block)
                if k > 0:
                    part += sum_buf[rows]
                elif total is not None:
                    part += total_ref[rows]
                if k < count - 1:
                    sum_buf[rows] = part
                elif digits is not None:
                    out_refs[array][:row_count] = part.astype(kind)
                else:
                    out_refs[0][rows] = part.astype(kind)
        if digits is not None:
            wanted = digit_ref[...]
            high = wanted >> DIGIT_BITS
            low = wanted - (high << DIGIT_BITS)
            rows = [high.astype(jnp.float32), low.astype(jnp.float32)]
            rows.append(jnp.zeros((TAIL - 2, wanted.shape[1]), jnp.float32))
            out_refs[0][row_count:] = jnp.concatenate(rows, axis=0).astype(kind)

    results = [(2 * row_count, width)]
    if digits is not None:
        results = [(row_count + TAIL, width), (row_count, width)]
    results = [jax.ShapeDtypeStruct(shape, kind) for shape in results]
    inside = pl.BlockSpec(memory_space=pltpu.VMEM)
    return pl.pallas_call(
        kernel,
        in_specs=[pl.BlockSpec(memory_space=pltpu.SMEM)]
        + [pl.BlockSpec(memory_space=pltpu.HBM)] * 2
        + [inside] * len(operands),
        out_specs=[inside] * len(results),
        scratch_shapes=[
            pltpu.VMEM((count, 2, row_count, depth), jnp.bfloat16),
            pltpu.VMEM((2 * row_count, width), jnp.float32),
            pltpu.SemaphoreType.DMA((count, 2)),
        ],
        out_shape=results,
        compiler_params=pltpu.CompilerParams(vmem_limit_bytes=12 * 1024 * 1024),
        cost_estimate=cost(time),
    )(blocks, prompts, responses, *operands)


def pick(prompts, responses, order, depth):
    half = prompts.shape[0] // 2

    def kernel(order_ref, prompt_ref, response_ref, out_ref, sem):
        rows = pl.ds(pl.multiple_of(order_ref[3] * half, half), half)
        for array, ref in enumerate((prompt_ref, response_ref)):

            @pl.when(order_ref[2] == 1 - array)
            def _(ref=ref):
                copies = []
                for k in range(2):
                    start = pl.multiple_of(order_ref[k] * depth, depth)
                    copy = pltpu.make_async_copy(
                        ref.at[rows, pl.ds(start, depth)],
                        out_ref.at[:, k * depth : (k + 1) * depth],
                        sem.at[k],
                    )
                    copy.start()
                    copies.append(copy)
                for copy in copies:
                    copy.wait()

    return pl.pallas_call(
        kernel,
        in_specs=[pl.BlockSpec(memory_space=pltpu.SMEM)]
        + [pl.BlockSpec(memory_space=pltpu.HBM)] * 2,
        out_specs=pl.BlockSpec(memory_space=pltpu.VMEM),
        out_shape=jax.ShapeDtypeStruct((half, 2 * depth), prompts.dtype),
        scratch_shapes=[pltpu.SemaphoreType.DMA((2,))],
        compiler_params=pltpu.CompilerParams(vmem_limit_bytes=4 * 1024 * 1024),
        cost_estimate=cost(1),
    )(order, prompts, responses)


def slices(prompts, responses, blocks, depth):
    count = blocks.shape[0]

    def kernel(block_ref, prompt_ref, response_ref, *refs):
        outs, sem = refs[:-1], refs[-1]
        copies = []
        for k in range(count):
            start = pl.multiple_of(block_ref[k] * depth, depth)
            for array, ref in enumerate((prompt_ref, response_ref)):
                copy = pltpu.make_async_copy(
                    ref.at[:, pl.ds(start, depth)], outs[array * count + k], sem.at[array, k]
                )
                copy.start()
                copies.append(copy)
        for copy in copies:
            copy.wait()

    shape = jax.ShapeDtypeStruct((prompts.shape[0], depth), prompts.dtype)
    return pl.pallas_call(
        kernel,
        in_specs=[pl.BlockSpec(memory_space=pltpu.SMEM)]
        + [pl.BlockSpec(memory_space=pltpu.HBM)] * 2,
        out_specs=[pl.BlockSpec(memory_space=pltpu.VMEM)] * (2 * count),
        out_shape=[shape] * (2 * count),
        scratch_shapes=[pltpu.SemaphoreType.DMA((2, count))],
        compiler_params=pltpu.CompilerParams(vmem_limit_bytes=8 * 1024 * 1024),
        cost_estimate=cost(1),
    )(blocks, prompts, responses)


def own_products(features, grads):
    rows, width = grads[0].shape
    depth = features[0][0].shape[1]
    kinds = [jnp.bfloat16] * 2 + [jnp.float32] * 4

    def kernel(*refs):
        grad_refs, refs = refs[:2], refs[2:]
        for k, kind in enumerate(kinds):
            total = cross_rows(grad_refs[0][...], refs[2 * k][...])
            total += cross_rows(grad_refs[1][...], refs[2 * k + 1][...])
            refs[2 * len(kinds) + k][...] = total.astype(kind)

    results = [jax.ShapeDtypeStruct((width, depth), kind) for kind in kinds]
    arrays = [array for block in features for array in block]
    return in_vmem(kernel, results, *grads, *arrays, time=1)


def in_order(order, fetched, messages):
    half, columns = fetched[0].shape
    height, width = messages[0].shape
    blocks = columns // width

    def kernel(order_ref, *refs):
        for k in range(2):
            for array in range(2):

                @pl.when(order_ref[0] == (array if k else 1 - array))
                def _(ref=refs[k], message=refs[2 + k], out=refs[4 + array]):
                    place = pl.multiple_of(order_ref[1] * half, half)
                    out[pl.ds(place, half)] = ref[...]
                    place = pl.multiple_of((1 - order_ref[1]) * half, half)
                    for block in range(blocks):
                        start = height - (blocks - block) * half
                        columns = slice(block * width, (block + 1) * width)
                        out[pl.ds(place, half), columns] = message[start : start + half]

    inside = pl.BlockSpec(memory_space=pltpu.VMEM)
    return pl.pallas_call(
        kernel,
        in_specs=[pl.BlockSpec(memory_space=pltpu.SMEM)] + [inside] * 4,
        out_specs=[inside] * 2,
        out_shape=[jax.ShapeDtypeStruct((2 * half, columns), fetched[0].dtype)] * 2,
        compiler_params=pltpu.CompilerParams(vmem_limit_bytes=8 * 1024 * 1024),
        cost_estimate=cost(0.5),
    )(order, *fetched, *messages)


def far_products(totals, features, grad, time, last=False):
    width, depth = totals[0].shape

    def kernel(first_ref, second_ref, grad_ref, feature_ref, *outs):
        for k, ref in ((1, second_ref), (0, first_ref)):
            columns = slice(k * depth, (k + 1) * depth)
            total = ref[...] + cross_rows(grad_ref[...], feature_ref[:, columns])
            outs[k][...] = total
            if last:
                outs[2 + k][...] = total.astype(jnp.bfloat16)

    results = [jax.ShapeDtypeStruct((width, depth), jnp.float32)] * 2
    results += [jax.ShapeDtypeStruct((width, depth), jnp.bfloat16)] * 2 * last
    return in_vmem(kernel, results, *totals, grad, features, time=time)


def second_round(*sums):
    def kernel(*refs):
        refs = list(refs)
        for terms, out in zip(sums, refs[-len(sums) :]):
            total = refs.pop(0)[...].astype(jnp.float32)
            for _ in terms[1:]:
                total += refs.pop(0)[...].astype(jnp.float32)
            out[...] = total.astype(jnp.bfloat16)

    shape = jax.ShapeDtypeStruct(sums[0][0].shape, jnp.bfloat16)
    arrays = [term for terms in sums for term in terms]
    return in_vmem(kernel, [shape] * len(sums), *arrays, time=0.5)


def turned_sum(*terms):
    def kernel(*refs):
        total = refs[0][...].astype(jnp.float32)
        for ref in refs[1:-1]:
            total += ref[...].astype(jnp.float32)
        refs[-1][...] = total.T

    shape = terms[0].shape[::-1]
    return in_vmem(kernel, [jax.ShapeDtypeStruct(shape, jnp.float32)], *terms, time=1)[0]


def stacked(blocks):
    rows, width = blocks[0].shape

    def kernel(*refs):
        for k, ref in enumerate(refs[:-1]):
            refs[-1][k * rows : (k + 1) * rows] = ref[...]

    result = jax.ShapeDtypeStruct((len(blocks) * rows, width), blocks[0].dtype)
    return in_vmem(kernel, [result], *blocks, time=0.1)[0]


def summed(terms, count):
    rows, width = terms[0].shape[0], terms[0].shape[1] // count

    def kernel(*refs):
        for k, out in enumerate(refs[len(terms) :]):
            columns = slice(k * width, (k + 1) * width)
            total = refs[0][:, columns]
            for ref in refs[1 : len(terms)]:
                total += ref[:, columns].astype(jnp.float32)
            out[...] = total.astype(jnp.bfloat16)

    result = jax.ShapeDtypeStruct((rows, width), jnp.bfloat16)
    return in_vmem(kernel, [result] * count, *terms, time=4)


def compare(groups, held, wanted, ids, row_count, blocks):
    rows, width = row_count, groups[0][0].shape[1]
    prompt_rows, across = rows * len(groups), len(groups[0])
    count, full = held.shape
    quarter = count // blocks
    factor = LOGIT_SCALE / math.sqrt(E)
    operands = [wanted, ids, *[piece for group in groups for piece in group], held]

    def kernel(wanted_ref, id_ref, *refs):
        group_refs = [refs[g * across : (g + 1) * across] for g in range(len(groups))]
        refs = refs[len(groups) * across :]
        rows_ref, loss_ref, mine_ref, away_ref, *part_refs = refs
        ids = id_ref[...]
        ids = jnp.concatenate([ids] * (rows // ids.shape[1]), axis=1)
        weights, losses = [], []
        for g, pieces in enumerate(group_refs):
            scores = jnp.zeros((count, rows), jnp.float32)
            for k, ref in enumerate(pieces):
                scores += cross_cols(rows_ref[:, k * width : (k + 1) * width], ref[:rows])
            scores = scores * factor + LOGIT_BIAS
            target = wanted_ref[...]
            if g > 0:
                tail = pieces[0][rows:].astype(jnp.float32)
                target = (tail[0:1] * 2.0**DIGIT_BITS + tail[1:2]).astype(jnp.int32)
            match = target == ids
            margin = jnp.where(match, -scores, scores)
            small = jnp.exp(-jnp.abs(margin))
            soft = jnp.maximum(margin, 0.0) + jnp.log1p(small)
            losses.append(jnp.sum(soft, axis=0, keepdims=True))
            share = jnp.where(margin >= 0.0, 1.0, small) / (1.0 + small)
            share = share * (factor / row_count)
            weights.append(jnp.where(match, -share, share).astype(jnp.bfloat16))
        for k in range(across):
            columns = slice(k * width, (k + 1) * width)
            part = sum(
                matmul(weight, pieces[k][:rows]) for weight, pieces in zip(weights, group_refs)
            )
            for block, part_ref in enumerate(part_refs):
                part_rows = part[block * quarter : (block + 1) * quarter]
                part_ref[:, columns] = part_rows.astype(part_ref.dtype)
        for k in range(across):
            out, goal = (mine_ref, away_ref)[k % 2], slice(k // 2 * width, (k // 2 + 1) * width)
            for g, weight in enumerate(weights):
                part = cross_rows(weight, rows_ref[:, k * width : (k + 1) * width])
                out[g * rows : (g + 1) * rows, goal] = part.astype(out.dtype)
        loss = jnp.concatenate(losses, axis=1)
        loss_ref[...] = loss
        away_ref[prompt_rows:] = tail_rows([loss])

    return pl.pallas_call(
        kernel,
        in_specs=[pl.BlockSpec(memory_space=pltpu.VMEM)] * len(operands),
        out_specs=[pl.BlockSpec(memory_space=pltpu.VMEM)] * (3 + blocks),
        out_shape=[
            jax.ShapeDtypeStruct((1, prompt_rows), jnp.float32),
            jax.ShapeDtypeStruct((prompt_rows, full // 2), jnp.float32),
            jax.ShapeDtypeStruct((prompt_rows + TAIL, full // 2), jnp.bfloat16),
            jax.ShapeDtypeStruct((quarter, full), jnp.float32),
        ]
        + [jax.ShapeDtypeStruct((quarter, full), jnp.bfloat16)] * (blocks - 1),
        compiler_params=pltpu.CompilerParams(vmem_limit_bytes=16 * 1024 * 1024),
        cost_estimate=cost(2),
    )(*operands)


def full_window(prompts, responses, head_projection_matrix, positive):
    row_count = prompts.shape[0]
    depth, width = head_projection_matrix.shape
    dp, mp = lax.axis_index("dp"), lax.axis_index("mp")
    z, y = dp // PAIR, dp % PAIR
    quarter = row_count // (SIDE * CORES)
    tie = lax.optimization_barrier

    here = [(z ^ k) * PAIR + y for k in range(LINE)]
    there = [(z ^ k) * PAIR + 1 - y for k in range(LINE)]
    even = (mp % CORES == 0).astype(jnp.int32)
    orders = (
        [there[2], there[3], even, mp // CORES],
        [here[0], there[0], here[1], there[1]],
        [here[3], there[3], here[2]],
        [there[2]],
        there[:2] + here,
        [even, mp // CORES],
    )
    ids = jnp.stack([here[0], here[1], there[1], there[0]]) * row_count + mp * quarter
    ids = (ids.astype(jnp.int32)[:, None] + lax.iota(jnp.int32, quarter)).reshape(-1, 1)
    ids = jnp.broadcast_to(ids, (LINE * quarter, LANES))
    own, orders, places, swap, left, ids = tie(
        (
            head_projection_matrix,
            [jnp.stack(order).astype(jnp.int32) for order in orders],
            [((mp ^ k) * quarter).astype(jnp.uint32) for k in range(SIDE * CORES)],
            even == 1,
            mp < CORES,
            ids,
        )
    )

    picked = pick(prompts, responses, orders[0], depth)
    own_y = send(own, ACROSS_Y)
    first, picked = tie((send(own, PAIRS), picked))
    third = send(own, OPPOSITE)
    second = send(third, PAIRS)
    first_y, third_y = send(first, ACROSS_Y), send(third, ACROSS_Y)
    first, own_y = tie((first, own_y))
    (emb,) = project(
        prompts,
        responses,
        orders[1],
        [(own,), (own_y,), (first,), (first_y,)],
        None,
        jnp.float32,
        20,
    )
    second, emb = tie((second, emb))
    second_y = send(second, ACROSS_Y)
    (emb,) = project(
        prompts,
        responses,
        orders[2],
        [(third,), (third_y,), (second,)],
        emb,
        jnp.float32,
        2.4,
    )
    second_y, emb = tie((second_y, emb))
    prompt_emb, response_emb = project(
        prompts, responses, orders[3], [(second_y,)], emb, jnp.bfloat16, 0.7, positive[None, :]
    )

    pieces = []
    for k in range(SIDE * CORES):
        piece = lax.dynamic_slice(response_emb, (places[k], jnp.uint32(0)), (quarter, width))
        pieces.append(piece if k == 0 else send(piece, MIX[k]))
    prompt_emb, picked = tie((prompt_emb, picked))
    fetched = send(picked, ACROSS_Y)
    prompt_far, prompt_far_x = send(prompt_emb, FAR), send(prompt_emb, FAR_X)
    beside = [send(prompt_emb, ACROSS_X), prompt_far_x]
    response_rows = jnp.concatenate(pieces, axis=1)

    rows_late, fetched = tie((response_rows, fetched))
    held = [send(response_rows, PAIRS), send(response_rows, PAIRS_Y), send(rows_late, ACROSS_Y)]
    held = stacked([response_rows, *held])
    groups = [[block, send(block, ACROSS_C)] for block in (prompt_emb, prompt_far)]
    sibling = send(fetched, ACROSS_C)
    features = slices(prompts, responses, tie((orders[4], response_rows))[0], depth)
    held = tie(held)
    cross = [send(x, ACROSS_C) for x in beside]
    held, features, cross_tied, fetched = tie((held, features, cross, fetched))
    cross = cross_tied
    features = list(zip(features[:6], features[6:]))
    groups = [[*group, x, across] for group, x, across in zip(groups, beside, cross)]
    losses, mine, away, *parts = compare(
        groups, held, positive[None, :], ids, row_count, LINE
    )

    back = [send(part, table) for part, table in zip(parts[1:], (PAIRS, PAIRS_Y, ACROSS_Y))]
    mine, *messages, losses = after_cores(mine, send(away, ACROSS_C), losses, fetched)
    messages = [send(part, table) for part, table in zip(messages, (FAR, FAR_X, ACROSS_X))]
    pieces = summed([parts[0], *back], SIDE * CORES)

    pieces = [pieces[0]] + [send(pieces[k], MIX[k]) for k in range(1, SIDE * CORES)]
    pieces, messages = tie((pieces, messages))
    swapped = [jnp.where(swap, pieces[k], pieces[k ^ 1]) for k in range(SIDE * CORES)]
    swapped = [jnp.where(left, swapped[k], swapped[k ^ 2]) for k in range(SIDE * CORES)]
    grad_response = jnp.concatenate(swapped, axis=0)
    grad_prompt, losses = after_line(mine, messages, losses)
    grads_y = [send(grad_prompt, ACROSS_Y), send(grad_response, ACROSS_Y)]

    own_y, first_y, own, first, second, third = own_products(
        features, (grad_prompt, grad_response)
    )
    far_features = in_order(
        orders[5], (fetched, sibling), (messages[2], send(messages[2], ACROSS_C))
    )
    own, first, second, third, far_features = tie((own, first, second, third, far_features))
    second, third = far_products((second, third), far_features[1], grads_y[1], 4)
    own_y, first_y = send(own_y, ACROSS_Y), send(first_y, ACROSS_Y)
    second, third, second_b, third_b = far_products(
        (second, third), far_features[0], grads_y[0], 1, last=True
    )
    terms = line_reduce(own, first, second, third, second_b, third_b, own_y, first_y)
    return (losses[0] / row_count, turned_sum(*terms))


def per_device(prompts, responses, head_projection_matrix, positive):
    whole = lax.axis_size("dp") == STEPS == LINE * PAIR
    whole = whole and lax.axis_size("mp") == SIDE * CORES
    step = full_window if whole else general
    return step(prompts, responses, head_projection_matrix, positive)


def solution(mesh):
    return jax.shard_map(
        per_device,
        mesh=mesh,
        in_specs=(P("dp", None), P("dp", None), P("dp", "mp"), P("dp")),
        out_specs=(P("dp"), P("dp", "mp")),
        check_vma=False,
    )
```

```python
import math

import jax
import jax.numpy as jnp
from jax import lax
from jax.experimental import pallas as pl
from jax.experimental.pallas import tpu as pltpu
from jax.sharding import PartitionSpec as P

E = 1024
STEPS = 8


LOGIT_SCALE = 3.0
LOGIT_BIAS = -3.0


def passed_along(block, axis, distance):
    devices = range(lax.axis_size(axis))
    route = [((i - distance) % len(devices), i) for i in devices]
    return lax.ppermute(block, axis, route)


def cross_rows(left_side, righthand_term):
    return lax.dot_general(
        left_side, righthand_term, (((0,), (0,)), ((), ())), preferred_element_type=jnp.float32
    )


def cross_cols(left_side, righthand_term):
    return lax.dot_general(
        left_side, righthand_term, (((1,), (1,)), ((), ())), preferred_element_type=jnp.float32
    )


def matmul(left_side, righthand_term):
    return jnp.dot(left_side, righthand_term, preferred_element_type=jnp.float32)


def general(prompts, responses, head_projection_matrix, positive):
    row_count = prompts.shape[0]
    col_count = head_projection_matrix.shape[1]
    factor = LOGIT_SCALE / math.sqrt(E)
    cycle_size = lax.axis_size("dp")
    position = lax.axis_index("dp")
    segment = lax.all_gather(head_projection_matrix, "dp", axis=0, tiled=True)
    prompt_emb = matmul(prompts, segment).astype(jnp.bfloat16)
    visiting = matmul(responses, segment).astype(jnp.bfloat16)
    local_ids = lax.iota(jnp.int32, row_count)
    prompt_gradient_total = jnp.zeros((row_count, col_count), jnp.float32)
    grad_response = jnp.zeros((row_count, col_count), jnp.float32)
    row_losses = jnp.zeros((row_count,), jnp.float32)
    for offset in range(STEPS):
        partial_logits = cross_cols(prompt_emb, visiting)
        pair_scores = lax.psum(partial_logits, "mp") * factor + LOGIT_BIAS
        anchor = (position - offset) % cycle_size
        column_ids = anchor * row_count + local_ids
        labels = jnp.where(positive[:, None] == column_ids[None, :], 1.0, -1.0).astype(jnp.float32)
        margin = -labels * pair_scores
        row_losses = row_losses + jnp.sum(jax.nn.softplus(margin), axis=1)
        pairwise_weight = (-labels * jax.nn.sigmoid(margin) * (factor / row_count)).astype(
            jnp.bfloat16
        )
        prompt_gradient_total = prompt_gradient_total + matmul(pairwise_weight, visiting)
        contribution = cross_rows(pairwise_weight, prompt_emb)
        if offset == 0:
            grad_response = contribution
        else:
            grad_response = grad_response + passed_along(contribution, "dp", -offset)
        if offset < STEPS - 1:
            visiting = passed_along(visiting, "dp", 1)
    grad_prompt_b = prompt_gradient_total.astype(jnp.bfloat16)
    grad_response_b = grad_response.astype(jnp.bfloat16)
    head_grad = lax.psum_scatter(
        cross_rows(prompts, grad_prompt_b) + cross_rows(responses, grad_response_b),
        "dp",
        scatter_dimension=0,
        tiled=True,
    )
    return (row_losses / row_count, head_grad)


LINE, PAIR, SIDE, CORES = 4, 2, 2, 2


def routes(move):
    table = []
    for z in range(LINE):
        for y in range(PAIR):
            for x in range(SIDE):
                for c in range(CORES):
                    goal = move(z, y, x, c)
                    if goal is not None:
                        gz, gy, gx, gc = goal
                        source = (z * PAIR + y) * SIDE * CORES + x * CORES + c
                        target = (gz * PAIR + gy) * SIDE * CORES + gx * CORES + gc
                        table.append((source, target))
    return table


def along_line(moves):
    return routes(lambda z, y, x, c: (moves[z], y, x, c) if z in moves else None)


def send(block, table):
    return lax.ppermute(block, ("dp", "mp"), table)


ACROSS_Y = routes(lambda z, y, x, c: (z, 1 - y, x, c))
ACROSS_X = routes(lambda z, y, x, c: (z, y, 1 - x, c))
ACROSS_C = routes(lambda z, y, x, c: (z, y, x, 1 - c))
PAIRS = along_line({0: 1, 1: 0, 2: 3, 3: 2})
MIDDLE = along_line({1: 2, 2: 1})
INWARD = along_line({0: 1, 3: 2})
TWO_IN = along_line({3: 1, 0: 2})
OPPOSITE = along_line({0: 3, 1: 2, 2: 1, 3: 0})
FAR = along_line({0: 2, 1: 3, 2: 0, 3: 1})
FAR_X = routes(lambda z, y, x, c: (z ^ 2, y, 1 - x, c))
PAIRS_Y = routes(lambda z, y, x, c: (z ^ 1, 1 - y, x, c))
MIX = [routes(lambda z, y, x, c, k=k: (z, y, x ^ (k >> 1), c ^ (k & 1))) for k in range(4)]


def line_reduce(own, first, second, third, second_b, third_b, own_y, first_y):
    inward, jumped, across, first_y = lax.optimization_barrier(
        (send(second_b, INWARD), send(third_b, TWO_IN), send(second_b, MIDDLE), first_y)
    )
    paired, last = second_round((first, first_y, across, jumped), (third, inward))
    return own, own_y, send(paired, PAIRS), send(last, MIDDLE)


TAIL = 16
DIGIT_BITS = 8
LANES = 128


def cost(microseconds):
    return pl.CostEstimate(flops=int(microseconds * 1e9), bytes_accessed=0, transcendentals=0)


def tail_rows(rows):
    terms = []
    for row in rows:
        for _ in range(3):
            term = row.astype(jnp.bfloat16).astype(jnp.float32)
            terms.append(term)
            row = row - term
    terms.append(jnp.zeros((TAIL - len(terms), rows[0].shape[1]), jnp.float32))
    return jnp.concatenate(terms, axis=0).astype(jnp.bfloat16)


def tail_of(message, row):
    terms = message.astype(jnp.float32)[3 * row : 3 * row + 3]
    return terms[0:1] + terms[1:2] + terms[2:3]


def in_vmem(kernel, results, *operands, time):
    inside = pl.BlockSpec(memory_space=pltpu.VMEM)
    return pl.pallas_call(
        kernel,
        in_specs=[inside] * len(operands),
        out_specs=[inside] * len(results),
        out_shape=results,
        compiler_params=pltpu.CompilerParams(vmem_limit_bytes=12 * 1024 * 1024),
        cost_estimate=cost(time),
    )(*operands)


def after_cores(mine, message, loss, fetched):
    rows, width = mine.shape[0] // 2, mine.shape[1] // 2

    below, blocks = fetched.shape[0], fetched.shape[1] // width

    def kernel(
        mine_ref, message_ref, loss_ref, fetched_ref, kept_ref, far_ref, far_x_ref, x_ref, total_ref
    ):
        total = loss_ref[...] + tail_of(message_ref[2 * rows :], 0)
        total_ref[...] = total[:, :rows]
        tails = [tail_rows([total[:, :rows]]), tail_rows([total[:, rows:]])]
        for k, ref in enumerate((kept_ref, x_ref, far_ref, far_x_ref)):
            place = slice(k // 2 * rows, (k // 2 + 1) * rows)
            columns = slice(k % 2 * width, (k % 2 + 1) * width)
            part = mine_ref[place, columns] + message_ref[place, columns].astype(jnp.float32)
            ref[:rows] = part.astype(ref.dtype)
            if k > 0:
                ref[rows : rows + TAIL] = tails[k // 2]
        for k in range(blocks):
            place = slice(rows + TAIL + k * below, rows + TAIL + (k + 1) * below)
            x_ref[place] = fetched_ref[:, k * width : (k + 1) * width]

    results = [jax.ShapeDtypeStruct((rows, width), jnp.float32)]
    heights = [rows + TAIL] * 2 + [rows + TAIL + below * blocks]
    results += [jax.ShapeDtypeStruct((height, width), jnp.bfloat16) for height in heights]
    results += [jax.ShapeDtypeStruct((1, rows), jnp.float32)]
    return in_vmem(kernel, results, mine, message, loss, fetched, time=0.5)


def after_line(own, messages, loss):
    rows, width = own.shape

    def kernel(own_ref, far_ref, far_x_ref, x_ref, loss_ref, out_ref, total_ref):
        total = own_ref[...]
        for ref in (x_ref, far_ref, far_x_ref):
            total += ref[:rows].astype(jnp.float32)
        out_ref[...] = total.astype(jnp.bfloat16)
        far = tail_of(far_ref[rows:], 0) + tail_of(far_x_ref[rows:], 0)
        total_ref[...] = (loss_ref[...] + tail_of(x_ref[rows : rows + TAIL], 0)) + far

    results = [
        jax.ShapeDtypeStruct((rows, width), jnp.bfloat16),
        jax.ShapeDtypeStruct((1, rows), jnp.float32),
    ]
    return in_vmem(kernel, results, own, *messages, loss, time=0.5)


def project(prompts, responses, blocks, weights, total, kind, time, digits=None):
    row_count = prompts.shape[0]
    depth, width = weights[0][0].shape
    count = len(weights)
    terms = [term for weight in weights for term in weight]
    operands = terms + ([total] if total is not None else [])
    operands += [digits] if digits is not None else []

    def kernel(block_ref, *refs):
        arrays, term_refs, refs = refs[:2], list(refs[2 : 2 + len(terms)]), refs[2 + len(terms) :]
        if total is not None:
            total_ref, *refs = refs
        if digits is not None:
            digit_ref, *refs = refs
        *out_refs, feature_buf, sum_buf, sem = refs

        def columns(array, k):
            start = pl.multiple_of(block_ref[k] * depth, depth)
            return arrays[array].at[:, pl.ds(start, depth)]

        loads = []
        for k in range(count):
            for array in range(2):
                load = pltpu.make_async_copy(
                    columns(array, k), feature_buf.at[k, array], sem.at[k, array]
                )
                load.start()
                loads.append(load)
        for k, weight in enumerate(weights):
            block = term_refs.pop(0)[...]
            for _ in weight[1:]:
                block = block + term_refs.pop(0)[...]
            for array in range(2):
                loads[2 * k + array].wait()
                rows = slice(array * row_count, (array + 1) * row_count)
                part = matmul(feature_buf[k, array], block)
                if k > 0:
                    part += sum_buf[rows]
                elif total is not None:
                    part += total_ref[rows]
                if k < count - 1:
                    sum_buf[rows] = part
                elif digits is not None:
                    out_refs[array][:row_count] = part.astype(kind)
                else:
                    out_refs[0][rows] = part.astype(kind)
        if digits is not None:
            wanted = digit_ref[...]
            high = wanted >> DIGIT_BITS
            low = wanted - (high << DIGIT_BITS)
            rows = [high.astype(jnp.float32), low.astype(jnp.float32)]
            rows.append(jnp.zeros((TAIL - 2, wanted.shape[1]), jnp.float32))
            out_refs[0][row_count:] = jnp.concatenate(rows, axis=0).astype(kind)

    results = [(2 * row_count, width)]
    if digits is not None:
        results = [(row_count + TAIL, width), (row_count, width)]
    results = [jax.ShapeDtypeStruct(shape, kind) for shape in results]
    inside = pl.BlockSpec(memory_space=pltpu.VMEM)
    return pl.pallas_call(
        kernel,
        in_specs=[pl.BlockSpec(memory_space=pltpu.SMEM)]
        + [pl.BlockSpec(memory_space=pltpu.HBM)] * 2
        + [inside] * len(operands),
        out_specs=[inside] * len(results),
        scratch_shapes=[
            pltpu.VMEM((count, 2, row_count, depth), jnp.bfloat16),
            pltpu.VMEM((2 * row_count, width), jnp.float32),
            pltpu.SemaphoreType.DMA((count, 2)),
        ],
        out_shape=results,
        compiler_params=pltpu.CompilerParams(vmem_limit_bytes=12 * 1024 * 1024),
        cost_estimate=cost(time),
    )(blocks, prompts, responses, *operands)


def finish(features, weight, total, wanted):
    (rows, _), width = features[0].shape, weight.shape[1]

    def kernel(prompt_ref, response_ref, weight_ref, total_ref, wanted_ref, out_ref, other_ref):
        block = weight_ref[...]
        prompt_part = total_ref[:rows] + matmul(prompt_ref[...], block)
        out_ref[:rows] = prompt_part.astype(jnp.bfloat16)
        response_part = total_ref[rows:] + matmul(response_ref[...], block)
        other_ref[...] = response_part.astype(jnp.bfloat16)
        high = wanted_ref[...] >> DIGIT_BITS
        low = wanted_ref[...] - (high << DIGIT_BITS)
        digits = [high.astype(jnp.float32), low.astype(jnp.float32)]
        digits.append(jnp.zeros((TAIL - 2, wanted_ref.shape[1]), jnp.float32))
        out_ref[rows:] = jnp.concatenate(digits, axis=0).astype(jnp.bfloat16)

    results = [
        jax.ShapeDtypeStruct((rows + TAIL, width), jnp.bfloat16),
        jax.ShapeDtypeStruct((rows, width), jnp.bfloat16),
    ]
    return in_vmem(kernel, results, *features, weight, total, wanted, time=0.7)


def pick(prompts, responses, order, depth):
    half = prompts.shape[0] // 2

    def kernel(order_ref, prompt_ref, response_ref, out_ref, sem):
        rows = pl.ds(pl.multiple_of(order_ref[3] * half, half), half)
        for array, ref in enumerate((prompt_ref, response_ref)):

            @pl.when(order_ref[2] == 1 - array)
            def _(ref=ref):
                copies = []
                for k in range(2):
                    start = pl.multiple_of(order_ref[k] * depth, depth)
                    copy = pltpu.make_async_copy(
                        ref.at[rows, pl.ds(start, depth)],
                        out_ref.at[:, k * depth : (k + 1) * depth],
                        sem.at[k],
                    )
                    copy.start()
                    copies.append(copy)
                for copy in copies:
                    copy.wait()

    return pl.pallas_call(
        kernel,
        in_specs=[pl.BlockSpec(memory_space=pltpu.SMEM)]
        + [pl.BlockSpec(memory_space=pltpu.HBM)] * 2,
        out_specs=pl.BlockSpec(memory_space=pltpu.VMEM),
        out_shape=jax.ShapeDtypeStruct((half, 2 * depth), prompts.dtype),
        scratch_shapes=[pltpu.SemaphoreType.DMA((2,))],
        compiler_params=pltpu.CompilerParams(vmem_limit_bytes=4 * 1024 * 1024),
        cost_estimate=cost(1),
    )(order, prompts, responses)


def slices(prompts, responses, blocks, depth):
    count = blocks.shape[0]

    def kernel(block_ref, prompt_ref, response_ref, *refs):
        outs, sem = refs[:-1], refs[-1]
        copies = []
        for k in range(count):
            start = pl.multiple_of(block_ref[k] * depth, depth)
            for array, ref in enumerate((prompt_ref, response_ref)):
                copy = pltpu.make_async_copy(
                    ref.at[:, pl.ds(start, depth)], outs[array * count + k], sem.at[array, k]
                )
                copy.start()
                copies.append(copy)
        for copy in copies:
            copy.wait()

    shape = jax.ShapeDtypeStruct((prompts.shape[0], depth), prompts.dtype)
    return pl.pallas_call(
        kernel,
        in_specs=[pl.BlockSpec(memory_space=pltpu.SMEM)]
        + [pl.BlockSpec(memory_space=pltpu.HBM)] * 2,
        out_specs=[pl.BlockSpec(memory_space=pltpu.VMEM)] * (2 * count),
        out_shape=[shape] * (2 * count),
        scratch_shapes=[pltpu.SemaphoreType.DMA((2, count))],
        compiler_params=pltpu.CompilerParams(vmem_limit_bytes=8 * 1024 * 1024),
        cost_estimate=cost(1),
    )(blocks, prompts, responses)


def own_products(features, grads):
    rows, width = grads[0].shape
    depth = features[0][0].shape[1]
    kinds = [jnp.bfloat16] * 2 + [jnp.float32] * 4

    def kernel(*refs):
        grad_refs, refs = refs[:2], refs[2:]
        for k, kind in enumerate(kinds):
            total = cross_rows(grad_refs[0][...], refs[2 * k][...])
            total += cross_rows(grad_refs[1][...], refs[2 * k + 1][...])
            refs[2 * len(kinds) + k][...] = total.astype(kind)

    results = [jax.ShapeDtypeStruct((width, depth), kind) for kind in kinds]
    arrays = [array for block in features for array in block]
    return in_vmem(kernel, results, *grads, *arrays, time=1)


def in_order(order, fetched, messages):
    half, columns = fetched[0].shape
    height, width = messages[0].shape
    blocks = columns // width

    def kernel(order_ref, *refs):
        for k in range(2):
            for array in range(2):

                @pl.when(order_ref[0] == (array if k else 1 - array))
                def _(ref=refs[k], message=refs[2 + k], out=refs[4 + array]):
                    place = pl.multiple_of(order_ref[1] * half, half)
                    out[pl.ds(place, half)] = ref[...]
                    place = pl.multiple_of((1 - order_ref[1]) * half, half)
                    for block in range(blocks):
                        start = height - (blocks - block) * half
                        columns = slice(block * width, (block + 1) * width)
                        out[pl.ds(place, half), columns] = message[start : start + half]

    inside = pl.BlockSpec(memory_space=pltpu.VMEM)
    return pl.pallas_call(
        kernel,
        in_specs=[pl.BlockSpec(memory_space=pltpu.SMEM)] + [inside] * 4,
        out_specs=[inside] * 2,
        out_shape=[jax.ShapeDtypeStruct((2 * half, columns), fetched[0].dtype)] * 2,
        compiler_params=pltpu.CompilerParams(vmem_limit_bytes=8 * 1024 * 1024),
        cost_estimate=cost(0.5),
    )(order, *fetched, *messages)


def far_products(totals, features, grad, time, last=False):
    width, depth = totals[0].shape

    def kernel(first_ref, second_ref, grad_ref, feature_ref, *outs):
        for k, ref in ((1, second_ref), (0, first_ref)):
            columns = slice(k * depth, (k + 1) * depth)
            total = ref[...] + cross_rows(grad_ref[...], feature_ref[:, columns])
            outs[k][...] = total
            if last:
                outs[2 + k][...] = total.astype(jnp.bfloat16)

    results = [jax.ShapeDtypeStruct((width, depth), jnp.float32)] * 2
    results += [jax.ShapeDtypeStruct((width, depth), jnp.bfloat16)] * 2 * last
    return in_vmem(kernel, results, *totals, grad, features, time=time)


def second_round(*sums):
    def kernel(*refs):
        refs = list(refs)
        for terms, out in zip(sums, refs[-len(sums) :]):
            total = refs.pop(0)[...].astype(jnp.float32)
            for _ in terms[1:]:
                total += refs.pop(0)[...].astype(jnp.float32)
            out[...] = total.astype(jnp.bfloat16)

    shape = jax.ShapeDtypeStruct(sums[0][0].shape, jnp.bfloat16)
    arrays = [term for terms in sums for term in terms]
    return in_vmem(kernel, [shape] * len(sums), *arrays, time=0.5)


def turned_sum(*terms):
    def kernel(*refs):
        total = refs[0][...].astype(jnp.float32)
        for ref in refs[1:-1]:
            total += ref[...].astype(jnp.float32)
        refs[-1][...] = total.T

    shape = terms[0].shape[::-1]
    return in_vmem(kernel, [jax.ShapeDtypeStruct(shape, jnp.float32)], *terms, time=1)[0]


def stacked(blocks):
    rows, width = blocks[0].shape

    def kernel(*refs):
        for k, ref in enumerate(refs[:-1]):
            refs[-1][k * rows : (k + 1) * rows] = ref[...]

    result = jax.ShapeDtypeStruct((len(blocks) * rows, width), blocks[0].dtype)
    return in_vmem(kernel, [result], *blocks, time=0.1)[0]


def summed(terms, count):
    rows, width = terms[0].shape[0], terms[0].shape[1] // count

    def kernel(*refs):
        for k, out in enumerate(refs[len(terms) :]):
            columns = slice(k * width, (k + 1) * width)
            total = refs[0][:, columns]
            for ref in refs[1 : len(terms)]:
                total += ref[:, columns].astype(jnp.float32)
            out[...] = total.astype(jnp.bfloat16)

    result = jax.ShapeDtypeStruct((rows, width), jnp.bfloat16)
    return in_vmem(kernel, [result] * count, *terms, time=4)


def compare(groups, held, wanted, ids, row_count, blocks):
    rows, width = row_count, groups[0][0].shape[1]
    prompt_rows, across = rows * len(groups), len(groups[0])
    count, full = held.shape
    quarter = count // blocks
    factor = LOGIT_SCALE / math.sqrt(E)
    operands = [wanted, ids, *[piece for group in groups for piece in group], held]

    def kernel(wanted_ref, id_ref, *refs):
        group_refs = [refs[g * across : (g + 1) * across] for g in range(len(groups))]
        refs = refs[len(groups) * across :]
        rows_ref, loss_ref, mine_ref, away_ref, *part_refs = refs
        ids = id_ref[...]
        ids = jnp.concatenate([ids] * (rows // ids.shape[1]), axis=1)
        weights, losses = [], []
        for g, pieces in enumerate(group_refs):
            scores = jnp.zeros((count, rows), jnp.float32)
            for k, ref in enumerate(pieces):
                scores += cross_cols(rows_ref[:, k * width : (k + 1) * width], ref[:rows])
            scores = scores * factor + LOGIT_BIAS
            target = wanted_ref[...]
            if g > 0:
                tail = pieces[0][rows:].astype(jnp.float32)
                target = (tail[0:1] * 2.0**DIGIT_BITS + tail[1:2]).astype(jnp.int32)
            match = target == ids
            margin = jnp.where(match, -scores, scores)
            small = jnp.exp(-jnp.abs(margin))
            soft = jnp.maximum(margin, 0.0) + jnp.log1p(small)
            losses.append(jnp.sum(soft, axis=0, keepdims=True))
            share = jnp.where(margin >= 0.0, 1.0, small) / (1.0 + small)
            share = share * (factor / row_count)
            weights.append(jnp.where(match, -share, share).astype(jnp.bfloat16))
        for k in range(across):
            columns = slice(k * width, (k + 1) * width)
            part = sum(
                matmul(weight, pieces[k][:rows]) for weight, pieces in zip(weights, group_refs)
            )
            for block, part_ref in enumerate(part_refs):
                part_rows = part[block * quarter : (block + 1) * quarter]
                part_ref[:, columns] = part_rows.astype(part_ref.dtype)
        for k in range(across):
            out, goal = (mine_ref, away_ref)[k % 2], slice(k // 2 * width, (k // 2 + 1) * width)
            for g, weight in enumerate(weights):
                part = cross_rows(weight, rows_ref[:, k * width : (k + 1) * width])
                out[g * rows : (g + 1) * rows, goal] = part.astype(out.dtype)
        loss = jnp.concatenate(losses, axis=1)
        loss_ref[...] = loss
        away_ref[prompt_rows:] = tail_rows([loss])

    return pl.pallas_call(
        kernel,
        in_specs=[pl.BlockSpec(memory_space=pltpu.VMEM)] * len(operands),
        out_specs=[pl.BlockSpec(memory_space=pltpu.VMEM)] * (3 + blocks),
        out_shape=[
            jax.ShapeDtypeStruct((1, prompt_rows), jnp.float32),
            jax.ShapeDtypeStruct((prompt_rows, full // 2), jnp.float32),
            jax.ShapeDtypeStruct((prompt_rows + TAIL, full // 2), jnp.bfloat16),
            jax.ShapeDtypeStruct((quarter, full), jnp.float32),
        ]
        + [jax.ShapeDtypeStruct((quarter, full), jnp.bfloat16)] * (blocks - 1),
        compiler_params=pltpu.CompilerParams(vmem_limit_bytes=16 * 1024 * 1024),
        cost_estimate=cost(2),
    )(*operands)


def full_window(prompts, responses, head_projection_matrix, positive):
    row_count = prompts.shape[0]
    depth, width = head_projection_matrix.shape
    dp, mp = lax.axis_index("dp"), lax.axis_index("mp")
    z, y = dp // PAIR, dp % PAIR
    quarter = row_count // (SIDE * CORES)
    tie = lax.optimization_barrier

    here = [(z ^ k) * PAIR + y for k in range(LINE)]
    there = [(z ^ k) * PAIR + 1 - y for k in range(LINE)]
    even = (mp % CORES == 0).astype(jnp.int32)
    orders = (
        [there[2], there[3], even, mp // CORES],
        [here[0], there[0], here[1], there[1]],
        [here[3], there[3], here[2]],
        [there[2]],
        there[:2] + here,
        [even, mp // CORES],
    )
    ids = jnp.stack([here[0], here[1], there[1], there[0]]) * row_count + mp * quarter
    ids = (ids.astype(jnp.int32)[:, None] + lax.iota(jnp.int32, quarter)).reshape(-1, 1)
    ids = jnp.broadcast_to(ids, (LINE * quarter, LANES))
    own, orders, places, swap, left, ids = tie(
        (
            head_projection_matrix,
            [jnp.stack(order).astype(jnp.int32) for order in orders],
            [((mp ^ k) * quarter).astype(jnp.uint32) for k in range(SIDE * CORES)],
            even == 1,
            mp < CORES,
            ids,
        )
    )

    picked = pick(prompts, responses, orders[0], depth)
    own_y = send(own, ACROSS_Y)
    first, picked = tie((send(own, PAIRS), picked))
    third = send(own, OPPOSITE)
    second = send(third, PAIRS)
    first_y, third_y = send(first, ACROSS_Y), send(third, ACROSS_Y)
    first, own_y = tie((first, own_y))
    (emb,) = project(
        prompts,
        responses,
        orders[1],
        [(own,), (own_y,), (first,), (first_y,)],
        None,
        jnp.float32,
        20,
    )
    second, emb = tie((second, emb))
    second_y = send(second, ACROSS_Y)
    (emb,) = project(
        prompts,
        responses,
        orders[2],
        [(third,), (third_y,), (second,)],
        emb,
        jnp.float32,
        2.4,
    )
    features = slices(prompts, responses, tie((orders[3], second))[0], depth)
    second_y, emb, features = tie((second_y, emb, features))
    prompt_emb, response_emb = finish(features, second_y, emb, positive[None, :])

    pieces = []
    for k in range(SIDE * CORES):
        piece = lax.dynamic_slice(response_emb, (places[k], jnp.uint32(0)), (quarter, width))
        pieces.append(piece if k == 0 else send(piece, MIX[k]))
    prompt_emb, picked = tie((prompt_emb, picked))
    fetched = send(picked, ACROSS_Y)
    prompt_far, prompt_far_x = send(prompt_emb, FAR), send(prompt_emb, FAR_X)
    beside = [send(prompt_emb, ACROSS_X), prompt_far_x]
    response_rows = jnp.concatenate(pieces, axis=1)

    rows_late, fetched = tie((response_rows, fetched))
    held = [send(response_rows, PAIRS), send(response_rows, PAIRS_Y), send(rows_late, ACROSS_Y)]
    held = stacked([response_rows, *held])
    groups = [[block, send(block, ACROSS_C)] for block in (prompt_emb, prompt_far)]
    sibling = send(fetched, ACROSS_C)
    features = slices(prompts, responses, tie((orders[4], response_rows))[0], depth)
    held = tie(held)
    cross = [send(x, ACROSS_C) for x in beside]
    held, features, cross_tied, fetched = tie((held, features, cross, fetched))
    cross = cross_tied
    features = list(zip(features[:6], features[6:]))
    groups = [[*group, x, across] for group, x, across in zip(groups, beside, cross)]
    losses, mine, away, *parts = compare(
        groups, held, positive[None, :], ids, row_count, LINE
    )

    back = [send(part, table) for part, table in zip(parts[1:], (PAIRS, PAIRS_Y, ACROSS_Y))]
    mine, *messages, losses = after_cores(mine, send(away, ACROSS_C), losses, fetched)
    messages = [send(part, table) for part, table in zip(messages, (FAR, FAR_X, ACROSS_X))]
    pieces = summed([parts[0], *back], SIDE * CORES)

    pieces = [pieces[0]] + [send(pieces[k], MIX[k]) for k in range(1, SIDE * CORES)]
    pieces, messages = tie((pieces, messages))
    swapped = [jnp.where(swap, pieces[k], pieces[k ^ 1]) for k in range(SIDE * CORES)]
    swapped = [jnp.where(left, swapped[k], swapped[k ^ 2]) for k in range(SIDE * CORES)]
    grad_response = jnp.concatenate(swapped, axis=0)
    grad_prompt, losses = after_line(mine, messages, losses)
    grads_y = [send(grad_prompt, ACROSS_Y), send(grad_response, ACROSS_Y)]

    own_y, first_y, own, first, second, third = own_products(
        features, (grad_prompt, grad_response)
    )
    far_features = in_order(
        orders[5], (fetched, sibling), (messages[2], send(messages[2], ACROSS_C))
    )
    own, first, second, third, far_features = tie((own, first, second, third, far_features))
    second, third = far_products((second, third), far_features[1], grads_y[1], 4)
    own_y, first_y = send(own_y, ACROSS_Y), send(first_y, ACROSS_Y)
    second, third, second_b, third_b = far_products(
        (second, third), far_features[0], grads_y[0], 1, last=True
    )
    terms = line_reduce(own, first, second, third, second_b, third_b, own_y, first_y)
    return (losses[0] / row_count, turned_sum(*terms))


def per_device(prompts, responses, head_projection_matrix, positive):
    whole = lax.axis_size("dp") == STEPS == LINE * PAIR
    whole = whole and lax.axis_size("mp") == SIDE * CORES
    step = full_window if whole else general
    return step(prompts, responses, head_projection_matrix, positive)


def solution(mesh):
    return jax.shard_map(
        per_device,
        mesh=mesh,
        in_specs=(P("dp", None), P("dp", None), P("dp", "mp"), P("dp")),
        out_specs=(P("dp"), P("dp", "mp")),
        check_vma=False,
    )
```

```python
import math

import jax
import jax.numpy as jnp
from jax import lax
from jax.experimental import pallas as pl
from jax.experimental.pallas import tpu as pltpu
from jax.sharding import PartitionSpec as P

E = 1024
STEPS = 8


LOGIT_SCALE = 3.0
LOGIT_BIAS = -3.0


def passed_along(block, axis, distance):
    devices = range(lax.axis_size(axis))
    route = [((i - distance) % len(devices), i) for i in devices]
    return lax.ppermute(block, axis, route)


def cross_rows(left_side, righthand_term):
    return lax.dot_general(
        left_side, righthand_term, (((0,), (0,)), ((), ())), preferred_element_type=jnp.float32
    )


def cross_cols(left_side, righthand_term):
    return lax.dot_general(
        left_side, righthand_term, (((1,), (1,)), ((), ())), preferred_element_type=jnp.float32
    )


def matmul(left_side, righthand_term):
    return jnp.dot(left_side, righthand_term, preferred_element_type=jnp.float32)


def general(prompts, responses, head_projection_matrix, positive):
    row_count = prompts.shape[0]
    col_count = head_projection_matrix.shape[1]
    factor = LOGIT_SCALE / math.sqrt(E)
    cycle_size = lax.axis_size("dp")
    position = lax.axis_index("dp")
    segment = lax.all_gather(head_projection_matrix, "dp", axis=0, tiled=True)
    prompt_emb = matmul(prompts, segment).astype(jnp.bfloat16)
    visiting = matmul(responses, segment).astype(jnp.bfloat16)
    local_ids = lax.iota(jnp.int32, row_count)
    prompt_gradient_total = jnp.zeros((row_count, col_count), jnp.float32)
    grad_response = jnp.zeros((row_count, col_count), jnp.float32)
    row_losses = jnp.zeros((row_count,), jnp.float32)
    for offset in range(STEPS):
        partial_logits = cross_cols(prompt_emb, visiting)
        pair_scores = lax.psum(partial_logits, "mp") * factor + LOGIT_BIAS
        anchor = (position - offset) % cycle_size
        column_ids = anchor * row_count + local_ids
        labels = jnp.where(positive[:, None] == column_ids[None, :], 1.0, -1.0).astype(jnp.float32)
        margin = -labels * pair_scores
        row_losses = row_losses + jnp.sum(jax.nn.softplus(margin), axis=1)
        pairwise_weight = (-labels * jax.nn.sigmoid(margin) * (factor / row_count)).astype(
            jnp.bfloat16
        )
        prompt_gradient_total = prompt_gradient_total + matmul(pairwise_weight, visiting)
        contribution = cross_rows(pairwise_weight, prompt_emb)
        if offset == 0:
            grad_response = contribution
        else:
            grad_response = grad_response + passed_along(contribution, "dp", -offset)
        if offset < STEPS - 1:
            visiting = passed_along(visiting, "dp", 1)
    grad_prompt_b = prompt_gradient_total.astype(jnp.bfloat16)
    grad_response_b = grad_response.astype(jnp.bfloat16)
    head_grad = lax.psum_scatter(
        cross_rows(prompts, grad_prompt_b) + cross_rows(responses, grad_response_b),
        "dp",
        scatter_dimension=0,
        tiled=True,
    )
    return (row_losses / row_count, head_grad)


LINE, PAIR, SIDE, CORES = 4, 2, 2, 2


def routes(move):
    table = []
    for z in range(LINE):
        for y in range(PAIR):
            for x in range(SIDE):
                for c in range(CORES):
                    goal = move(z, y, x, c)
                    if goal is not None:
                        gz, gy, gx, gc = goal
                        source = (z * PAIR + y) * SIDE * CORES + x * CORES + c
                        target = (gz * PAIR + gy) * SIDE * CORES + gx * CORES + gc
                        table.append((source, target))
    return table


def along_line(moves):
    return routes(lambda z, y, x, c: (moves[z], y, x, c) if z in moves else None)


def send(block, table):
    return lax.ppermute(block, ("dp", "mp"), table)


ACROSS_Y = routes(lambda z, y, x, c: (z, 1 - y, x, c))
ACROSS_X = routes(lambda z, y, x, c: (z, y, 1 - x, c))
ACROSS_C = routes(lambda z, y, x, c: (z, y, x, 1 - c))
PAIRS = along_line({0: 1, 1: 0, 2: 3, 3: 2})
MIDDLE = along_line({1: 2, 2: 1})
INWARD = along_line({0: 1, 3: 2})
TWO_IN = along_line({3: 1, 0: 2})
OPPOSITE = along_line({0: 3, 1: 2, 2: 1, 3: 0})
FAR = along_line({0: 2, 1: 3, 2: 0, 3: 1})
FAR_X = routes(lambda z, y, x, c: (z ^ 2, y, 1 - x, c))
PAIRS_Y = routes(lambda z, y, x, c: (z ^ 1, 1 - y, x, c))
MIX = [routes(lambda z, y, x, c, k=k: (z, y, x ^ (k >> 1), c ^ (k & 1))) for k in range(4)]


def line_reduce(own, first, second, third, second_b, third_b, own_y, first_y):
    inward, jumped, across, first_y = lax.optimization_barrier(
        (send(second_b, INWARD), send(third_b, TWO_IN), send(second_b, MIDDLE), first_y)
    )
    paired, last = second_round((first, first_y, across, jumped), (third, inward))
    return own, own_y, send(paired, PAIRS), send(last, MIDDLE)


TAIL = 16
DIGIT_BITS = 8
LANES = 128


def cost(microseconds):
    return pl.CostEstimate(flops=int(microseconds * 1e9), bytes_accessed=0, transcendentals=0)


def tail_rows(rows):
    terms = []
    for row in rows:
        for _ in range(3):
            term = row.astype(jnp.bfloat16).astype(jnp.float32)
            terms.append(term)
            row = row - term
    terms.append(jnp.zeros((TAIL - len(terms), rows[0].shape[1]), jnp.float32))
    return jnp.concatenate(terms, axis=0).astype(jnp.bfloat16)


def tail_of(message, row):
    terms = message.astype(jnp.float32)[3 * row : 3 * row + 3]
    return terms[0:1] + terms[1:2] + terms[2:3]


def in_vmem(kernel, results, *operands, time):
    inside = pl.BlockSpec(memory_space=pltpu.VMEM)
    return pl.pallas_call(
        kernel,
        in_specs=[inside] * len(operands),
        out_specs=[inside] * len(results),
        out_shape=results,
        compiler_params=pltpu.CompilerParams(vmem_limit_bytes=12 * 1024 * 1024),
        cost_estimate=cost(time),
    )(*operands)


def after_cores(mine, message, loss, fetched):
    rows, width = mine.shape[0] // 2, mine.shape[1] // 2

    below, blocks = fetched.shape[0], fetched.shape[1] // width

    def kernel(
        mine_ref, message_ref, loss_ref, fetched_ref, kept_ref, far_ref, far_x_ref, x_ref, total_ref
    ):
        total = loss_ref[...] + tail_of(message_ref[2 * rows :], 0)
        total_ref[...] = total[:, :rows]
        tails = [tail_rows([total[:, :rows]]), tail_rows([total[:, rows:]])]
        for k, ref in enumerate((kept_ref, x_ref, far_ref, far_x_ref)):
            place = slice(k // 2 * rows, (k // 2 + 1) * rows)
            columns = slice(k % 2 * width, (k % 2 + 1) * width)
            part = mine_ref[place, columns] + message_ref[place, columns].astype(jnp.float32)
            ref[:rows] = part.astype(ref.dtype)
            if k > 0:
                ref[rows : rows + TAIL] = tails[k // 2]
        for k in range(blocks):
            place = slice(rows + TAIL + k * below, rows + TAIL + (k + 1) * below)
            x_ref[place] = fetched_ref[:, k * width : (k + 1) * width]

    results = [jax.ShapeDtypeStruct((rows, width), jnp.float32)]
    heights = [rows + TAIL] * 2 + [rows + TAIL + below * blocks]
    results += [jax.ShapeDtypeStruct((height, width), jnp.bfloat16) for height in heights]
    results += [jax.ShapeDtypeStruct((1, rows), jnp.float32)]
    return in_vmem(kernel, results, mine, message, loss, fetched, time=0.5)


def after_line(own, messages, loss):
    rows, width = own.shape

    def kernel(own_ref, far_ref, far_x_ref, x_ref, loss_ref, out_ref, total_ref):
        total = own_ref[...]
        for ref in (x_ref, far_ref, far_x_ref):
            total += ref[:rows].astype(jnp.float32)
        out_ref[...] = total.astype(jnp.bfloat16)
        far = tail_of(far_ref[rows:], 0) + tail_of(far_x_ref[rows:], 0)
        total_ref[...] = (loss_ref[...] + tail_of(x_ref[rows : rows + TAIL], 0)) + far

    results = [
        jax.ShapeDtypeStruct((rows, width), jnp.bfloat16),
        jax.ShapeDtypeStruct((1, rows), jnp.float32),
    ]
    return in_vmem(kernel, results, own, *messages, loss, time=0.5)


def project(prompts, responses, blocks, weights, total, kind, time, digits=None):
    row_count = prompts.shape[0]
    depth, width = weights[0][0].shape
    count = len(weights)
    terms = [term for weight in weights for term in weight]
    operands = terms + ([total] if total is not None else [])
    operands += [digits] if digits is not None else []

    def kernel(block_ref, *refs):
        arrays, term_refs, refs = refs[:2], list(refs[2 : 2 + len(terms)]), refs[2 + len(terms) :]
        if total is not None:
            total_ref, *refs = refs
        if digits is not None:
            digit_ref, *refs = refs
        *out_refs, feature_buf, sum_buf, sem = refs

        def columns(array, k):
            start = pl.multiple_of(block_ref[k] * depth, depth)
            return arrays[array].at[:, pl.ds(start, depth)]

        loads = []
        for k in range(count):
            for array in range(2):
                load = pltpu.make_async_copy(
                    columns(array, k), feature_buf.at[k, array], sem.at[k, array]
                )
                load.start()
                loads.append(load)
        for k, weight in enumerate(weights):
            block = term_refs.pop(0)[...]
            for _ in weight[1:]:
                block = block + term_refs.pop(0)[...]
            for array in range(2):
                loads[2 * k + array].wait()
                rows = slice(array * row_count, (array + 1) * row_count)
                part = matmul(feature_buf[k, array], block)
                if k > 0:
                    part += sum_buf[rows]
                elif total is not None:
                    part += total_ref[rows]
                if k < count - 1:
                    sum_buf[rows] = part
                elif digits is not None:
                    out_refs[array][:row_count] = part.astype(kind)
                else:
                    out_refs[0][rows] = part.astype(kind)
        if digits is not None:
            wanted = digit_ref[...]
            high = wanted >> DIGIT_BITS
            low = wanted - (high << DIGIT_BITS)
            rows = [high.astype(jnp.float32), low.astype(jnp.float32)]
            rows.append(jnp.zeros((TAIL - 2, wanted.shape[1]), jnp.float32))
            out_refs[0][row_count:] = jnp.concatenate(rows, axis=0).astype(kind)

    results = [(2 * row_count, width)]
    if digits is not None:
        results = [(row_count + TAIL, width), (row_count, width)]
    results = [jax.ShapeDtypeStruct(shape, kind) for shape in results]
    inside = pl.BlockSpec(memory_space=pltpu.VMEM)
    return pl.pallas_call(
        kernel,
        in_specs=[pl.BlockSpec(memory_space=pltpu.SMEM)]
        + [pl.BlockSpec(memory_space=pltpu.HBM)] * 2
        + [inside] * len(operands),
        out_specs=[inside] * len(results),
        scratch_shapes=[
            pltpu.VMEM((count, 2, row_count, depth), jnp.bfloat16),
            pltpu.VMEM((2 * row_count, width), jnp.float32),
            pltpu.SemaphoreType.DMA((count, 2)),
        ],
        out_shape=results,
        compiler_params=pltpu.CompilerParams(vmem_limit_bytes=12 * 1024 * 1024),
        cost_estimate=cost(time),
    )(blocks, prompts, responses, *operands)


def finish(features, weight, total, wanted):
    (rows, _), width = features[0].shape, weight.shape[1]

    def kernel(prompt_ref, response_ref, weight_ref, total_ref, wanted_ref, out_ref, other_ref):
        block = weight_ref[...]
        prompt_part = total_ref[:rows] + matmul(prompt_ref[...], block)
        out_ref[:rows] = prompt_part.astype(jnp.bfloat16)
        response_part = total_ref[rows:] + matmul(response_ref[...], block)
        other_ref[...] = response_part.astype(jnp.bfloat16)
        high = wanted_ref[...] >> DIGIT_BITS
        low = wanted_ref[...] - (high << DIGIT_BITS)
        digits = [high.astype(jnp.float32), low.astype(jnp.float32)]
        digits.append(jnp.zeros((TAIL - 2, wanted_ref.shape[1]), jnp.float32))
        out_ref[rows:] = jnp.concatenate(digits, axis=0).astype(jnp.bfloat16)

    results = [
        jax.ShapeDtypeStruct((rows + TAIL, width), jnp.bfloat16),
        jax.ShapeDtypeStruct((rows, width), jnp.bfloat16),
    ]
    return in_vmem(kernel, results, *features, weight, total, wanted, time=0.7)


def pick(prompts, responses, order, depth):
    half = prompts.shape[0] // 2

    def kernel(order_ref, prompt_ref, response_ref, out_ref, sem):
        rows = pl.ds(pl.multiple_of(order_ref[3] * half, half), half)
        for array, ref in enumerate((prompt_ref, response_ref)):

            @pl.when(order_ref[2] == 1 - array)
            def _(ref=ref):
                copies = []
                for k in range(2):
                    start = pl.multiple_of(order_ref[k] * depth, depth)
                    copy = pltpu.make_async_copy(
                        ref.at[rows, pl.ds(start, depth)],
                        out_ref.at[:, k * depth : (k + 1) * depth],
                        sem.at[k],
                    )
                    copy.start()
                    copies.append(copy)
                for copy in copies:
                    copy.wait()

    return pl.pallas_call(
        kernel,
        in_specs=[pl.BlockSpec(memory_space=pltpu.SMEM)]
        + [pl.BlockSpec(memory_space=pltpu.HBM)] * 2,
        out_specs=pl.BlockSpec(memory_space=pltpu.VMEM),
        out_shape=jax.ShapeDtypeStruct((half, 2 * depth), prompts.dtype),
        scratch_shapes=[pltpu.SemaphoreType.DMA((2,))],
        compiler_params=pltpu.CompilerParams(vmem_limit_bytes=4 * 1024 * 1024),
        cost_estimate=cost(1),
    )(order, prompts, responses)


def slices(prompts, responses, blocks, depth):
    count = blocks.shape[0]

    def kernel(block_ref, prompt_ref, response_ref, *refs):
        outs, sem = refs[:-1], refs[-1]
        copies = []
        for k in range(count):
            start = pl.multiple_of(block_ref[k] * depth, depth)
            for array, ref in enumerate((prompt_ref, response_ref)):
                copy = pltpu.make_async_copy(
                    ref.at[:, pl.ds(start, depth)], outs[array * count + k], sem.at[array, k]
                )
                copy.start()
                copies.append(copy)
        for copy in copies:
            copy.wait()

    shape = jax.ShapeDtypeStruct((prompts.shape[0], depth), prompts.dtype)
    return pl.pallas_call(
        kernel,
        in_specs=[pl.BlockSpec(memory_space=pltpu.SMEM)]
        + [pl.BlockSpec(memory_space=pltpu.HBM)] * 2,
        out_specs=[pl.BlockSpec(memory_space=pltpu.VMEM)] * (2 * count),
        out_shape=[shape] * (2 * count),
        scratch_shapes=[pltpu.SemaphoreType.DMA((2, count))],
        compiler_params=pltpu.CompilerParams(vmem_limit_bytes=8 * 1024 * 1024),
        cost_estimate=cost(1),
    )(blocks, prompts, responses)


def own_products(features, grads):
    rows, width = grads[0].shape
    depth = features[0][0].shape[1]
    kinds = [jnp.bfloat16] * 2 + [jnp.float32] * 4

    def kernel(*refs):
        grad_refs, refs = refs[:2], refs[2:]
        for k, kind in enumerate(kinds):
            total = cross_rows(grad_refs[0][...], refs[2 * k][...])
            total += cross_rows(grad_refs[1][...], refs[2 * k + 1][...])
            refs[2 * len(kinds) + k][...] = total.astype(kind)

    results = [jax.ShapeDtypeStruct((width, depth), kind) for kind in kinds]
    arrays = [array for block in features for array in block]
    return in_vmem(kernel, results, *grads, *arrays, time=1)


def in_order(order, fetched, messages):
    half, columns = fetched[0].shape
    height, width = messages[0].shape
    blocks = columns // width

    def kernel(order_ref, *refs):
        for k in range(2):
            for array in range(2):

                @pl.when(order_ref[0] == (array if k else 1 - array))
                def _(ref=refs[k], message=refs[2 + k], out=refs[4 + array]):
                    place = pl.multiple_of(order_ref[1] * half, half)
                    out[pl.ds(place, half)] = ref[...]
                    place = pl.multiple_of((1 - order_ref[1]) * half, half)
                    for block in range(blocks):
                        start = height - (blocks - block) * half
                        columns = slice(block * width, (block + 1) * width)
                        out[pl.ds(place, half), columns] = message[start : start + half]

    inside = pl.BlockSpec(memory_space=pltpu.VMEM)
    return pl.pallas_call(
        kernel,
        in_specs=[pl.BlockSpec(memory_space=pltpu.SMEM)] + [inside] * 4,
        out_specs=[inside] * 2,
        out_shape=[jax.ShapeDtypeStruct((2 * half, columns), fetched[0].dtype)] * 2,
        compiler_params=pltpu.CompilerParams(vmem_limit_bytes=8 * 1024 * 1024),
        cost_estimate=cost(0.5),
    )(order, *fetched, *messages)


def far_products(totals, features, grad, time, last=False):
    width, depth = totals[0].shape

    def kernel(first_ref, second_ref, grad_ref, feature_ref, *outs):
        for k, ref in ((1, second_ref), (0, first_ref)):
            columns = slice(k * depth, (k + 1) * depth)
            total = ref[...] + cross_rows(grad_ref[...], feature_ref[:, columns])
            outs[k][...] = total
            if last:
                outs[2 + k][...] = total.astype(jnp.bfloat16)

    results = [jax.ShapeDtypeStruct((width, depth), jnp.float32)] * 2
    results += [jax.ShapeDtypeStruct((width, depth), jnp.bfloat16)] * 2 * last
    return in_vmem(kernel, results, *totals, grad, features, time=time)


def second_round(*sums):
    def kernel(*refs):
        refs = list(refs)
        for terms, out in zip(sums, refs[-len(sums) :]):
            total = refs.pop(0)[...].astype(jnp.float32)
            for _ in terms[1:]:
                total += refs.pop(0)[...].astype(jnp.float32)
            out[...] = total.astype(jnp.bfloat16)

    shape = jax.ShapeDtypeStruct(sums[0][0].shape, jnp.bfloat16)
    arrays = [term for terms in sums for term in terms]
    return in_vmem(kernel, [shape] * len(sums), *arrays, time=0.5)


def turned_sum(*terms):
    def kernel(*refs):
        total = refs[0][...].astype(jnp.float32)
        for ref in refs[1:-1]:
            total += ref[...].astype(jnp.float32)
        refs[-1][...] = total.T

    shape = terms[0].shape[::-1]
    return in_vmem(kernel, [jax.ShapeDtypeStruct(shape, jnp.float32)], *terms, time=1)[0]


def stacked(blocks):
    rows, width = blocks[0].shape

    def kernel(*refs):
        for k, ref in enumerate(refs[:-1]):
            refs[-1][k * rows : (k + 1) * rows] = ref[...]

    result = jax.ShapeDtypeStruct((len(blocks) * rows, width), blocks[0].dtype)
    return in_vmem(kernel, [result], *blocks, time=0.1)[0]


def summed(terms, count):
    rows, width = terms[0].shape[0], terms[0].shape[1] // count

    def kernel(*refs):
        for k, out in enumerate(refs[len(terms) :]):
            columns = slice(k * width, (k + 1) * width)
            total = refs[0][:, columns]
            for ref in refs[1 : len(terms)]:
                total += ref[:, columns].astype(jnp.float32)
            out[...] = total.astype(jnp.bfloat16)

    result = jax.ShapeDtypeStruct((rows, width), jnp.bfloat16)
    return in_vmem(kernel, [result] * count, *terms, time=4)


def compare(groups, held, wanted, ids, row_count, blocks):
    rows, width = row_count, groups[0][0].shape[1]
    prompt_rows, across = rows * len(groups), len(groups[0])
    count, full = held.shape
    quarter = count // blocks
    factor = LOGIT_SCALE / math.sqrt(E)
    operands = [wanted, ids, *[piece for group in groups for piece in group], held]

    def kernel(wanted_ref, id_ref, *refs):
        group_refs = [refs[g * across : (g + 1) * across] for g in range(len(groups))]
        refs = refs[len(groups) * across :]
        rows_ref, loss_ref, mine_ref, away_ref, *part_refs = refs
        ids = id_ref[...]
        ids = jnp.concatenate([ids] * (rows // ids.shape[1]), axis=1)
        weights, losses = [], []
        for g, pieces in enumerate(group_refs):
            scores = jnp.zeros((count, rows), jnp.float32)
            for k, ref in enumerate(pieces):
                scores += cross_cols(rows_ref[:, k * width : (k + 1) * width], ref[:rows])
            scores = scores * factor + LOGIT_BIAS
            target = wanted_ref[...]
            if g > 0:
                tail = pieces[0][rows:].astype(jnp.float32)
                target = (tail[0:1] * 2.0**DIGIT_BITS + tail[1:2]).astype(jnp.int32)
            match = target == ids
            margin = jnp.where(match, -scores, scores)
            small = jnp.exp(-jnp.abs(margin))
            soft = jnp.maximum(margin, 0.0) + jnp.log1p(small)
            losses.append(jnp.sum(soft, axis=0, keepdims=True))
            share = jnp.where(margin >= 0.0, 1.0, small) / (1.0 + small)
            share = share * (factor / row_count)
            weights.append(jnp.where(match, -share, share).astype(jnp.bfloat16))
        for k in range(across):
            columns = slice(k * width, (k + 1) * width)
            part = sum(
                matmul(weight, pieces[k][:rows]) for weight, pieces in zip(weights, group_refs)
            )
            for block, part_ref in enumerate(part_refs):
                part_rows = part[block * quarter : (block + 1) * quarter]
                part_ref[:, columns] = part_rows.astype(part_ref.dtype)
        for k in range(across):
            out, goal = (mine_ref, away_ref)[k % 2], slice(k // 2 * width, (k // 2 + 1) * width)
            for g, weight in enumerate(weights):
                part = cross_rows(weight, rows_ref[:, k * width : (k + 1) * width])
                out[g * rows : (g + 1) * rows, goal] = part.astype(out.dtype)
        loss = jnp.concatenate(losses, axis=1)
        loss_ref[...] = loss
        away_ref[prompt_rows:] = tail_rows([loss])

    return pl.pallas_call(
        kernel,
        in_specs=[pl.BlockSpec(memory_space=pltpu.VMEM)] * len(operands),
        out_specs=[pl.BlockSpec(memory_space=pltpu.VMEM)] * (3 + blocks),
        out_shape=[
            jax.ShapeDtypeStruct((1, prompt_rows), jnp.float32),
            jax.ShapeDtypeStruct((prompt_rows, full // 2), jnp.float32),
            jax.ShapeDtypeStruct((prompt_rows + TAIL, full // 2), jnp.bfloat16),
            jax.ShapeDtypeStruct((quarter, full), jnp.float32),
        ]
        + [jax.ShapeDtypeStruct((quarter, full), jnp.bfloat16)] * (blocks - 1),
        compiler_params=pltpu.CompilerParams(vmem_limit_bytes=16 * 1024 * 1024),
        cost_estimate=cost(2),
    )(*operands)


def full_window(prompts, responses, head_projection_matrix, positive):
    row_count = prompts.shape[0]
    depth, width = head_projection_matrix.shape
    dp, mp = lax.axis_index("dp"), lax.axis_index("mp")
    z, y = dp // PAIR, dp % PAIR
    quarter = row_count // (SIDE * CORES)
    tie = lax.optimization_barrier

    here = [(z ^ k) * PAIR + y for k in range(LINE)]
    there = [(z ^ k) * PAIR + 1 - y for k in range(LINE)]
    even = (mp % CORES == 0).astype(jnp.int32)
    orders = (
        [there[2], there[3], even, mp // CORES],
        [here[0], there[0], here[1], there[1]],
        [here[3], there[3], here[2]],
        [there[2]],
        there[:2] + here,
        [even, mp // CORES],
    )
    ids = jnp.stack([here[0], here[1], there[1], there[0]]) * row_count + mp * quarter
    ids = (ids.astype(jnp.int32)[:, None] + lax.iota(jnp.int32, quarter)).reshape(-1, 1)
    ids = jnp.broadcast_to(ids, (LINE * quarter, LANES))
    own, orders, places, swap, left, ids = tie(
        (
            head_projection_matrix,
            [jnp.stack(order).astype(jnp.int32) for order in orders],
            [((mp ^ k) * quarter).astype(jnp.uint32) for k in range(SIDE * CORES)],
            even == 1,
            mp < CORES,
            ids,
        )
    )

    picked = pick(prompts, responses, orders[0], depth)
    own_y = send(own, ACROSS_Y)
    first, picked = tie((send(own, PAIRS), picked))
    third = send(own, OPPOSITE)
    second = send(third, PAIRS)
    first_y, third_y = send(first, ACROSS_Y), send(third, ACROSS_Y)
    first, own_y = tie((first, own_y))
    (emb,) = project(
        prompts,
        responses,
        orders[1],
        [(own,), (own_y,), (first,), (first_y,)],
        None,
        jnp.float32,
        20,
    )
    second, emb = tie((second, emb))
    second_y = send(second, ACROSS_Y)
    (emb,) = project(
        prompts,
        responses,
        orders[2],
        [(third,), (third_y,), (second,)],
        emb,
        jnp.float32,
        2.4,
    )
    features = slices(prompts, responses, tie((orders[3], second))[0], depth)
    second_y, emb, features = tie((second_y, emb, features))
    prompt_emb, response_emb = finish(features, second_y, emb, positive[None, :])

    pieces = []
    for k in range(SIDE * CORES):
        piece = lax.dynamic_slice(response_emb, (places[k], jnp.uint32(0)), (quarter, width))
        pieces.append(piece if k == 0 else send(piece, MIX[k]))
    pieces, picked = tie((pieces, picked))
    fetched = send(picked, ACROSS_Y)
    prompt_far, prompt_far_x = send(prompt_emb, FAR), send(prompt_emb, FAR_X)
    beside = [send(prompt_emb, ACROSS_X), prompt_far_x]
    response_rows = jnp.concatenate(pieces, axis=1)

    rows_late, fetched = tie((response_rows, fetched))
    held = [send(response_rows, PAIRS), send(response_rows, PAIRS_Y), send(rows_late, ACROSS_Y)]
    held = stacked([response_rows, *held])
    groups = [[block, send(block, ACROSS_C)] for block in (prompt_emb, prompt_far)]
    sibling = send(fetched, ACROSS_C)
    features = slices(prompts, responses, tie((orders[4], response_rows))[0], depth)
    held = tie(held)
    cross = [send(x, ACROSS_C) for x in beside]
    held, features, cross_tied, fetched = tie((held, features, cross, fetched))
    cross = cross_tied
    features = list(zip(features[:6], features[6:]))
    groups = [[*group, x, across] for group, x, across in zip(groups, beside, cross)]
    losses, mine, away, *parts = compare(
        groups, held, positive[None, :], ids, row_count, LINE
    )

    back = [send(part, table) for part, table in zip(parts[1:], (PAIRS, PAIRS_Y, ACROSS_Y))]
    mine, *messages, losses = after_cores(mine, send(away, ACROSS_C), losses, fetched)
    messages = [send(part, table) for part, table in zip(messages, (FAR, FAR_X, ACROSS_X))]
    pieces = summed([parts[0], *back], SIDE * CORES)

    pieces = [pieces[0]] + [send(pieces[k], MIX[k]) for k in range(1, SIDE * CORES)]
    pieces, messages = tie((pieces, messages))
    swapped = [jnp.where(swap, pieces[k], pieces[k ^ 1]) for k in range(SIDE * CORES)]
    swapped = [jnp.where(left, swapped[k], swapped[k ^ 2]) for k in range(SIDE * CORES)]
    grad_response = jnp.concatenate(swapped, axis=0)
    grad_prompt, losses = after_line(mine, messages, losses)
    grads_y = [send(grad_prompt, ACROSS_Y), send(grad_response, ACROSS_Y)]

    own_y, first_y, own, first, second, third = own_products(
        features, (grad_prompt, grad_response)
    )
    far_features = in_order(
        orders[5], (fetched, sibling), (messages[2], send(messages[2], ACROSS_C))
    )
    own, first, second, third, far_features = tie((own, first, second, third, far_features))
    second, third = far_products((second, third), far_features[1], grads_y[1], 4)
    own_y, first_y = send(own_y, ACROSS_Y), send(first_y, ACROSS_Y)
    second, third, second_b, third_b = far_products(
        (second, third), far_features[0], grads_y[0], 1, last=True
    )
    terms = line_reduce(own, first, second, third, second_b, third_b, own_y, first_y)
    return (losses[0] / row_count, turned_sum(*terms))


def per_device(prompts, responses, head_projection_matrix, positive):
    whole = lax.axis_size("dp") == STEPS == LINE * PAIR
    whole = whole and lax.axis_size("mp") == SIDE * CORES
    step = full_window if whole else general
    return step(prompts, responses, head_projection_matrix, positive)


def solution(mesh):
    return jax.shard_map(
        per_device,
        mesh=mesh,
        in_specs=(P("dp", None), P("dp", None), P("dp", "mp"), P("dp")),
        out_specs=(P("dp"), P("dp", "mp")),
        check_vma=False,
    )
```

```python
import math

import jax
import jax.numpy as jnp
from jax import lax
from jax.experimental import pallas as pl
from jax.experimental.pallas import tpu as pltpu
from jax.sharding import PartitionSpec as P

E = 1024
STEPS = 8


LOGIT_SCALE = 3.0
LOGIT_BIAS = -3.0


def passed_along(block, axis, distance):
    devices = range(lax.axis_size(axis))
    route = [((i - distance) % len(devices), i) for i in devices]
    return lax.ppermute(block, axis, route)


def cross_rows(left_side, righthand_term):
    return lax.dot_general(
        left_side, righthand_term, (((0,), (0,)), ((), ())), preferred_element_type=jnp.float32
    )


def cross_cols(left_side, righthand_term):
    return lax.dot_general(
        left_side, righthand_term, (((1,), (1,)), ((), ())), preferred_element_type=jnp.float32
    )


def matmul(left_side, righthand_term):
    return jnp.dot(left_side, righthand_term, preferred_element_type=jnp.float32)


def general(prompts, responses, head_projection_matrix, positive):
    row_count = prompts.shape[0]
    col_count = head_projection_matrix.shape[1]
    factor = LOGIT_SCALE / math.sqrt(E)
    cycle_size = lax.axis_size("dp")
    position = lax.axis_index("dp")
    segment = lax.all_gather(head_projection_matrix, "dp", axis=0, tiled=True)
    prompt_emb = matmul(prompts, segment).astype(jnp.bfloat16)
    visiting = matmul(responses, segment).astype(jnp.bfloat16)
    local_ids = lax.iota(jnp.int32, row_count)
    prompt_gradient_total = jnp.zeros((row_count, col_count), jnp.float32)
    grad_response = jnp.zeros((row_count, col_count), jnp.float32)
    row_losses = jnp.zeros((row_count,), jnp.float32)
    for offset in range(STEPS):
        partial_logits = cross_cols(prompt_emb, visiting)
        pair_scores = lax.psum(partial_logits, "mp") * factor + LOGIT_BIAS
        anchor = (position - offset) % cycle_size
        column_ids = anchor * row_count + local_ids
        labels = jnp.where(positive[:, None] == column_ids[None, :], 1.0, -1.0).astype(jnp.float32)
        margin = -labels * pair_scores
        row_losses = row_losses + jnp.sum(jax.nn.softplus(margin), axis=1)
        pairwise_weight = (-labels * jax.nn.sigmoid(margin) * (factor / row_count)).astype(
            jnp.bfloat16
        )
        prompt_gradient_total = prompt_gradient_total + matmul(pairwise_weight, visiting)
        contribution = cross_rows(pairwise_weight, prompt_emb)
        if offset == 0:
            grad_response = contribution
        else:
            grad_response = grad_response + passed_along(contribution, "dp", -offset)
        if offset < STEPS - 1:
            visiting = passed_along(visiting, "dp", 1)
    grad_prompt_b = prompt_gradient_total.astype(jnp.bfloat16)
    grad_response_b = grad_response.astype(jnp.bfloat16)
    head_grad = lax.psum_scatter(
        cross_rows(prompts, grad_prompt_b) + cross_rows(responses, grad_response_b),
        "dp",
        scatter_dimension=0,
        tiled=True,
    )
    return (row_losses / row_count, head_grad)


LINE, PAIR, SIDE, CORES = 4, 2, 2, 2


def routes(move):
    table = []
    for z in range(LINE):
        for y in range(PAIR):
            for x in range(SIDE):
                for c in range(CORES):
                    goal = move(z, y, x, c)
                    if goal is not None:
                        gz, gy, gx, gc = goal
                        source = (z * PAIR + y) * SIDE * CORES + x * CORES + c
                        target = (gz * PAIR + gy) * SIDE * CORES + gx * CORES + gc
                        table.append((source, target))
    return table


def along_line(moves):
    return routes(lambda z, y, x, c: (moves[z], y, x, c) if z in moves else None)


def send(block, table):
    return lax.ppermute(block, ("dp", "mp"), table)


ACROSS_Y = routes(lambda z, y, x, c: (z, 1 - y, x, c))
ACROSS_X = routes(lambda z, y, x, c: (z, y, 1 - x, c))
ACROSS_C = routes(lambda z, y, x, c: (z, y, x, 1 - c))
PAIRS = along_line({0: 1, 1: 0, 2: 3, 3: 2})
MIDDLE = along_line({1: 2, 2: 1})
INWARD = along_line({0: 1, 3: 2})
TWO_IN = along_line({3: 1, 0: 2})
OPPOSITE = along_line({0: 3, 1: 2, 2: 1, 3: 0})
FAR = along_line({0: 2, 1: 3, 2: 0, 3: 1})
FAR_X = routes(lambda z, y, x, c: (z ^ 2, y, 1 - x, c))
PAIRS_Y = routes(lambda z, y, x, c: (z ^ 1, 1 - y, x, c))
MIX = [routes(lambda z, y, x, c, k=k: (z, y, x ^ (k >> 1), c ^ (k & 1))) for k in range(4)]


def line_reduce(own, first, second, third, second_b, third_b, own_y, first_y):
    inward, jumped, across, first_y = lax.optimization_barrier(
        (send(second_b, INWARD), send(third_b, TWO_IN), send(second_b, MIDDLE), first_y)
    )
    paired, last = second_round((first, first_y, across, jumped), (third, inward))
    return own, own_y, send(paired, PAIRS), send(last, MIDDLE)


TAIL = 16
DIGIT_BITS = 8
LANES = 128


def cost(microseconds):
    return pl.CostEstimate(flops=int(microseconds * 1e9), bytes_accessed=0, transcendentals=0)


def tail_rows(rows):
    terms = []
    for row in rows:
        for _ in range(3):
            term = row.astype(jnp.bfloat16).astype(jnp.float32)
            terms.append(term)
            row = row - term
    terms.append(jnp.zeros((TAIL - len(terms), rows[0].shape[1]), jnp.float32))
    return jnp.concatenate(terms, axis=0).astype(jnp.bfloat16)


def tail_of(message, row):
    terms = message.astype(jnp.float32)[3 * row : 3 * row + 3]
    return terms[0:1] + terms[1:2] + terms[2:3]


def in_vmem(kernel, results, *operands, time):
    inside = pl.BlockSpec(memory_space=pltpu.VMEM)
    return pl.pallas_call(
        kernel,
        in_specs=[inside] * len(operands),
        out_specs=[inside] * len(results),
        out_shape=results,
        compiler_params=pltpu.CompilerParams(vmem_limit_bytes=12 * 1024 * 1024),
        cost_estimate=cost(time),
    )(*operands)


def after_cores(mine, message, loss, fetched):
    rows, width = mine.shape[0] // 2, mine.shape[1] // 2

    below, blocks = fetched.shape[0], fetched.shape[1] // width

    def kernel(
        mine_ref, message_ref, loss_ref, fetched_ref, kept_ref, far_ref, far_x_ref, x_ref, total_ref
    ):
        total = loss_ref[...] + tail_of(message_ref[2 * rows :], 0)
        total_ref[...] = total[:, :rows]
        tails = [tail_rows([total[:, :rows]]), tail_rows([total[:, rows:]])]
        for k, ref in enumerate((kept_ref, x_ref, far_ref, far_x_ref)):
            place = slice(k // 2 * rows, (k // 2 + 1) * rows)
            columns = slice(k % 2 * width, (k % 2 + 1) * width)
            part = mine_ref[place, columns] + message_ref[place, columns].astype(jnp.float32)
            ref[:rows] = part.astype(ref.dtype)
            if k > 0:
                ref[rows : rows + TAIL] = tails[k // 2]
        for k in range(blocks):
            place = slice(rows + TAIL + k * below, rows + TAIL + (k + 1) * below)
            x_ref[place] = fetched_ref[:, k * width : (k + 1) * width]

    results = [jax.ShapeDtypeStruct((rows, width), jnp.float32)]
    heights = [rows + TAIL] * 2 + [rows + TAIL + below * blocks]
    results += [jax.ShapeDtypeStruct((height, width), jnp.bfloat16) for height in heights]
    results += [jax.ShapeDtypeStruct((1, rows), jnp.float32)]
    return in_vmem(kernel, results, mine, message, loss, fetched, time=0.5)


def after_line(own, messages, loss):
    rows, width = own.shape

    def kernel(own_ref, far_ref, far_x_ref, x_ref, loss_ref, out_ref, total_ref):
        total = own_ref[...]
        for ref in (x_ref, far_ref, far_x_ref):
            total += ref[:rows].astype(jnp.float32)
        out_ref[...] = total.astype(jnp.bfloat16)
        far = tail_of(far_ref[rows:], 0) + tail_of(far_x_ref[rows:], 0)
        total_ref[...] = (loss_ref[...] + tail_of(x_ref[rows : rows + TAIL], 0)) + far

    results = [
        jax.ShapeDtypeStruct((rows, width), jnp.bfloat16),
        jax.ShapeDtypeStruct((1, rows), jnp.float32),
    ]
    return in_vmem(kernel, results, own, *messages, loss, time=0.5)


def project(prompts, responses, blocks, weights, total, kind, time, digits=None):
    row_count = prompts.shape[0]
    depth, width = weights[0][0].shape
    count = len(weights)
    terms = [term for weight in weights for term in weight]
    operands = terms + ([total] if total is not None else [])
    operands += [digits] if digits is not None else []

    def kernel(block_ref, *refs):
        arrays, term_refs, refs = refs[:2], list(refs[2 : 2 + len(terms)]), refs[2 + len(terms) :]
        if total is not None:
            total_ref, *refs = refs
        if digits is not None:
            digit_ref, *refs = refs
        *out_refs, feature_buf, sum_buf, sem = refs

        def columns(array, k):
            start = pl.multiple_of(block_ref[k] * depth, depth)
            return arrays[array].at[:, pl.ds(start, depth)]

        loads = []
        for k in range(count):
            for array in range(2):
                load = pltpu.make_async_copy(
                    columns(array, k), feature_buf.at[k, array], sem.at[k, array]
                )
                load.start()
                loads.append(load)
        for k, weight in enumerate(weights):
            block = term_refs.pop(0)[...]
            for _ in weight[1:]:
                block = block + term_refs.pop(0)[...]
            for array in range(2):
                loads[2 * k + array].wait()
                rows = slice(array * row_count, (array + 1) * row_count)
                part = matmul(feature_buf[k, array], block)
                if k > 0:
                    part += sum_buf[rows]
                elif total is not None:
                    part += total_ref[rows]
                if k < count - 1:
                    sum_buf[rows] = part
                elif digits is not None:
                    out_refs[array][:row_count] = part.astype(kind)
                else:
                    out_refs[0][rows] = part.astype(kind)
        if digits is not None:
            wanted = digit_ref[...]
            high = wanted >> DIGIT_BITS
            low = wanted - (high << DIGIT_BITS)
            rows = [high.astype(jnp.float32), low.astype(jnp.float32)]
            rows.append(jnp.zeros((TAIL - 2, wanted.shape[1]), jnp.float32))
            out_refs[0][row_count:] = jnp.concatenate(rows, axis=0).astype(kind)

    results = [(2 * row_count, width)]
    if digits is not None:
        results = [(row_count + TAIL, width), (row_count, width)]
    results = [jax.ShapeDtypeStruct(shape, kind) for shape in results]
    inside = pl.BlockSpec(memory_space=pltpu.VMEM)
    return pl.pallas_call(
        kernel,
        in_specs=[pl.BlockSpec(memory_space=pltpu.SMEM)]
        + [pl.BlockSpec(memory_space=pltpu.HBM)] * 2
        + [inside] * len(operands),
        out_specs=[inside] * len(results),
        scratch_shapes=[
            pltpu.VMEM((count, 2, row_count, depth), jnp.bfloat16),
            pltpu.VMEM((2 * row_count, width), jnp.float32),
            pltpu.SemaphoreType.DMA((count, 2)),
        ],
        out_shape=results,
        compiler_params=pltpu.CompilerParams(vmem_limit_bytes=12 * 1024 * 1024),
        cost_estimate=cost(time),
    )(blocks, prompts, responses, *operands)


def finish(features, weight, total, wanted):
    (rows, _), width = features[0].shape, weight.shape[1]

    def kernel(prompt_ref, response_ref, weight_ref, total_ref, wanted_ref, out_ref, other_ref):
        block = weight_ref[...]
        prompt_part = total_ref[:rows] + matmul(prompt_ref[...], block)
        out_ref[:rows] = prompt_part.astype(jnp.bfloat16)
        response_part = total_ref[rows:] + matmul(response_ref[...], block)
        other_ref[...] = response_part.astype(jnp.bfloat16)
        high = wanted_ref[...] >> DIGIT_BITS
        low = wanted_ref[...] - (high << DIGIT_BITS)
        digits = [high.astype(jnp.float32), low.astype(jnp.float32)]
        digits.append(jnp.zeros((TAIL - 2, wanted_ref.shape[1]), jnp.float32))
        out_ref[rows:] = jnp.concatenate(digits, axis=0).astype(jnp.bfloat16)

    results = [
        jax.ShapeDtypeStruct((rows + TAIL, width), jnp.bfloat16),
        jax.ShapeDtypeStruct((rows, width), jnp.bfloat16),
    ]
    return in_vmem(kernel, results, *features, weight, total, wanted, time=0.7)


def pick(prompts, responses, order, depth):
    half = prompts.shape[0] // 2

    def kernel(order_ref, prompt_ref, response_ref, out_ref, sem):
        rows = pl.ds(pl.multiple_of(order_ref[3] * half, half), half)
        for array, ref in enumerate((prompt_ref, response_ref)):

            @pl.when(order_ref[2] == 1 - array)
            def _(ref=ref):
                copies = []
                for k in range(2):
                    start = pl.multiple_of(order_ref[k] * depth, depth)
                    copy = pltpu.make_async_copy(
                        ref.at[rows, pl.ds(start, depth)],
                        out_ref.at[:, k * depth : (k + 1) * depth],
                        sem.at[k],
                    )
                    copy.start()
                    copies.append(copy)
                for copy in copies:
                    copy.wait()

    return pl.pallas_call(
        kernel,
        in_specs=[pl.BlockSpec(memory_space=pltpu.SMEM)]
        + [pl.BlockSpec(memory_space=pltpu.HBM)] * 2,
        out_specs=pl.BlockSpec(memory_space=pltpu.VMEM),
        out_shape=jax.ShapeDtypeStruct((half, 2 * depth), prompts.dtype),
        scratch_shapes=[pltpu.SemaphoreType.DMA((2,))],
        compiler_params=pltpu.CompilerParams(vmem_limit_bytes=4 * 1024 * 1024),
        cost_estimate=cost(1),
    )(order, prompts, responses)


def slices(prompts, responses, blocks, depth):
    count = blocks.shape[0]

    def kernel(block_ref, prompt_ref, response_ref, *refs):
        outs, sem = refs[:-1], refs[-1]
        copies = []
        for k in range(count):
            start = pl.multiple_of(block_ref[k] * depth, depth)
            for array, ref in enumerate((prompt_ref, response_ref)):
                copy = pltpu.make_async_copy(
                    ref.at[:, pl.ds(start, depth)], outs[array * count + k], sem.at[array, k]
                )
                copy.start()
                copies.append(copy)
        for copy in copies:
            copy.wait()

    shape = jax.ShapeDtypeStruct((prompts.shape[0], depth), prompts.dtype)
    return pl.pallas_call(
        kernel,
        in_specs=[pl.BlockSpec(memory_space=pltpu.SMEM)]
        + [pl.BlockSpec(memory_space=pltpu.HBM)] * 2,
        out_specs=[pl.BlockSpec(memory_space=pltpu.VMEM)] * (2 * count),
        out_shape=[shape] * (2 * count),
        scratch_shapes=[pltpu.SemaphoreType.DMA((2, count))],
        compiler_params=pltpu.CompilerParams(vmem_limit_bytes=8 * 1024 * 1024),
        cost_estimate=cost(1),
    )(blocks, prompts, responses)


def own_products(features, grads):
    rows, width = grads[0].shape
    depth = features[0][0].shape[1]
    kinds = [jnp.bfloat16] * 2 + [jnp.float32] * 4

    def kernel(*refs):
        grad_refs, refs = refs[:2], refs[2:]
        for k, kind in enumerate(kinds):
            total = cross_rows(grad_refs[0][...], refs[2 * k][...])
            total += cross_rows(grad_refs[1][...], refs[2 * k + 1][...])
            refs[2 * len(kinds) + k][...] = total.astype(kind)

    results = [jax.ShapeDtypeStruct((width, depth), kind) for kind in kinds]
    arrays = [array for block in features for array in block]
    return in_vmem(kernel, results, *grads, *arrays, time=1)


def in_order(order, fetched, messages):
    half, columns = fetched[0].shape
    height, width = messages[0].shape
    blocks = columns // width

    def kernel(order_ref, *refs):
        for k in range(2):
            for array in range(2):

                @pl.when(order_ref[0] == (array if k else 1 - array))
                def _(ref=refs[k], message=refs[2 + k], out=refs[4 + array]):
                    place = pl.multiple_of(order_ref[1] * half, half)
                    out[pl.ds(place, half)] = ref[...]
                    place = pl.multiple_of((1 - order_ref[1]) * half, half)
                    for block in range(blocks):
                        start = height - (blocks - block) * half
                        columns = slice(block * width, (block + 1) * width)
                        out[pl.ds(place, half), columns] = message[start : start + half]

    inside = pl.BlockSpec(memory_space=pltpu.VMEM)
    return pl.pallas_call(
        kernel,
        in_specs=[pl.BlockSpec(memory_space=pltpu.SMEM)] + [inside] * 4,
        out_specs=[inside] * 2,
        out_shape=[jax.ShapeDtypeStruct((2 * half, columns), fetched[0].dtype)] * 2,
        compiler_params=pltpu.CompilerParams(vmem_limit_bytes=8 * 1024 * 1024),
        cost_estimate=cost(0.5),
    )(order, *fetched, *messages)


def far_products(totals, features, grad, time, last=False):
    width, depth = totals[0].shape

    def kernel(first_ref, second_ref, grad_ref, feature_ref, *outs):
        for k, ref in ((1, second_ref), (0, first_ref)):
            columns = slice(k * depth, (k + 1) * depth)
            total = ref[...] + cross_rows(grad_ref[...], feature_ref[:, columns])
            outs[k][...] = total
            if last:
                outs[2 + k][...] = total.astype(jnp.bfloat16)

    results = [jax.ShapeDtypeStruct((width, depth), jnp.float32)] * 2
    results += [jax.ShapeDtypeStruct((width, depth), jnp.bfloat16)] * 2 * last
    return in_vmem(kernel, results, *totals, grad, features, time=time)


def second_round(*sums):
    def kernel(*refs):
        refs = list(refs)
        for terms, out in zip(sums, refs[-len(sums) :]):
            total = refs.pop(0)[...].astype(jnp.float32)
            for _ in terms[1:]:
                total += refs.pop(0)[...].astype(jnp.float32)
            out[...] = total.astype(jnp.bfloat16)

    shape = jax.ShapeDtypeStruct(sums[0][0].shape, jnp.bfloat16)
    arrays = [term for terms in sums for term in terms]
    return in_vmem(kernel, [shape] * len(sums), *arrays, time=0.5)


def turned_sum(*terms):
    def kernel(*refs):
        total = refs[0][...].astype(jnp.float32)
        for ref in refs[1:-1]:
            total += ref[...].astype(jnp.float32)
        refs[-1][...] = total.T

    shape = terms[0].shape[::-1]
    return in_vmem(kernel, [jax.ShapeDtypeStruct(shape, jnp.float32)], *terms, time=1)[0]


def stacked(blocks):
    rows, width = blocks[0].shape

    def kernel(*refs):
        for k, ref in enumerate(refs[:-1]):
            refs[-1][k * rows : (k + 1) * rows] = ref[...]

    result = jax.ShapeDtypeStruct((len(blocks) * rows, width), blocks[0].dtype)
    return in_vmem(kernel, [result], *blocks, time=0.1)[0]


def summed(terms, count):
    rows, width = terms[0].shape[0], terms[0].shape[1] // count

    def kernel(*refs):
        for k, out in enumerate(refs[len(terms) :]):
            columns = slice(k * width, (k + 1) * width)
            total = refs[0][:, columns]
            for ref in refs[1 : len(terms)]:
                total += ref[:, columns].astype(jnp.float32)
            out[...] = total.astype(jnp.bfloat16)

    result = jax.ShapeDtypeStruct((rows, width), jnp.bfloat16)
    return in_vmem(kernel, [result] * count, *terms, time=4)


def compare(groups, held, wanted, ids, row_count, blocks):
    rows, width = row_count, groups[0][0].shape[1]
    prompt_rows, across = rows * len(groups), len(groups[0])
    count, full = held.shape
    quarter = count // blocks
    factor = LOGIT_SCALE / math.sqrt(E)
    operands = [wanted, ids, *[piece for group in groups for piece in group], held]

    def kernel(wanted_ref, id_ref, *refs):
        group_refs = [refs[g * across : (g + 1) * across] for g in range(len(groups))]
        refs = refs[len(groups) * across :]
        rows_ref, loss_ref, mine_ref, away_ref, *part_refs = refs
        ids = id_ref[...]
        ids = jnp.concatenate([ids] * (rows // ids.shape[1]), axis=1)
        weights, losses = [], []
        for g, pieces in enumerate(group_refs):
            scores = jnp.zeros((count, rows), jnp.float32)
            for k, ref in enumerate(pieces):
                scores += cross_cols(rows_ref[:, k * width : (k + 1) * width], ref[:rows])
            scores = scores * factor + LOGIT_BIAS
            target = wanted_ref[...]
            if g > 0:
                tail = pieces[0][rows:].astype(jnp.float32)
                target = (tail[0:1] * 2.0**DIGIT_BITS + tail[1:2]).astype(jnp.int32)
            match = target == ids
            margin = jnp.where(match, -scores, scores)
            small = jnp.exp(-jnp.abs(margin))
            soft = jnp.maximum(margin, 0.0) + jnp.log1p(small)
            losses.append(jnp.sum(soft, axis=0, keepdims=True))
            share = jnp.where(margin >= 0.0, 1.0, small) / (1.0 + small)
            share = share * (factor / row_count)
            weights.append(jnp.where(match, -share, share).astype(jnp.bfloat16))
        for k in range(across):
            columns = slice(k * width, (k + 1) * width)
            part = sum(
                matmul(weight, pieces[k][:rows]) for weight, pieces in zip(weights, group_refs)
            )
            for block, part_ref in enumerate(part_refs):
                part_rows = part[block * quarter : (block + 1) * quarter]
                part_ref[:, columns] = part_rows.astype(part_ref.dtype)
        for k in range(across):
            out, goal = (mine_ref, away_ref)[k % 2], slice(k // 2 * width, (k // 2 + 1) * width)
            for g, weight in enumerate(weights):
                part = cross_rows(weight, rows_ref[:, k * width : (k + 1) * width])
                out[g * rows : (g + 1) * rows, goal] = part.astype(out.dtype)
        loss = jnp.concatenate(losses, axis=1)
        loss_ref[...] = loss
        away_ref[prompt_rows:] = tail_rows([loss])

    return pl.pallas_call(
        kernel,
        in_specs=[pl.BlockSpec(memory_space=pltpu.VMEM)] * len(operands),
        out_specs=[pl.BlockSpec(memory_space=pltpu.VMEM)] * (3 + blocks),
        out_shape=[
            jax.ShapeDtypeStruct((1, prompt_rows), jnp.float32),
            jax.ShapeDtypeStruct((prompt_rows, full // 2), jnp.float32),
            jax.ShapeDtypeStruct((prompt_rows + TAIL, full // 2), jnp.bfloat16),
            jax.ShapeDtypeStruct((quarter, full), jnp.float32),
        ]
        + [jax.ShapeDtypeStruct((quarter, full), jnp.bfloat16)] * (blocks - 1),
        compiler_params=pltpu.CompilerParams(vmem_limit_bytes=16 * 1024 * 1024),
        cost_estimate=cost(2),
    )(*operands)


def full_window(prompts, responses, head_projection_matrix, positive):
    row_count = prompts.shape[0]
    depth, width = head_projection_matrix.shape
    dp, mp = lax.axis_index("dp"), lax.axis_index("mp")
    z, y = dp // PAIR, dp % PAIR
    quarter = row_count // (SIDE * CORES)
    tie = lax.optimization_barrier

    here = [(z ^ k) * PAIR + y for k in range(LINE)]
    there = [(z ^ k) * PAIR + 1 - y for k in range(LINE)]
    even = (mp % CORES == 0).astype(jnp.int32)
    orders = (
        [there[2], there[3], even, mp // CORES],
        [here[0], there[0], here[1], there[1]],
        [here[3], there[3], here[2]],
        [there[2]],
        there[:2] + here,
        [even, mp // CORES],
    )
    ids = jnp.stack([here[0], here[1], there[1], there[0]]) * row_count + mp * quarter
    ids = (ids.astype(jnp.int32)[:, None] + lax.iota(jnp.int32, quarter)).reshape(-1, 1)
    ids = jnp.broadcast_to(ids, (LINE * quarter, LANES))
    own, orders, places, swap, left, ids = tie(
        (
            head_projection_matrix,
            [jnp.stack(order).astype(jnp.int32) for order in orders],
            [((mp ^ k) * quarter).astype(jnp.uint32) for k in range(SIDE * CORES)],
            even == 1,
            mp < CORES,
            ids,
        )
    )

    picked = pick(prompts, responses, orders[0], depth)
    own_y = send(own, ACROSS_Y)
    first, picked = tie((send(own, PAIRS), picked))
    third = send(own, OPPOSITE)
    second = send(third, PAIRS)
    first_y, third_y = send(first, ACROSS_Y), send(third, ACROSS_Y)
    first, own_y = tie((first, own_y))
    (emb,) = project(
        prompts,
        responses,
        orders[1],
        [(own,), (own_y,), (first,), (first_y,)],
        None,
        jnp.float32,
        20,
    )
    second, emb = tie((second, emb))
    second_y = send(second, ACROSS_Y)
    (emb,) = project(
        prompts,
        responses,
        orders[2],
        [(third,), (third_y,), (second,)],
        emb,
        jnp.float32,
        2.4,
    )
    features = slices(prompts, responses, tie((orders[3], second))[0], depth)
    second_y, emb, features = tie((second_y, emb, features))
    prompt_emb, response_emb = finish(features, second_y, emb, positive[None, :])

    pieces = []
    for k in range(SIDE * CORES):
        piece = lax.dynamic_slice(response_emb, (places[k], jnp.uint32(0)), (quarter, width))
        pieces.append(piece if k == 0 else send(piece, MIX[k]))
    pieces, picked, prompt_late = tie((pieces, picked, prompt_emb))
    fetched = send(picked, ACROSS_Y)
    prompt_far, prompt_far_x = send(prompt_emb, FAR), send(prompt_emb, FAR_X)
    beside = [send(prompt_late, ACROSS_X), prompt_far_x]
    response_rows = jnp.concatenate(pieces, axis=1)

    rows_late, fetched = tie((response_rows, fetched))
    held = [send(response_rows, PAIRS), send(response_rows, PAIRS_Y), send(rows_late, ACROSS_Y)]
    held = stacked([response_rows, *held])
    groups = [[block, send(block, ACROSS_C)] for block in (prompt_emb, prompt_far)]
    sibling = send(fetched, ACROSS_C)
    features = slices(prompts, responses, tie((orders[4], response_rows))[0], depth)
    held = tie(held)
    cross = [send(x, ACROSS_C) for x in beside]
    held, features, cross_tied, fetched = tie((held, features, cross, fetched))
    cross = cross_tied
    features = list(zip(features[:6], features[6:]))
    groups = [[*group, x, across] for group, x, across in zip(groups, beside, cross)]
    losses, mine, away, *parts = compare(
        groups, held, positive[None, :], ids, row_count, LINE
    )

    back = [send(part, table) for part, table in zip(parts[1:], (PAIRS, PAIRS_Y, ACROSS_Y))]
    mine, *messages, losses = after_cores(mine, send(away, ACROSS_C), losses, fetched)
    messages = [send(part, table) for part, table in zip(messages, (FAR, FAR_X, ACROSS_X))]
    pieces = summed([parts[0], *back], SIDE * CORES)

    pieces = [pieces[0]] + [send(pieces[k], MIX[k]) for k in range(1, SIDE * CORES)]
    pieces, messages = tie((pieces, messages))
    swapped = [jnp.where(swap, pieces[k], pieces[k ^ 1]) for k in range(SIDE * CORES)]
    swapped = [jnp.where(left, swapped[k], swapped[k ^ 2]) for k in range(SIDE * CORES)]
    grad_response = jnp.concatenate(swapped, axis=0)
    grad_prompt, losses = after_line(mine, messages, losses)
    grads_y = [send(grad_prompt, ACROSS_Y), send(grad_response, ACROSS_Y)]

    own_y, first_y, own, first, second, third = own_products(
        features, (grad_prompt, grad_response)
    )
    far_features = in_order(
        orders[5], (fetched, sibling), (messages[2], send(messages[2], ACROSS_C))
    )
    own, first, second, third, far_features = tie((own, first, second, third, far_features))
    second, third = far_products((second, third), far_features[1], grads_y[1], 4)
    own_y, first_y = send(own_y, ACROSS_Y), send(first_y, ACROSS_Y)
    second, third, second_b, third_b = far_products(
        (second, third), far_features[0], grads_y[0], 1, last=True
    )
    terms = line_reduce(own, first, second, third, second_b, third_b, own_y, first_y)
    return (losses[0] / row_count, turned_sum(*terms))


def per_device(prompts, responses, head_projection_matrix, positive):
    whole = lax.axis_size("dp") == STEPS == LINE * PAIR
    whole = whole and lax.axis_size("mp") == SIDE * CORES
    step = full_window if whole else general
    return step(prompts, responses, head_projection_matrix, positive)


def solution(mesh):
    return jax.shard_map(
        per_device,
        mesh=mesh,
        in_specs=(P("dp", None), P("dp", None), P("dp", "mp"), P("dp")),
        out_specs=(P("dp"), P("dp", "mp")),
        check_vma=False,
    )
```
